512 devices in a mesh: pulse: 128 (over z, y, x_lo), rng: 4 (over x_hi, core).
Axes of the slice: x: 4 (x_hi: 2, x_lo: 2; x = x_hi * 2 + x_lo), y: 4, z: 16, core: 2. Of those that a mesh axis runs over, the one named last changes fastest.
Arguments:
- raw: float32 [2, 2048, 24576], P(None, 'pulse', 'rng'), may hold values from -6 to 6
- range_filter: float32 [2, 24576], replicated, may hold values from -4 to 4
- azimuth_filter: float32 [2, 24576, 2048], P(None, ('pulse', 'rng')), may hold values from -4 to 4
- shifts: int32 [2048], replicated, may hold values from 0 to 16, as said below
- frac_index: int32 [2048], replicated, may hold values from 0 to 15
- kernel_table: float32 [16, 8], replicated, may hold values from 0.05 to 1
Outputs:
- image: float32 [2, 24576, 2048], P(None, ('pulse', 'rng'))
The draws below stay inside these ranges and needn't reach their ends.
Inputs may be any that keep to these rules, and one draw needn't show every extreme that they name: shifts[0] is 0 and shifts[1024] is 16.
All inputs are finite; a program needn't handle non-finite values.
Results may differ from the reference program's by a relative error of at most 0.000071.
Values sent between devices are 32-bit elements; how exact they have to be, the bound alone decides.
A program may use at most 64 MiB of HBM per device.

```python
import jax
import jax.numpy as jnp
from jax import lax

MIGRATION = 16
TAPS = 8
TABLE_ROWS = 16
PULSES = 2048
SAMPLES = 24576


def draw_shifts(key, part):
    key = jax.random.fold_in(key, 7)
    bins = jnp.arange(PULSES, dtype=jnp.int32)
    half_len = PULSES // 2
    distance = jnp.minimum(bins, PULSES - bins)
    base_shift = MIGRATION * distance * distance // (half_len * half_len)
    jitter = jax.random.randint(key, (PULSES,), -1, 2, dtype=jnp.int32)
    result = jnp.clip(base_shift + jitter, 0, MIGRATION)
    result = jnp.where(bins == 0, 0, result)
    result = jnp.where(distance == half_len, MIGRATION, result)
    return result.astype(jnp.int32)


def touch_ends(array, key, smallest, high):
    longest = array.shape.index(max(array.shape))
    spots = []
    for shift in (0, 1):
        where = [jax.random.randint(jax.random.fold_in(key, axis), (), 0, length) for axis, length in enumerate(array.shape)]
        where[longest] = (where[longest] + shift) % array.shape[longest]
        spots.append(tuple(where))
    return array.at[spots[0]].set(smallest).at[spots[1]].set(high)


def levels(key, shape, pieces, least, top_value):
    factor_of = 1.0
    for position, blocks in pieces:
        draws = jax.random.uniform(jax.random.fold_in(jax.random.fold_in(key, 6), position), (blocks,), jnp.float32, least / len(pieces), top_value / len(pieces))
        factor_of = factor_of * jnp.repeat(jnp.exp(draws), shape[position] // blocks).reshape((-1,) + (1,) * (len(shape) - 1 - position))
    return factor_of


def gaussian(own_key, extent, width, bound, cuts=(), kind=jnp.bfloat16):
    level = levels(own_key, extent, cuts, -0.22, 0.18) if cuts else 1.0
    values = jax.random.normal(own_key, extent, jnp.float32) * width * level
    return jnp.minimum(jnp.maximum(values, -bound), bound).astype(kind)


def setup_inputs(seed: int = 0) -> dict:
    splits = jax.random.split(jax.random.key(seed), 7)
    return {
        "raw": gaussian(splits[0], (2, PULSES, SAMPLES), 1.0, 6.0, ((1, 128), (2, 4)), jnp.float32),
        "range_filter": gaussian(splits[1], (2, SAMPLES), 0.7, 4.0, (), jnp.float32),
        "azimuth_filter": gaussian(splits[2], (2, SAMPLES, PULSES), 0.7, 4.0, ((1, 512),), jnp.float32),
        "shifts": draw_shifts(jax.random.fold_in(splits[6], 71), 0),
        "frac_index": touch_ends(jax.random.randint(splits[4], (PULSES,), 0, TABLE_ROWS), jax.random.fold_in(splits[4], 1), 0, TABLE_ROWS - 1).astype(jnp.int32),
        "kernel_table": jnp.clip(jax.random.uniform(splits[5], (TABLE_ROWS, TAPS), jnp.float32, 0.05, 1.0), 0.05, 1.0),
    }


def reference(raw, range_filter, azimuth_filter, shifts, frac_index, kernel_table):
    echoes = lax.complex(raw[0], raw[1])
    range_response = lax.complex(range_filter[0], range_filter[1])
    range_spectrum = jnp.fft.fft(echoes, axis=1) * range_response[None, :]
    compressed = jnp.fft.ifft(range_spectrum, axis=1)
    doppler = jnp.fft.fft(compressed, axis=0)
    row_weights = kernel_table[frac_index]
    padded = jnp.pad(doppler, ((0, 0), (3, MIGRATION + 4)))
    corrected = jnp.zeros_like(doppler)
    for tap_index in range(TAPS):
        taken = jax.vmap(lambda row_line, row_shift: lax.dynamic_slice_in_dim(row_line, row_shift + tap_index, SAMPLES))(padded, shifts)
        corrected = corrected + row_weights[:, tap_index:tap_index + 1] * taken
    azimuth_response = lax.complex(azimuth_filter[0], azimuth_filter[1]).T
    focused = corrected * azimuth_response
    image = jnp.fft.ifft(focused, axis=0).T
    return jnp.stack([jnp.real(image), jnp.imag(image)]).astype(jnp.float32)
```

```python
import functools
import math

import jax
import jax.numpy as jnp
import ml_dtypes
import numpy as np
from jax import lax
from jax.experimental import pallas as pl
from jax.experimental.pallas import tpu as pltpu
from jax.sharding import PartitionSpec as P

MESH = pl.DeviceIdType.MESH
F32 = jnp.float32
BF16 = jnp.bfloat16

PULSES = 2048
SAMPLES = 24576
ROWS = 192
LANES = 128
PLANES = 16
PEERS = 32
LANE_PULSES = 4
BINS = 48
SEGMENT = 1536
SEG_ROWS = 12
BLOCK = 2 * SEG_ROWS * LANE_PULSES
BELOW = 8
ABOVE = 24
WINDOW = BELOW + BINS + ABOVE
TAPS = 8


def turn(product, period, sign):
    angle = sign * 2.0 * math.pi * (product % period) / period
    return np.cos(angle), np.sin(angle)


def halves(table):
    high = table.astype(ml_dtypes.bfloat16)
    low = (table - high.astype(np.float64)).astype(ml_dtypes.bfloat16)
    return high, low


def left_factor(table):
    high, low = halves(table)
    return np.concatenate([high, high, low], axis=1)


def right_factor(table):
    high, low = halves(table)
    return np.concatenate([high, high, low], axis=-2)


def lane_bins():
    lanes = np.arange(LANES)
    return 8 * (lanes % 16) + lanes // 16


def table_first():
    ids = np.arange(ROWS)
    re, im = turn(np.outer(ids, ids), ROWS, -1)
    return left_factor(np.block([[re, -im], [im, re]]))


def table_last():
    ids = np.arange(ROWS)
    re, im = turn(np.outer(ids, ids), ROWS, 1)
    re, im = re / SAMPLES, im / SAMPLES
    real_rows = np.concatenate([re, -im], axis=1).reshape(PLANES, 1, SEG_ROWS, 2 * ROWS)
    imag_rows = np.concatenate([im, re], axis=1).reshape(PLANES, 1, SEG_ROWS, 2 * ROWS)
    return left_factor(np.concatenate([real_rows, imag_rows], axis=1).reshape(2 * ROWS, 2 * ROWS))


def filter_order():
    lanes = np.arange(LANES)
    return 2 * (lanes % 64) + lanes // 64


def table_columns(rows, cols, sign, scale=1.0):
    re, im = turn(np.outer(rows, cols), LANES, sign)
    return np.block([[re, im], [-im, re]]) * scale


def table_twist():
    re, im = turn(np.outer(np.arange(ROWS), np.arange(LANES)), SAMPLES, -1)
    return np.stack([re, im]).astype(np.float32)


def table_planes():
    place = np.arange(PEERS)[:, None, None, None]
    r = np.arange(LANE_PULSES)[None, :, None, None]
    z = np.arange(PLANES)[None, None, :, None]
    k1 = np.arange(16)[None, None, None, :]
    re, im = turn((128 * z + 4 * place + r) * k1, PULSES, -1)
    full = np.zeros((PEERS, 2, LANE_PULSES, PLANES, 16, 2, LANE_PULSES))
    for q in range(LANE_PULSES):
        full[:, 0, q, :, :, 0, q] = re[:, q]
        full[:, 1, q, :, :, 0, q] = -im[:, q]
        full[:, 0, q, :, :, 1, q] = im[:, q]
        full[:, 1, q, :, :, 1, q] = re[:, q]
    return right_factor(full.reshape(PEERS, 128, 128))


def table_azimuth():
    place = np.arange(PEERS)[:, None, None]
    r = np.arange(LANE_PULSES)[None, :, None]
    re, im = turn((4 * place + r) * lane_bins()[None, None, :], LANES, -1)
    full = np.zeros((PEERS, 2, LANE_PULSES, 2, LANES))
    full[:, 0, :, 0] = re
    full[:, 1, :, 0] = -im
    full[:, 0, :, 1] = im
    full[:, 1, :, 1] = re
    return right_factor(full.reshape(2 * LANES, 2 * LANES))


def table_back():
    return right_factor(table_columns(lane_bins(), np.arange(LANES), 1, 1.0 / PULSES))


def table_back_twist():
    re, im = turn(np.outer(np.arange(16), np.arange(LANES)), PULSES, 1)
    return np.stack([re, im]).astype(np.float32)


def split(values):
    high = values.astype(BF16)
    low = (values - high.astype(F32)).astype(BF16)
    return high, low


def times_left(table, values):
    high, low = split(values)
    return jnp.dot(table, jnp.concatenate([high, low, high], axis=0), preferred_element_type=F32)


def times_right(values, table):
    high, low = split(values)
    return jnp.dot(jnp.concatenate([high, low, high], axis=1), table, preferred_element_type=F32)


def cmul(a_re, a_im, b_re, b_im):
    return a_re * b_re - a_im * b_im, a_re * b_im + a_im * b_re


def fft_list(values, sign):
    count = len(values)
    if count == 1:
        return values
    even = fft_list(values[0::2], sign)
    odd = fft_list(values[1::2], sign)
    low, high = [], []
    for k in range(count // 2):
        re, im = odd[k]
        if 4 * k == count:
            re, im = (-im, re) if sign > 0 else (im, -re)
        elif k:
            w_re = math.cos(2.0 * math.pi * k / count)
            w_im = sign * math.sin(2.0 * math.pi * k / count)
            re, im = re * w_re - im * w_im, re * w_im + im * w_re
        low.append((even[k][0] + re, even[k][1] + im))
        high.append((even[k][0] - re, even[k][1] - im))
    return low + high


def swap_blocks(arrays, width):
    arrays = list(arrays)
    lane = lax.broadcasted_iota(jnp.int32, arrays[0].shape, 1)
    for bit in (1, 2, 4, 8):
        keep = (lane // width) & bit == 0
        for a in range(16):
            if a & bit:
                continue
            first, second = arrays[a], arrays[a + bit]
            arrays[a] = jnp.where(keep, first, pltpu.roll(second, bit * width, 1))
            arrays[a + bit] = jnp.where(keep, pltpu.roll(first, LANES - bit * width, 1), second)
    return arrays


def compress_kernel(x_ref, filt_ref, first_ref, last_ref, twist_ref, fwd_ref, back_ref, y_ref):
    twist_re, twist_im = twist_ref[0], twist_ref[1]
    filt = []
    for c in range(2):
        cols = [filt_ref[pl.ds(2 * u + c, 64, stride=6), :].T for u in range(3)]
        tall = jnp.concatenate(cols, axis=0)
        filt.append(jnp.concatenate([tall[:ROWS], tall[ROWS:]], axis=1))
    for r in range(LANE_PULSES):
        x = jnp.concatenate(
            [x_ref[pl.ds(c * 768 + r, ROWS, stride=LANE_PULSES), :] for c in range(2)], axis=0
        )
        v = times_left(first_ref[...], x)
        re, im = cmul(v[:ROWS], v[ROWS:], twist_re, twist_im)
        s = times_right(jnp.concatenate([re, im], axis=1), fwd_ref[...])
        re, im = cmul(s[:, :LANES], s[:, LANES:], filt[0], filt[1])
        s = times_right(jnp.concatenate([re, im], axis=1), back_ref[...])
        re, im = cmul(s[:, :LANES], s[:, LANES:], twist_re, -twist_im)
        out = times_left(last_ref[...], jnp.concatenate([re, im], axis=0))
        for z in range(PLANES):
            start = BLOCK * z + 2 * SEG_ROWS * r
            y_ref[start : start + 2 * SEG_ROWS] = out[2 * SEG_ROWS * z : 2 * SEG_ROWS * (z + 1)]


def plane_kernel(z_ref, table_hbm, t_ref, table_ref, sem):
    place = 4 * lax.rem(lax.axis_index("pulse"), 8) + lax.axis_index("rng")
    copy = pltpu.make_async_copy(table_hbm.at[place], table_ref, sem)
    copy.start()
    copy.wait()

    def step(row, _):
        parts = []
        for c in range(2):
            for r in range(LANE_PULSES):
                start = 2 * SEG_ROWS * r + SEG_ROWS * c + row
                parts.append(z_ref[pl.ds(start, PLANES, stride=BLOCK), :])
        t_ref[pl.ds(pl.multiple_of(row * LANES, LANES), LANES), :] = times_right(
            jnp.concatenate(parts, axis=0).T, table_ref[...]
        )
        return 0

    lax.fori_loop(0, SEG_ROWS, step, 0)


def azimuth_kernel(
    g_ref, azf_ref, shift_ref, frac_ref, ktab_ref, fwd_ref, back_ref, twist_ref, out_ref,
    h_ref, d_ref, e_ref, a_ref, f_ref, w_ref,
):
    def turn_group(step, _):
        rows = pl.ds(pl.multiple_of(8 * step, 8), 8)
        for half in range(2):
            got = swap_blocks([g_ref[16 * half + i, rows, :] for i in range(16)], 8)
            for k1 in range(16):
                h_ref[k1, rows, LANES * half : LANES * (half + 1)] = got[k1]
        return 0

    lax.fori_loop(0, WINDOW // 8, turn_group, 0)

    def turn_filter(step, _):
        rows = pl.ds(pl.multiple_of(8 * step, 8), 8)
        for c in range(2):
            got = swap_blocks(
                [azf_ref[c, rows, LANES * t : LANES * (t + 1)] for t in range(16)], 1
            )
            for k1 in range(16):
                a_ref[c, k1, rows, :] = got[k1]
        return 0

    lax.fori_loop(0, BINS // 8, turn_filter, 0)

    frac = frac_ref[...]
    for tap in range(TAPS):
        weight = jnp.zeros(frac.shape, F32)
        for row in range(16):
            weight = jnp.where(frac == row, ktab_ref[row, tap], weight)
        w_ref[tap] = weight

    def per_bin(k1, _):
        d = times_right(h_ref[k1], fwd_ref[...])
        shift = shift_ref[pl.ds(k1, 1), :]
        weights = [w_ref[tap, pl.ds(k1, 1), :] for tap in range(TAPS)]
        moved = []
        for c in range(2):
            x = d[:, LANES * c : LANES * (c + 1)]
            near = jnp.where((shift & 16) != 0, x[16:80], x[0:64])
            x = jnp.concatenate([near, x[64:80]], axis=0)
            d_ref[c, 0:72] = jnp.where((shift & 8) != 0, x[8:80], x[0:72])
            e_ref[c, 0:64] = jnp.where((shift & 4) != 0, d_ref[c, 4:68], d_ref[c, 0:64])
            d_ref[c, 0:62] = jnp.where((shift & 2) != 0, e_ref[c, 2:64], e_ref[c, 0:62])
            e_ref[c, 0:61] = jnp.where((shift & 1) != 0, d_ref[c, 1:62], d_ref[c, 0:61])
            total = weights[0] * e_ref[c, 5 : 5 + BINS]
            for tap in range(1, TAPS):
                total = total + weights[tap] * e_ref[c, 5 + tap : 5 + tap + BINS]
            moved.append(total)
        re, im = cmul(moved[0], moved[1], a_ref[0, k1], a_ref[1, k1])
        s = times_right(jnp.concatenate([re, im], axis=1), back_ref[...])
        re, im = cmul(
            s[:, :LANES], s[:, LANES:], twist_ref[0, pl.ds(k1, 1), :], twist_ref[1, pl.ds(k1, 1), :]
        )
        f_ref[0, k1] = re
        f_ref[1, k1] = im
        return 0

    lax.fori_loop(0, 16, per_bin, 0)

    def finish(step, _):
        rows = pl.ds(pl.multiple_of(8 * step, 8), 8)
        got = fft_list([(f_ref[0, k1, rows, :], f_ref[1, k1, rows, :]) for k1 in range(16)], 1)
        for tile in range(16):
            out_ref[0, rows, LANES * tile : LANES * (tile + 1)] = got[tile][0]
            out_ref[1, rows, LANES * tile : LANES * (tile + 1)] = got[tile][1]
        return 0

    lax.fori_loop(0, BINS // 8, finish, 0)


def range_exchange_kernel(raw_ref, x_ref, send_sem, recv_sem, own_sem):
    me = lax.axis_index("rng")
    barrier = pltpu.get_barrier_semaphore()
    for off in range(1, 4):
        pl.semaphore_signal(
            barrier, inc=1, device_id={"rng": lax.rem(me + off, 4)}, device_id_type=MESH
        )
    pl.semaphore_wait(barrier, 3)
    copies = []
    for off in range(1, 4):
        to = lax.rem(me + off, 4)
        copy = pltpu.make_async_remote_copy(
            src_ref=raw_ref.at[:, lax.div(to, 2), :, lax.rem(to, 2)],
            dst_ref=x_ref.at[:, pl.ds(48 * me, 48)],
            send_sem=send_sem.at[off],
            recv_sem=recv_sem.at[off],
            device_id={"rng": to},
            device_id_type=MESH,
        )
        copy.start()
        copies.append(copy)
    own = pltpu.make_async_copy(
        raw_ref.at[:, lax.div(me, 2), :, lax.rem(me, 2)], x_ref.at[:, pl.ds(48 * me, 48)], own_sem
    )
    own.start()
    own.wait()
    for copy in copies:
        copy.wait()


def plane_peers(z, off, place):
    to = lax.rem(place + off, PEERS)
    return to, (8 * z + lax.div(to, 4), lax.rem(to, 4))


def z_exchange_kernel(y_ref, z_ref, send_sem, recv_sem, own_sem):
    pulse = lax.axis_index("pulse")
    me = lax.div(pulse, 8)
    rest = lax.rem(pulse, 8)
    barrier = pltpu.get_barrier_semaphore()
    for off in range(1, PLANES):
        to = lax.rem(me + off, PLANES)
        pl.semaphore_signal(barrier, inc=1, device_id={"pulse": 8 * to + rest}, device_id_type=MESH)
    pl.semaphore_wait(barrier, PLANES - 1)
    copies = []
    for near in range(1, 9):
        for off in sorted({near, PLANES - near}):
            to = lax.rem(me + off, PLANES)
            copy = pltpu.make_async_remote_copy(
                src_ref=y_ref.at[pl.ds(pl.multiple_of(BLOCK * to, 8), BLOCK)],
                dst_ref=z_ref.at[pl.ds(pl.multiple_of(BLOCK * me, 8), BLOCK)],
                send_sem=send_sem.at[off],
                recv_sem=recv_sem.at[off],
                device_id={"pulse": 8 * to + rest},
                device_id_type=MESH,
            )
            copy.start()
            copies.append(copy)
    mine = pl.ds(pl.multiple_of(BLOCK * me, 8), BLOCK)
    own = pltpu.make_async_copy(y_ref.at[mine], z_ref.at[mine], own_sem)
    own.start()
    own.wait()
    for copy in copies:
        copy.wait()


def plane_exchange_kernel(t_ref, zero_ref, g_ref, send_sem, recv_sem, halo_send, halo_recv, own_sem, zero_sem):
    pulse = lax.axis_index("pulse")
    z = lax.div(pulse, 8)
    place = 4 * lax.rem(pulse, 8) + lax.axis_index("rng")
    first = place == 0
    last = place == PEERS - 1
    barrier = pltpu.get_barrier_semaphore()

    def signal(device):
        pl.semaphore_signal(barrier, inc=1, device_id=device, device_id_type=MESH)

    def greet(off, _):
        signal(plane_peers(z, off, place)[1])
        return 0

    lax.fori_loop(1, PEERS, greet, 0)

    def greet_halo(other):
        def body(off, _):
            signal(plane_peers(other, off, place)[1])
            return 0

        lax.fori_loop(0, PEERS, body, 0)

    has_below = z > 0
    has_above = z < PLANES - 1
    takes_below = jnp.logical_and(first, has_below)
    takes_above = jnp.logical_and(last, has_above)
    pl.when(takes_below)(lambda: greet_halo(z - 1))
    pl.when(takes_above)(lambda: greet_halo(z + 1))
    pl.semaphore_wait(
        barrier,
        PEERS - 1 + jnp.where(has_below, 1, 0) + jnp.where(has_above, 1, 0),
    )

    def rows_of(to):
        return 48 * to - BELOW

    def copy_to(off, to, device, start, dst, size):
        return pltpu.make_async_remote_copy(
            src_ref=t_ref.at[pl.ds(start, size)],
            dst_ref=g_ref.at[place, pl.ds(dst, size)],
            send_sem=send_sem.at[off],
            recv_sem=recv_sem.at[off],
            device_id=device,
            device_id_type=MESH,
        )

    def three(to, act):
        pl.when(to == 0)(lambda: act(0, BELOW, WINDOW - BELOW))
        pl.when(to == PEERS - 1)(lambda: act(SEGMENT - BELOW - BINS, 0, BELOW + BINS))
        middle = jnp.logical_and(to > 0, to < PEERS - 1)
        pl.when(middle)(lambda: act(pl.multiple_of(48 * to - BELOW, 8), 0, WINDOW))

    def send(off, _):
        to, device = plane_peers(z, off, place)
        three(to, lambda start, dst, size: copy_to(off, to, device, start, dst, size).start())
        return 0

    lax.fori_loop(1, PEERS, send, 0)

    def halo_down():
        return pltpu.make_async_remote_copy(
            src_ref=t_ref.at[pl.ds(0, ABOVE)],
            dst_ref=g_ref.at[place, pl.ds(BELOW + BINS, ABOVE)],
            send_sem=halo_send.at[0],
            recv_sem=halo_recv.at[place],
            device_id=(8 * (z - 1) + 7, 3),
            device_id_type=MESH,
        )

    def halo_up():
        return pltpu.make_async_remote_copy(
            src_ref=t_ref.at[pl.ds(SEGMENT - BELOW, BELOW)],
            dst_ref=g_ref.at[place, pl.ds(0, BELOW)],
            send_sem=halo_send.at[1],
            recv_sem=halo_recv.at[place],
            device_id=(8 * (z + 1), 0),
            device_id_type=MESH,
        )

    pl.when(has_below)(lambda: halo_down().start())
    pl.when(has_above)(lambda: halo_up().start())

    def own(start, dst, size):
        copy = pltpu.make_async_copy(
            t_ref.at[pl.ds(start, size)], g_ref.at[place, pl.ds(dst, size)], own_sem
        )
        copy.start()
        copy.wait()

    three(place, own)

    def blank(dst, size):
        copy = pltpu.make_async_copy(
            zero_ref.at[:, pl.ds(0, size)], g_ref.at[:, pl.ds(dst, size)], zero_sem
        )
        copy.start()
        copy.wait()

    pl.when(jnp.logical_and(first, z == 0))(lambda: blank(0, BELOW))
    pl.when(jnp.logical_and(last, z == PLANES - 1))(lambda: blank(BELOW + BINS, ABOVE))

    def wait_send(off, _):
        to, device = plane_peers(z, off, place)
        three(to, lambda start, dst, size: copy_to(off, to, device, start, dst, size).wait_send())
        return 0

    def wait_recv(off, _):
        to, device = plane_peers(z, off, place)
        three(place, lambda start, dst, size: copy_to(off, to, device, start, dst, size).wait_recv())
        return 0

    lax.fori_loop(1, PEERS, wait_send, 0)
    lax.fori_loop(1, PEERS, wait_recv, 0)
    pl.when(has_below)(lambda: halo_down().wait_send())
    pl.when(has_above)(lambda: halo_up().wait_send())

    def wait_halo(dst, size):
        def body(index, _):
            pltpu.make_async_remote_copy(
                src_ref=t_ref.at[pl.ds(0, size)],
                dst_ref=g_ref.at[index, pl.ds(dst, size)],
                send_sem=halo_send.at[0],
                recv_sem=halo_recv.at[index],
                device_id=(pulse, lax.axis_index("rng")),
                device_id_type=MESH,
            ).wait_recv()
            return 0

        lax.fori_loop(0, PEERS, body, 0)

    pl.when(takes_below)(lambda: wait_halo(0, BELOW))
    pl.when(takes_above)(lambda: wait_halo(BELOW + BINS, ABOVE))


ANY = pl.BlockSpec(memory_space=pl.ANY)
WHOLE = pl.BlockSpec(memory_space=pltpu.VMEM)
SCALARS = pl.BlockSpec(memory_space=pltpu.SMEM)
DMA = pltpu.SemaphoreType.DMA


def params(collective=None, limit=40):
    extra = {} if collective is None else dict(collective_id=collective, has_side_effects=True)
    return pltpu.CompilerParams(vmem_limit_bytes=limit * 2**20, **extra)


def range_exchange(raw):
    tiles = raw.reshape(2, 2, 2, 4, 48, LANES).transpose(0, 1, 4, 2, 3, 5)
    return pl.pallas_call(
        range_exchange_kernel,
        out_shape=jax.ShapeDtypeStruct((2, ROWS, LANE_PULSES, LANES), F32),
        in_specs=[ANY],
        out_specs=ANY,
        scratch_shapes=[DMA((4,)), DMA((4,)), DMA],
        compiler_params=params(0),
    )(tiles)


def compress(x, range_filter):
    filt = range_filter.reshape(2, ROWS, LANES).transpose(1, 0, 2).reshape(2 * ROWS, LANES)
    order = filter_order()
    return pl.pallas_call(
        compress_kernel,
        out_shape=jax.ShapeDtypeStruct((PLANES * BLOCK, LANES), F32),
        in_specs=[WHOLE] * 7,
        out_specs=WHOLE,
        compiler_params=params(),
    )(
        x.reshape(2 * ROWS * LANE_PULSES, LANES),
        filt,
        table_first(),
        table_last(),
        table_twist(),
        right_factor(table_columns(np.arange(LANES), order, -1)),
        right_factor(table_columns(order, np.arange(LANES), 1)),
    )


def z_exchange(y):
    return pl.pallas_call(
        z_exchange_kernel,
        out_shape=jax.ShapeDtypeStruct(y.shape, F32),
        in_specs=[ANY],
        out_specs=ANY,
        scratch_shapes=[DMA((PLANES,)), DMA((PLANES,)), DMA],
        compiler_params=params(1),
    )(y)


def to_planes(z):
    table = table_planes()
    return pl.pallas_call(
        plane_kernel,
        out_shape=jax.ShapeDtypeStruct((SEGMENT, LANES), F32),
        in_specs=[WHOLE, ANY],
        out_specs=WHOLE,
        scratch_shapes=[pltpu.VMEM(table.shape[1:], BF16), DMA],
        compiler_params=params(),
    )(z, table)


def plane_exchange(t):
    return pl.pallas_call(
        plane_exchange_kernel,
        out_shape=jax.ShapeDtypeStruct((PEERS, WINDOW, LANES), F32),
        in_specs=[ANY, ANY],
        out_specs=ANY,
        scratch_shapes=[DMA((PEERS,)), DMA((PEERS,)), DMA((2,)), DMA((PEERS,)), DMA, DMA],
        compiler_params=params(2),
    )(t, np.zeros((PEERS, ABOVE, LANES), np.float32))


def by_bin(values):
    return values.reshape(16, 8, 16).transpose(2, 1, 0).reshape(16, LANES)


def azimuth(g, azimuth_filter, shifts, frac_index, kernel_table):
    return pl.pallas_call(
        azimuth_kernel,
        out_shape=jax.ShapeDtypeStruct((2, BINS, PULSES), F32),
        in_specs=[WHOLE] * 4 + [SCALARS] + [WHOLE] * 3,
        out_specs=WHOLE,
        scratch_shapes=[
            pltpu.VMEM((16, WINDOW, 2 * LANES), F32),
            pltpu.VMEM((2, WINDOW, LANES), F32),
            pltpu.VMEM((2, WINDOW, LANES), F32),
            pltpu.VMEM((2, 16, BINS, LANES), F32),
            pltpu.VMEM((2, 16, BINS, LANES), F32),
            pltpu.VMEM((TAPS, 16, LANES), F32),
        ],
        compiler_params=params(),
    )(
        g, azimuth_filter, by_bin(shifts), by_bin(frac_index), kernel_table,
        table_azimuth(), table_back(), table_back_twist(),
    )


def shards(raw, range_filter, azimuth_filter, shifts, frac_index, kernel_table):
    y = compress(range_exchange(raw), range_filter)
    g = plane_exchange(to_planes(z_exchange(y)))
    return azimuth(g, azimuth_filter, shifts, frac_index, kernel_table)


def solution(mesh):
    in_specs = (P(None, "pulse", "rng"), P(), P(None, ("pulse", "rng"), None), P(), P(), P())
    out_specs = P(None, ("pulse", "rng"), None)
    return jax.shard_map(shards, mesh=mesh, in_specs=in_specs, out_specs=out_specs, check_vma=False)
```

```python
import functools
import math

import jax
import jax.numpy as jnp
import ml_dtypes
import numpy as np
from jax import lax
from jax.experimental import pallas as pl
from jax.experimental.pallas import tpu as pltpu
from jax.sharding import PartitionSpec as P

MESH = pl.DeviceIdType.MESH
F32 = jnp.float32
BF16 = jnp.bfloat16

PULSES = 2048
SAMPLES = 24576
ROWS = 192
LANES = 128
PLANES = 16
PEERS = 32
CHIPS = 16
LANE_PULSES = 4
BINS = 48
CHUNKS = 4
CHUNK_ROWS = 3
CHUNK = CHUNK_ROWS * LANES
PIECE = 2 * CHUNK_ROWS * LANE_PULSES
BELOW = 8
ABOVE = 24
WINDOW = BELOW + BINS + ABOVE
PAIR = BELOW + 2 * BINS + ABOVE
TAPS = 8
ORDER = (2, 1, 3, 0)


def turn(product, period, sign):
    angle = sign * 2.0 * math.pi * (product % period) / period
    return np.cos(angle), np.sin(angle)


def halves(table):
    high = table.astype(ml_dtypes.bfloat16)
    low = (table - high.astype(np.float64)).astype(ml_dtypes.bfloat16)
    return high, low


def left_factor(table):
    high, low = halves(table)
    return np.concatenate([high, high, low], axis=1)


def right_factor(table):
    high, low = halves(table)
    return np.concatenate([high, high, low], axis=-2)


def lane_bins():
    lanes = np.arange(LANES)
    return 8 * (lanes % 16) + lanes // 16


def table_first():
    ids = np.arange(ROWS)
    re, im = turn(np.outer(ids, ids), ROWS, -1)
    return left_factor(np.block([[re, -im], [im, re]]))


def table_last():
    ids = np.arange(ROWS)
    re, im = turn(np.outer(ids, ids), ROWS, 1)
    full = np.stack([np.concatenate([re, -im], axis=1), np.concatenate([im, re], axis=1)]) / SAMPLES
    full = full.reshape(2, PLANES, CHUNKS, CHUNK_ROWS, 2 * ROWS).transpose(2, 1, 0, 3, 4)
    return left_factor(full.reshape(2 * ROWS, 2 * ROWS)).reshape(CHUNKS, 2 * ROWS // CHUNKS, -1)


def filter_order():
    lanes = np.arange(LANES)
    return 2 * (lanes % 64) + lanes // 64


def table_columns(rows, cols, sign, scale=1.0):
    re, im = turn(np.outer(rows, cols), LANES, sign)
    return np.block([[re, im], [-im, re]]) * scale


def table_twist():
    re, im = turn(np.outer(np.arange(ROWS), np.arange(LANES)), SAMPLES, -1)
    return np.stack([re, im]).astype(np.float32)


def table_planes():
    place = np.arange(PEERS)[:, None, None, None]
    r = np.arange(LANE_PULSES)[None, :, None, None]
    z = np.arange(PLANES)[None, None, :, None]
    k1 = np.arange(16)[None, None, None, :]
    re, im = turn((128 * z + 4 * place + r) * k1, PULSES, -1)
    full = np.zeros((PEERS, 2, LANE_PULSES, PLANES, 16, 2, LANE_PULSES))
    for q in range(LANE_PULSES):
        full[:, 0, q, :, :, 0, q] = re[:, q]
        full[:, 1, q, :, :, 0, q] = -im[:, q]
        full[:, 0, q, :, :, 1, q] = im[:, q]
        full[:, 1, q, :, :, 1, q] = re[:, q]
    return right_factor(full.reshape(PEERS, 128, 128))


def table_azimuth():
    place = np.arange(PEERS)[:, None, None]
    r = np.arange(LANE_PULSES)[None, :, None]
    re, im = turn((4 * place + r) * lane_bins()[None, None, :], LANES, -1)
    full = np.zeros((PEERS, 2, LANE_PULSES, 2, LANES))
    full[:, 0, :, 0] = re
    full[:, 1, :, 0] = -im
    full[:, 0, :, 1] = im
    full[:, 1, :, 1] = re
    by_core = full.reshape(CHIPS, 2, 8, 2 * LANES).transpose(1, 0, 2, 3)
    return right_factor(by_core.reshape(2 * LANES, 2 * LANES))


def table_back():
    return right_factor(table_columns(lane_bins(), np.arange(LANES), 1, 1.0 / PULSES))


def table_back_twist():
    re, im = turn(np.outer(np.arange(16), np.arange(LANES)), PULSES, 1)
    return np.stack([re, im]).astype(np.float32)


def split(values):
    high = values.astype(BF16)
    low = (values - high.astype(F32)).astype(BF16)
    return high, low


def times_left(table, values):
    high, low = split(values)
    return jnp.dot(table, jnp.concatenate([high, low, high], axis=0), preferred_element_type=F32)


def times_right(values, table):
    high, low = split(values)
    return jnp.dot(jnp.concatenate([high, low, high], axis=1), table, preferred_element_type=F32)


def cmul(a_re, a_im, b_re, b_im):
    return a_re * b_re - a_im * b_im, a_re * b_im + a_im * b_re


def fft_list(values, sign):
    count = len(values)
    if count == 1:
        return values
    even = fft_list(values[0::2], sign)
    odd = fft_list(values[1::2], sign)
    low, high = [], []
    for k in range(count // 2):
        re, im = odd[k]
        if 4 * k == count:
            re, im = (-im, re) if sign > 0 else (im, -re)
        elif k:
            w_re = math.cos(2.0 * math.pi * k / count)
            w_im = sign * math.sin(2.0 * math.pi * k / count)
            re, im = re * w_re - im * w_im, re * w_im + im * w_re
        low.append((even[k][0] + re, even[k][1] + im))
        high.append((even[k][0] - re, even[k][1] - im))
    return low + high


def swap_blocks(arrays, width):
    arrays = list(arrays)
    lane = lax.broadcasted_iota(jnp.int32, arrays[0].shape, 1)
    for bit in (1, 2, 4, 8):
        keep = (lane // width) & bit == 0
        for a in range(16):
            if a & bit:
                continue
            first, second = arrays[a], arrays[a + bit]
            arrays[a] = jnp.where(keep, first, pltpu.roll(second, bit * width, 1))
            arrays[a + bit] = jnp.where(keep, pltpu.roll(first, LANES - bit * width, 1), second)
    return arrays


def kernel(
    raw_hbm, filt_hbm, azf_hbm, shift_hbm, frac_hbm, ktab_hbm,
    first_hbm, last_hbm, twist_hbm, fwd_hbm, back_hbm, planes_hbm, az_fwd_hbm, az_back_hbm, az_twist_hbm,
    out_ref,
    filt_in, azf_in, shift_in, frac_in, ktab, first, last, twist, fwd, back, planes, az_fwd, az_back, az_twist,
    load_sem,
    tiles, outgoing, x_ref, filt, v_ref, y_ref, z_ref, t_ref, g_ref, o_ref,
    shift_ref, w_ref, a_ref, h_ref, d_ref, e_ref, f_ref,
    tile_sem, x_send, x_recv, core_send, core_recv, z_send, z_recv, z_own,
    p_send, p_recv, h_send, h_recv, own_sem, halo_own, fwd_send, fwd_recv,
):
    pulse = lax.axis_index("pulse")
    lane = lax.axis_index("rng")
    z = lax.div(pulse, 8)
    y = lax.rem(lax.div(pulse, 2), 4)
    xh = lax.div(lane, 2)
    core = lax.rem(lane, 2)
    q_me = 2 * lax.rem(pulse, 2) + xh
    chip = 4 * y + q_me
    has_below = z > 0
    has_above = z < PLANES - 1

    def device(plane, other_chip, other_core):
        return (8 * plane + lax.div(other_chip, 2), 2 * lax.rem(other_chip, 2) + other_core)

    x_partner = (pulse, 2 * (1 - xh) + core)
    core_partner = (pulse, 2 * xh + 1 - core)

    barrier = pltpu.get_barrier_semaphore()

    def greet(to):
        pl.semaphore_signal(barrier, inc=1, device_id=to, device_id_type=MESH)

    greet(x_partner)
    greet(core_partner)

    def greet_z(off, _):
        greet(device(lax.rem(z + off, PLANES), chip, core))
        return 0

    def greet_plane(off, _):
        greet(device(z, lax.rem(chip + off, CHIPS), core))
        return 0

    def greet_all(plane):
        def body(other, _):
            greet(device(plane, other, core))
            return 0

        lax.fori_loop(0, CHIPS, body, 0)

    lax.fori_loop(1, PLANES, greet_z, 0)
    lax.fori_loop(1, CHIPS, greet_plane, 0)
    pl.when(jnp.logical_and(chip == 0, has_below))(lambda: greet_all(z - 1))
    pl.when(jnp.logical_and(chip == CHIPS - 1, has_above))(lambda: greet_all(z + 1))

    place = 2 * chip + core
    loads = [
        (filt_hbm, filt_in), (first_hbm, first), (twist_hbm, twist), (fwd_hbm, fwd), (back_hbm, back),
        (last_hbm, last), (planes_hbm.at[place], planes), (azf_hbm, azf_in), (shift_hbm, shift_in),
        (frac_hbm, frac_in), (ktab_hbm, ktab), (az_fwd_hbm, az_fwd), (az_back_hbm, az_back),
        (az_twist_hbm, az_twist),
    ]
    loads = [pltpu.make_async_copy(src, dst, load_sem.at[k]) for k, (src, dst) in enumerate(loads)]
    own_tiles = pltpu.make_async_copy(raw_hbm.at[:, xh], tiles.at[0], tile_sem)
    own_tiles.start()
    for load in loads:
        load.start()

    def blank(start, size):
        def body(other, _):
            g_ref[other, start : start + size, :] = jnp.zeros((size, LANES), F32)
            return 0

        lax.fori_loop(0, CHIPS, body, 0)

    pl.when(jnp.logical_and(chip == 0, z == 0))(lambda: blank(0, BELOW))
    pl.when(jnp.logical_and(chip == CHIPS - 1, z == PLANES - 1))(lambda: blank(PAIR - ABOVE, ABOVE))

    pl.semaphore_wait(
        barrier,
        2 + PLANES - 1 + CHIPS - 1 + jnp.where(has_below, 1, 0) + jnp.where(has_above, 1, 0),
    )

    to_x = pltpu.make_async_remote_copy(
        src_ref=raw_hbm.at[:, 1 - xh],
        dst_ref=tiles.at[1],
        send_sem=x_send,
        recv_sem=x_recv,
        device_id=x_partner,
        device_id_type=MESH,
    )
    to_x.start()

    def to_core(which):
        quarter = 2 * xh + core if which == 0 else 2 * (1 - xh) + core
        return pltpu.make_async_remote_copy(
            src_ref=outgoing.at[which],
            dst_ref=x_ref.at[:, :, pl.ds(pl.multiple_of(48 * quarter, 8), 48)],
            send_sem=core_send.at[which],
            recv_sem=core_recv.at[which],
            device_id=core_partner,
            device_id_type=MESH,
        )

    def sort_tiles(which):
        quarter = 2 * xh + core if which == 0 else 2 * (1 - xh) + core
        rows = pl.ds(pl.multiple_of(48 * quarter, 8), 48)
        for c in range(2):
            for r in range(LANE_PULSES):
                outgoing[which, c, r] = tiles[which, c, pl.ds(4 * (1 - core) + r, 48, stride=8), :]
        to_core(which).start()
        for c in range(2):
            for r in range(LANE_PULSES):
                x_ref[c, r, rows, :] = tiles[which, c, pl.ds(4 * core + r, 48, stride=8), :]

    own_tiles.wait()
    sort_tiles(0)

    for load in loads:
        load.wait()
    for c in range(2):
        cols = [filt_in[pl.ds(2 * u + c, 64, stride=6), :].T for u in range(3)]
        tall = jnp.concatenate(cols, axis=0)
        filt[c] = jnp.concatenate([tall[:ROWS], tall[ROWS:]], axis=1)

    to_x.wait_recv()
    sort_tiles(1)
    to_core(0).wait_recv()
    to_core(1).wait_recv()

    twist_re, twist_im = twist[0], twist[1]
    for half in range(2):
        pulses = (2 * half, 2 * half + 1)
        x = jnp.concatenate(
            [jnp.concatenate([x_ref[0, r], x_ref[1, r]], axis=0) for r in pulses], axis=1
        )
        v = times_left(first[...], x)
        rows = []
        for p in range(2):
            part = v[:, LANES * p : LANES * (p + 1)]
            rows.append(jnp.concatenate(cmul(part[:ROWS], part[ROWS:], twist_re, twist_im), axis=1))
        s = times_right(jnp.concatenate(rows, axis=0), fwd[...])
        rows = []
        for p in range(2):
            part = s[ROWS * p : ROWS * (p + 1)]
            rows.append(
                jnp.concatenate(cmul(part[:, :LANES], part[:, LANES:], filt[0], filt[1]), axis=1)
            )
        s = times_right(jnp.concatenate(rows, axis=0), back[...])
        for p in range(2):
            part = s[ROWS * p : ROWS * (p + 1)]
            turned = jnp.concatenate(
                cmul(part[:, :LANES], part[:, LANES:], twist_re, -twist_im), axis=0
            )
            high, low = split(turned)
            cols = slice(LANES * pulses[p], LANES * (pulses[p] + 1))
            v_ref[0 : 2 * ROWS, cols] = high
            v_ref[2 * ROWS : 4 * ROWS, cols] = low
            v_ref[4 * ROWS : 6 * ROWS, cols] = high

    def chunk_of(t):
        step = jnp.where(t == 0, ORDER[0], jnp.where(t == 1, ORDER[1], jnp.where(t == 2, ORDER[2], ORDER[3])))
        return lax.rem(y + step, CHUNKS)

    def z_copy(t, off):
        to = lax.rem(z + off, PLANES)
        return pltpu.make_async_remote_copy(
            src_ref=y_ref.at[t, to],
            dst_ref=z_ref.at[t, pl.ds(pl.multiple_of(PIECE * z, 8), PIECE)],
            send_sem=z_send.at[t, off],
            recv_sem=z_recv.at[t, off],
            device_id=device(to, chip, core),
            device_id_type=MESH,
        )

    def z_mine(t):
        return pltpu.make_async_copy(
            y_ref.at[t, z], z_ref.at[t, pl.ds(pl.multiple_of(PIECE * z, 8), PIECE)], z_own.at[t]
        )

    def send_chunk(t, _):
        out = jnp.dot(last[chunk_of(t)], v_ref[...], preferred_element_type=F32)
        size = 2 * CHUNK_ROWS
        for r in range(LANE_PULSES):
            for to in range(PLANES):
                y_ref[t, to, size * r : size * (r + 1), :] = out[
                    size * to : size * (to + 1), LANES * r : LANES * (r + 1)
                ]

        def start(near, _):
            z_copy(t, near).start()
            z_copy(t, PLANES - near).start()
            return 0

        z_copy(t, PLANES // 2).start()
        lax.fori_loop(1, PLANES // 2, start, 0)
        z_mine(t).start()
        return 0

    lax.fori_loop(0, CHUNKS, send_chunk, 0)

    def turn_filter(step, _):
        rows = pl.ds(pl.multiple_of(8 * step, 8), 8)
        for c in range(2):
            got = swap_blocks([azf_in[c, rows, LANES * k : LANES * (k + 1)] for k in range(16)], 1)
            for k1 in range(16):
                a_ref[c, k1, rows, :] = got[k1]
        return 0

    lax.fori_loop(0, BINS // 8, turn_filter, 0)

    def by_bin(values):
        tall = values.T
        return jnp.concatenate([tall[16 * u : 16 * (u + 1)] for u in range(8)], axis=1)

    shift_ref[...] = by_bin(shift_in[...])
    frac = by_bin(frac_in[...])
    for tap in range(TAPS):
        weight = jnp.zeros(frac.shape, F32)
        for row in range(16):
            weight = jnp.where(frac == row, ktab[tap, row], weight)
        w_ref[tap] = weight

    def main_copy(t, q, src, dst, size):
        return pltpu.make_async_remote_copy(
            src_ref=t_ref.at[t, pl.ds(src, size)],
            dst_ref=g_ref.at[chip, pl.ds(dst, size)],
            send_sem=p_send.at[t, q],
            recv_sem=p_recv.at[chip],
            device_id=device(z, 4 * chunk_of(t) + q, core),
            device_id_type=MESH,
        )

    def main_recv(other, src, dst, size):
        return pltpu.make_async_remote_copy(
            src_ref=t_ref.at[0, pl.ds(src, size)],
            dst_ref=g_ref.at[other, pl.ds(dst, size)],
            send_sem=p_send.at[0, 0],
            recv_sem=p_recv.at[other],
            device_id=core_partner,
            device_id_type=MESH,
        )

    def main_own(src, dst, size):
        return pltpu.make_async_copy(
            t_ref.at[CHUNKS - 1, pl.ds(src, size)], g_ref.at[chip, pl.ds(dst, size)], own_sem
        )

    def windows(q, act):
        pl.when(q == 0)(lambda: act(0, BELOW, PAIR - BELOW))
        pl.when(q == 3)(lambda: act(CHUNK - BELOW - 2 * BINS, 0, PAIR - ABOVE))
        middle = jnp.logical_and(q > 0, q < 3)
        pl.when(middle)(lambda: act(pl.multiple_of(2 * BINS * q - BELOW, 8), 0, PAIR))

    def halo_targets(chunk):
        down_chip = lax.rem(4 * chunk + CHIPS - 1, CHIPS)
        up_chip = lax.rem(4 * chunk + 4, CHIPS)
        down_plane = jnp.where(chunk == 0, z - 1, z)
        up_plane = jnp.where(chunk == CHUNKS - 1, z + 1, z)
        return down_plane, down_chip, up_plane, up_chip

    DOWN = (0, PAIR - ABOVE, ABOVE)
    UP = (CHUNK - BELOW, 0, BELOW)

    def halo_copy(t, which, plane, to):
        src, dst, size = (DOWN, UP)[which]
        return pltpu.make_async_remote_copy(
            src_ref=t_ref.at[t, pl.ds(src, size)],
            dst_ref=g_ref.at[chip, pl.ds(dst, size)],
            send_sem=h_send.at[t, which],
            recv_sem=h_recv.at[chip],
            device_id=device(plane, to, core),
            device_id_type=MESH,
        )

    def halo_mine(t, which):
        src, dst, size = (DOWN, UP)[which]
        return pltpu.make_async_copy(
            t_ref.at[t, pl.ds(src, size)], g_ref.at[chip, pl.ds(dst, size)], halo_own
        )

    def halo_recv(other, which):
        src, dst, size = (DOWN, UP)[which]
        return pltpu.make_async_remote_copy(
            src_ref=t_ref.at[0, pl.ds(src, size)],
            dst_ref=g_ref.at[other, pl.ds(dst, size)],
            send_sem=h_send.at[0, which],
            recv_sem=h_recv.at[other],
            device_id=core_partner,
            device_id_type=MESH,
        )

    def each_halo(t, remote, local):
        down_plane, down_chip, up_plane, up_chip = halo_targets(chunk_of(t))
        for which, plane, to in ((0, down_plane, down_chip), (1, up_plane, up_chip)):
            inside = jnp.logical_and(plane >= 0, plane < PLANES)
            me = jnp.logical_and(plane == z, to == chip)
            pl.when(jnp.logical_and(inside, jnp.logical_not(me)))(
                functools.partial(remote, t, which, plane, to)
            )
            pl.when(me)(functools.partial(local, t, which))

    def each_main(t, act):
        for off in range(4):
            q = lax.rem(q_me + off, 4)
            to_me = jnp.logical_and(t == CHUNKS - 1, off == 0)

            def remote(q=q):
                windows(q, functools.partial(act, t, q))

            pl.when(jnp.logical_not(to_me))(remote)

    def plane_step(t, _):
        def wait_z(off, _):
            z_copy(t, off).wait_recv()
            return 0

        lax.fori_loop(1, PLANES, wait_z, 0)
        z_mine(t).wait()
        for row in range(CHUNK_ROWS):
            parts = []
            for c in range(2):
                for r in range(LANE_PULSES):
                    start = CHUNK_ROWS * (2 * r + c) + row
                    parts.append(z_ref[t, pl.ds(start, PLANES, stride=PIECE), :])
            t_ref[t, LANES * row : LANES * (row + 1), :] = times_right(
                jnp.concatenate(parts, axis=0).T, planes[...]
            )
        each_main(t, lambda *a: main_copy(*a).start())

        def local(t, which):
            halo_mine(t, which).start()
            halo_mine(t, which).wait()

        each_halo(t, lambda *a: halo_copy(*a).start(), local)
        return 0

    lax.fori_loop(0, CHUNKS, plane_step, 0)

    def own(src, dst, size):
        main_own(src, dst, size).start()
        main_own(src, dst, size).wait()

    windows(q_me, own)

    def core_copy(row):
        return pltpu.make_async_remote_copy(
            src_ref=g_ref.at[pl.ds(4 * row, 4), pl.ds(pl.multiple_of(BINS * (1 - core), 8), WINDOW)],
            dst_ref=o_ref.at[pl.ds(4 * row, 4)],
            send_sem=fwd_send.at[row],
            recv_sem=fwd_recv.at[row],
            device_id=core_partner,
            device_id_type=MESH,
        )

    takes_up = jnp.logical_and(q_me == 0, jnp.logical_or(y > 0, has_below))
    takes_down = jnp.logical_and(q_me == 3, jnp.logical_or(y < 3, has_above))
    other_plane = jnp.where(q_me == 0, y == 0, y == 3)

    def gather(t, _):
        row = lax.rem(y + CHUNKS - chunk_of(t) + y, CHUNKS)

        def one(k, _):
            other = 4 * row + k
            mine = other == chip
            pl.when(jnp.logical_not(mine))(
                lambda: windows(q_me, lambda *a: main_recv(other, *a).wait_recv())
            )
            remote = jnp.logical_or(other_plane, jnp.logical_not(mine))
            pl.when(jnp.logical_and(takes_up, remote))(lambda: halo_recv(other, 1).wait_recv())
            pl.when(jnp.logical_and(takes_down, remote))(lambda: halo_recv(other, 0).wait_recv())
            return 0

        lax.fori_loop(0, 4, one, 0)
        core_copy(row).start()
        return 0

    lax.fori_loop(0, CHUNKS, gather, 0)

    def turn_own(step, _):
        rows = pl.ds(pl.multiple_of(8 * step, 8), 8)
        start = pl.ds(pl.multiple_of(BINS * core + 8 * step, 8), 8)
        got = swap_blocks([g_ref[k, start, :] for k in range(CHIPS)], 8)
        for k1 in range(16):
            h_ref[core, k1, rows, :] = got[k1]
        return 0

    def turn_other(step, _):
        rows = pl.ds(pl.multiple_of(8 * step, 8), 8)
        got = swap_blocks([o_ref[k, rows, :] for k in range(CHIPS)], 8)
        for k1 in range(16):
            h_ref[1 - core, k1, rows, :] = got[k1]
        return 0

    lax.fori_loop(0, WINDOW // 8, turn_own, 0)

    def wait_core(row, _):
        core_copy(row).wait_recv()
        return 0

    lax.fori_loop(0, 4, wait_core, 0)
    lax.fori_loop(0, WINDOW // 8, turn_other, 0)

    def per_bin(k1, _):
        d = times_right(jnp.concatenate([h_ref[0, k1], h_ref[1, k1]], axis=1), az_fwd[...])
        shift = shift_ref[pl.ds(k1, 1), :]
        weights = [w_ref[tap, pl.ds(k1, 1), :] for tap in range(TAPS)]
        moved = []
        for c in range(2):
            x = d[:, LANES * c : LANES * (c + 1)]
            near = jnp.where((shift & 16) != 0, x[16:80], x[0:64])
            x = jnp.concatenate([near, x[64:80]], axis=0)
            d_ref[c, 0:72] = jnp.where((shift & 8) != 0, x[8:80], x[0:72])
            e_ref[c, 0:64] = jnp.where((shift & 4) != 0, d_ref[c, 4:68], d_ref[c, 0:64])
            d_ref[c, 0:62] = jnp.where((shift & 2) != 0, e_ref[c, 2:64], e_ref[c, 0:62])
            e_ref[c, 0:61] = jnp.where((shift & 1) != 0, d_ref[c, 1:62], d_ref[c, 0:61])
            total = weights[0] * e_ref[c, 5 : 5 + BINS]
            for tap in range(1, TAPS):
                total = total + weights[tap] * e_ref[c, 5 + tap : 5 + tap + BINS]
            moved.append(total)
        re, im = cmul(moved[0], moved[1], a_ref[0, k1], a_ref[1, k1])
        s = times_right(jnp.concatenate([re, im], axis=1), az_back[...])
        re, im = cmul(
            s[:, :LANES], s[:, LANES:], az_twist[0, pl.ds(k1, 1), :], az_twist[1, pl.ds(k1, 1), :]
        )
        f_ref[0, k1] = re
        f_ref[1, k1] = im
        return 0

    lax.fori_loop(0, 16, per_bin, 0)

    def finish(step, _):
        rows = pl.ds(pl.multiple_of(8 * step, 8), 8)
        got = fft_list([(f_ref[0, k1, rows, :], f_ref[1, k1, rows, :]) for k1 in range(16)], 1)
        for tile in range(16):
            out_ref[0, rows, LANES * tile : LANES * (tile + 1)] = got[tile][0]
            out_ref[1, rows, LANES * tile : LANES * (tile + 1)] = got[tile][1]
        return 0

    lax.fori_loop(0, BINS // 8, finish, 0)

    to_x.wait_send()
    to_core(0).wait_send()
    to_core(1).wait_send()

    def wait_sends(t, _):
        def wait_z_send(off, _):
            z_copy(t, off).wait_send()
            return 0

        lax.fori_loop(1, PLANES, wait_z_send, 0)
        each_main(t, lambda *a: main_copy(*a).wait_send())
        each_halo(t, lambda *a: halo_copy(*a).wait_send(), lambda *a: None)
        core_copy(t).wait_send()
        return 0

    lax.fori_loop(0, CHUNKS, wait_sends, 0)


ANY = pl.BlockSpec(memory_space=pl.ANY)
DMA = pltpu.SemaphoreType.DMA


def shards(raw, range_filter, azimuth_filter, shifts, frac_index, kernel_table):
    order = filter_order()
    tables = [
        table_first(),
        table_last(),
        table_twist(),
        right_factor(table_columns(np.arange(LANES), order, -1)),
        right_factor(table_columns(order, np.arange(LANES), 1)),
        table_planes(),
        table_azimuth(),
        table_back(),
        table_back_twist(),
    ]
    operands = [
        raw.reshape(2, 2, 8, 48, LANES).transpose(0, 1, 3, 2, 4).reshape(2, 2, 384, LANES),
        range_filter.reshape(2, ROWS, LANES).transpose(1, 0, 2).reshape(2 * ROWS, LANES),
        azimuth_filter,
        shifts.reshape(16, LANES),
        frac_index.reshape(16, LANES),
        kernel_table.T,
    ]

    def like(array, shape=None):
        return pltpu.VMEM(array.shape if shape is None else shape, array.dtype)

    loads = [like(a) for a in operands[1:5]] + [pltpu.SMEM(operands[5].shape, F32)]
    loads += [like(a) for a in tables]
    loads[5 + 5] = like(tables[5], tables[5].shape[1:])
    scratch = [
        pltpu.VMEM((2, 2, 384, LANES), F32),
        pltpu.VMEM((2, 2, LANE_PULSES, 48, LANES), F32),
        pltpu.VMEM((2, LANE_PULSES, ROWS, LANES), F32),
        pltpu.VMEM((2, ROWS, LANES), F32),
        pltpu.VMEM((6 * ROWS, LANE_PULSES * LANES), BF16),
        pltpu.VMEM((CHUNKS, PLANES, PIECE, LANES), F32),
        pltpu.VMEM((CHUNKS, PLANES * PIECE, LANES), F32),
        pltpu.VMEM((CHUNKS, CHUNK, LANES), F32),
        pltpu.VMEM((CHIPS, PAIR, LANES), F32),
        pltpu.VMEM((CHIPS, WINDOW, LANES), F32),
        pltpu.VMEM((16, LANES), jnp.int32),
        pltpu.VMEM((TAPS, 16, LANES), F32),
        pltpu.VMEM((2, 16, BINS, LANES), F32),
        pltpu.VMEM((2, 16, WINDOW, LANES), F32),
        pltpu.VMEM((2, WINDOW, LANES), F32),
        pltpu.VMEM((2, WINDOW, LANES), F32),
        pltpu.VMEM((2, 16, BINS, LANES), F32),
        DMA, DMA, DMA, DMA((2,)), DMA((2,)),
        DMA((CHUNKS, PLANES)), DMA((CHUNKS, PLANES)), DMA((CHUNKS,)),
        DMA((CHUNKS, 4)), DMA((CHIPS,)), DMA((CHUNKS, 2)), DMA((CHIPS,)), DMA, DMA, DMA((4,)), DMA((4,)),
    ]
    return pl.pallas_call(
        kernel,
        out_shape=jax.ShapeDtypeStruct((2, BINS, PULSES), F32),
        in_specs=[ANY] * (len(operands) + len(tables)),
        out_specs=pl.BlockSpec(memory_space=pltpu.VMEM),
        scratch_shapes=loads + [DMA((len(loads),))] + scratch,
        compiler_params=pltpu.CompilerParams(
            vmem_limit_bytes=60 * 2**20, collective_id=0, has_side_effects=True
        ),
    )(*operands, *tables)


def solution(mesh):
    in_specs = (P(None, "pulse", "rng"), P(), P(None, ("pulse", "rng"), None), P(), P(), P())
    out_specs = P(None, ("pulse", "rng"), None)
    return jax.shard_map(shards, mesh=mesh, in_specs=in_specs, out_specs=out_specs, check_vma=False)
```

```python
import functools
import math

import jax
import jax.numpy as jnp
import ml_dtypes
import numpy as np
from jax import lax
from jax.experimental import pallas as pl
from jax.experimental.pallas import tpu as pltpu
from jax.sharding import PartitionSpec as P

MESH = pl.DeviceIdType.MESH
F32 = jnp.float32
BF16 = jnp.bfloat16

PULSES = 2048
SAMPLES = 24576
ROWS = 192
LANES = 128
PLANES = 16
PEERS = 32
CHIPS = 16
LANE_PULSES = 4
BINS = 48
CHUNKS = 4
CHUNK_ROWS = 3
CHUNK = CHUNK_ROWS * LANES
PIECE = 2 * CHUNK_ROWS * LANE_PULSES
BELOW = 8
ABOVE = 24
WINDOW = BELOW + BINS + ABOVE
PAIR = BELOW + 2 * BINS + ABOVE
TAPS = 8
ORDER = (2, 1, 3, 0)


def turn(product, period, sign):
    angle = sign * 2.0 * math.pi * (product % period) / period
    return np.cos(angle), np.sin(angle)


def halves(table):
    high = table.astype(ml_dtypes.bfloat16)
    low = (table - high.astype(np.float64)).astype(ml_dtypes.bfloat16)
    return high, low


def left_factor(table):
    high, low = halves(table)
    return np.concatenate([high, high, low], axis=1)


def right_factor(table):
    high, low = halves(table)
    return np.concatenate([high, high, low], axis=-2)


def lane_bins():
    lanes = np.arange(LANES)
    return 8 * (lanes % 16) + lanes // 16


def table_first():
    ids = np.arange(ROWS)
    re, im = turn(np.outer(ids, ids), ROWS, -1)
    return left_factor(np.block([[re, -im], [im, re]]))


def table_last():
    ids = np.arange(ROWS)
    re, im = turn(np.outer(ids, ids), ROWS, 1)
    full = np.stack([np.concatenate([re, -im], axis=1), np.concatenate([im, re], axis=1)]) / SAMPLES
    full = full.reshape(2, PLANES, CHUNKS, CHUNK_ROWS, 2 * ROWS).transpose(2, 1, 0, 3, 4)
    return left_factor(full.reshape(2 * ROWS, 2 * ROWS)).reshape(CHUNKS, 2 * ROWS // CHUNKS, -1)


def filter_order():
    lanes = np.arange(LANES)
    return 2 * (lanes % 64) + lanes // 64


def table_columns(rows, cols, sign, scale=1.0):
    re, im = turn(np.outer(rows, cols), LANES, sign)
    return np.block([[re, im], [-im, re]]) * scale


def table_twist():
    re, im = turn(np.outer(np.arange(ROWS), np.arange(LANES)), SAMPLES, -1)
    return np.stack([re, im]).astype(np.float32)


def table_planes():
    place = np.arange(PEERS)[:, None, None, None]
    r = np.arange(LANE_PULSES)[None, :, None, None]
    z = np.arange(PLANES)[None, None, :, None]
    k1 = np.arange(16)[None, None, None, :]
    re, im = turn((128 * z + 4 * place + r) * k1, PULSES, -1)
    full = np.zeros((PEERS, 2, LANE_PULSES, PLANES, 16, 2, LANE_PULSES))
    for q in range(LANE_PULSES):
        full[:, 0, q, :, :, 0, q] = re[:, q]
        full[:, 1, q, :, :, 0, q] = -im[:, q]
        full[:, 0, q, :, :, 1, q] = im[:, q]
        full[:, 1, q, :, :, 1, q] = re[:, q]
    return right_factor(full.reshape(PEERS, 128, 128))


def table_azimuth():
    place = np.arange(PEERS)[:, None, None]
    r = np.arange(LANE_PULSES)[None, :, None]
    re, im = turn((4 * place + r) * lane_bins()[None, None, :], LANES, -1)
    full = np.zeros((PEERS, 2, LANE_PULSES, 2, LANES))
    full[:, 0, :, 0] = re
    full[:, 1, :, 0] = -im
    full[:, 0, :, 1] = im
    full[:, 1, :, 1] = re
    by_core = full.reshape(CHIPS, 2, 8, 2 * LANES).transpose(1, 0, 2, 3)
    return right_factor(by_core.reshape(2, LANES, 2 * LANES))


def table_back():
    return right_factor(table_columns(lane_bins(), np.arange(LANES), 1, 1.0 / PULSES))


def table_back_twist():
    re, im = turn(np.outer(np.arange(16), np.arange(LANES)), PULSES, 1)
    return np.stack([re, im]).astype(np.float32)


def split(values):
    high = values.astype(BF16)
    low = (values - high.astype(F32)).astype(BF16)
    return high, low


def times_left(table, values):
    high, low = split(values)
    return jnp.dot(table, jnp.concatenate([high, low, high], axis=0), preferred_element_type=F32)


def times_right(values, table):
    high, low = split(values)
    return jnp.dot(jnp.concatenate([high, low, high], axis=1), table, preferred_element_type=F32)


def cmul(a_re, a_im, b_re, b_im):
    return a_re * b_re - a_im * b_im, a_re * b_im + a_im * b_re


def fft_list(values, sign):
    count = len(values)
    if count == 1:
        return values
    even = fft_list(values[0::2], sign)
    odd = fft_list(values[1::2], sign)
    low, high = [], []
    for k in range(count // 2):
        re, im = odd[k]
        if 4 * k == count:
            re, im = (-im, re) if sign > 0 else (im, -re)
        elif k:
            w_re = math.cos(2.0 * math.pi * k / count)
            w_im = sign * math.sin(2.0 * math.pi * k / count)
            re, im = re * w_re - im * w_im, re * w_im + im * w_re
        low.append((even[k][0] + re, even[k][1] + im))
        high.append((even[k][0] - re, even[k][1] - im))
    return low + high


def swap_blocks(arrays, width):
    arrays = list(arrays)
    lane = lax.broadcasted_iota(jnp.int32, arrays[0].shape, 1)
    for bit in (1, 2, 4, 8):
        keep = (lane // width) & bit == 0
        for a in range(16):
            if a & bit:
                continue
            first, second = arrays[a], arrays[a + bit]
            arrays[a] = jnp.where(keep, first, pltpu.roll(second, bit * width, 1))
            arrays[a + bit] = jnp.where(keep, pltpu.roll(first, LANES - bit * width, 1), second)
    return arrays


def kernel(
    raw_hbm, filt_hbm, azf_hbm, shift_hbm, frac_hbm, ktab_hbm,
    first_hbm, last_hbm, twist_hbm, fwd_hbm, back_hbm, planes_hbm, az_fwd_hbm, az_back_hbm, az_twist_hbm,
    out_ref,
    filt_in, azf_in, shift_in, frac_in, ktab, first, last, twist, fwd, back, planes, az_fwd, az_back, az_twist,
    load_sem,
    tiles, to_like, to_relay, relay, to_core, x_ref, filt, v_ref, y_ref, z_ref, t_ref, g_ref, o_ref,
    shift_ref, w_ref, a_ref, h_ref, d_ref, m_ref, e_ref, f_ref,
    tile_sem, x_send, x_recv, core_send, core_recv, z_send, z_recv, z_own,
    p_send, p_recv, h_send, h_recv, own_sem, halo_own, fwd_send, fwd_recv,
):
    pulse = lax.axis_index("pulse")
    lane = lax.axis_index("rng")
    z = lax.div(pulse, 8)
    y = lax.rem(lax.div(pulse, 2), 4)
    xh = lax.div(lane, 2)
    core = lax.rem(lane, 2)
    q_me = 2 * lax.rem(pulse, 2) + xh
    chip = 4 * y + q_me
    has_below = z > 0
    has_above = z < PLANES - 1

    def device(plane, other_chip, other_core):
        return (8 * plane + lax.div(other_chip, 2), 2 * lax.rem(other_chip, 2) + other_core)

    x_partner = (pulse, 2 * (1 - xh) + core)
    core_partner = (pulse, 2 * xh + 1 - core)

    barrier = pltpu.get_barrier_semaphore()

    def greet(to):
        pl.semaphore_signal(barrier, inc=1, device_id=to, device_id_type=MESH)

    greet(x_partner)
    greet(core_partner)

    def greet_z(off, _):
        greet(device(lax.rem(z + off, PLANES), chip, core))
        return 0

    def greet_plane(off, _):
        greet(device(z, lax.rem(chip + off, CHIPS), core))
        return 0

    def greet_all(plane):
        def body(other, _):
            greet(device(plane, other, core))
            return 0

        lax.fori_loop(0, CHIPS, body, 0)

    lax.fori_loop(1, PLANES, greet_z, 0)
    lax.fori_loop(1, CHIPS, greet_plane, 0)
    pl.when(jnp.logical_and(chip == 0, has_below))(lambda: greet_all(z - 1))
    pl.when(jnp.logical_and(chip == CHIPS - 1, has_above))(lambda: greet_all(z + 1))

    place = 2 * chip + core
    loads = [
        (filt_hbm, filt_in), (first_hbm, first), (twist_hbm, twist), (fwd_hbm, fwd), (back_hbm, back),
        (last_hbm, last), (planes_hbm.at[place], planes), (azf_hbm, azf_in), (shift_hbm, shift_in),
        (frac_hbm, frac_in), (ktab_hbm, ktab), (az_fwd_hbm, az_fwd), (az_back_hbm, az_back),
        (az_twist_hbm, az_twist),
    ]
    loads = [pltpu.make_async_copy(src, dst, load_sem.at[k]) for k, (src, dst) in enumerate(loads)]
    tile_loads = [
        pltpu.make_async_copy(raw_hbm.at[:, 1 - xh], tiles.at[1], tile_sem.at[1]),
        pltpu.make_async_copy(raw_hbm.at[:, xh], tiles.at[0], tile_sem.at[0]),
    ]
    for load in tile_loads + loads:
        load.start()

    def blank(start, size):
        def body(other, _):
            g_ref[other, start : start + size, :] = jnp.zeros((size, LANES), F32)
            return 0

        lax.fori_loop(0, CHIPS, body, 0)

    pl.when(jnp.logical_and(chip == 0, z == 0))(lambda: blank(0, BELOW))
    pl.when(jnp.logical_and(chip == CHIPS - 1, z == PLANES - 1))(lambda: blank(PAIR - ABOVE, ABOVE))

    my_quarter = 2 * xh + core
    x_quarter = 2 * (1 - xh) + core

    def quarter_rows(quarter):
        return pl.ds(pl.multiple_of(48 * quarter, 8), 48)

    for load in tile_loads:
        load.wait()
    for r in range(LANE_PULSES):
        like = pl.ds(4 * core + r, 48, stride=8)
        other = pl.ds(4 * (1 - core) + r, 48, stride=8)
        for c in range(2):
            to_like[r, c] = tiles[1, c, like, :]
            to_relay[r, c] = tiles[1, c, other, :]
            to_core[r, c] = tiles[0, c, other, :]
            x_ref[r, c, quarter_rows(my_quarter), :] = tiles[0, c, like, :]

    pl.semaphore_wait(
        barrier,
        2 + PLANES - 1 + CHIPS - 1 + jnp.where(has_below, 1, 0) + jnp.where(has_above, 1, 0),
    )

    def x_copy(r, which):
        return pltpu.make_async_remote_copy(
            src_ref=(to_like, to_relay)[which].at[r],
            dst_ref=x_ref.at[r, :, quarter_rows(my_quarter)] if which == 0 else relay.at[r],
            send_sem=x_send.at[r, which],
            recv_sem=x_recv.at[r, which],
            device_id=x_partner,
            device_id_type=MESH,
        )

    def core_swap(r, which):
        return pltpu.make_async_remote_copy(
            src_ref=(to_core, relay)[which].at[r],
            dst_ref=x_ref.at[r, :, quarter_rows((my_quarter, x_quarter)[which])],
            send_sem=core_send.at[r, which],
            recv_sem=core_recv.at[r, which],
            device_id=core_partner,
            device_id_type=MESH,
        )

    for r in range(LANE_PULSES):
        x_copy(r, 1).start()
        x_copy(r, 0).start()
    for r in range(LANE_PULSES):
        core_swap(r, 0).start()

    for load in loads:
        load.wait()
    for c in range(2):
        cols = [filt_in[pl.ds(2 * u + c, 64, stride=6), :].T for u in range(3)]
        tall = jnp.concatenate(cols, axis=0)
        filt[c] = jnp.concatenate([tall[:ROWS], tall[ROWS:]], axis=1)

    def compress(r):
        x_copy(r, 1).wait_recv()
        core_swap(r, 1).start()
        x_copy(r, 0).wait_recv()
        core_swap(r, 0).wait_recv()
        core_swap(r, 1).wait_recv()
        twist_re, twist_im = twist[0], twist[1]
        v = times_left(first[...], jnp.concatenate([x_ref[r, 0], x_ref[r, 1]], axis=0))
        re, im = cmul(v[:ROWS], v[ROWS:], twist_re, twist_im)
        s = times_right(jnp.concatenate([re, im], axis=1), fwd[...])
        re, im = cmul(s[:, :LANES], s[:, LANES:], filt[0], filt[1])
        s = times_right(jnp.concatenate([re, im], axis=1), back[...])
        re, im = cmul(s[:, :LANES], s[:, LANES:], twist_re, -twist_im)
        high, low = split(jnp.concatenate([re, im], axis=0))
        v_ref[r, 0 : 2 * ROWS] = high
        v_ref[r, 2 * ROWS : 4 * ROWS] = low
        v_ref[r, 4 * ROWS : 6 * ROWS] = high

    def chunk_of(t):
        step = jnp.where(t == 0, ORDER[0], jnp.where(t == 1, ORDER[1], jnp.where(t == 2, ORDER[2], ORDER[3])))
        return lax.rem(y + step, CHUNKS)

    def z_copy(block, off):
        to = lax.rem(z + off, PLANES)
        return pltpu.make_async_remote_copy(
            src_ref=y_ref.at[block, to],
            dst_ref=z_ref.at[block, pl.ds(pl.multiple_of(PIECE * z, 8), PIECE)],
            send_sem=z_send.at[block, off],
            recv_sem=z_recv.at[block, off],
            device_id=device(to, chip, core),
            device_id_type=MESH,
        )

    def z_mine(block):
        return pltpu.make_async_copy(
            y_ref.at[block, z], z_ref.at[block, pl.ds(pl.multiple_of(PIECE * z, 8), PIECE)], z_own.at[block]
        )

    def send_block(block):
        def start(near, _):
            z_copy(block, near).start()
            z_copy(block, PLANES - near).start()
            return 0

        z_copy(block, PLANES // 2).start()
        lax.fori_loop(1, PLANES // 2, start, 0)
        z_mine(block).start()

    size = 2 * CHUNK_ROWS

    def one_pulse(r, _):
        compress(r)
        for chunk in range(CHUNKS):
            out = jnp.dot(last[chunk], v_ref[r], preferred_element_type=F32)
            for to in range(PLANES):
                y_ref[r, to, size * chunk : size * (chunk + 1), :] = out[size * to : size * (to + 1)]
        send_block(r)
        return 0

    def two_chunks(pair, _):
        both = jnp.concatenate([v_ref[2], v_ref[3]], axis=1)
        for half in range(2):
            out = jnp.dot(last[chunk_of(2 * pair + half)], both, preferred_element_type=F32)
            for r in range(2):
                place = size * (2 * half + r)
                for to in range(PLANES):
                    y_ref[2 + pair, to, place : place + size, :] = out[
                        size * to : size * (to + 1), LANES * r : LANES * (r + 1)
                    ]
        send_block(2 + pair)
        return 0

    def later_pulse(r, _):
        compress(r)
        return 0

    lax.fori_loop(0, 2, one_pulse, 0)
    lax.fori_loop(2, 4, later_pulse, 0)
    lax.fori_loop(0, 2, two_chunks, 0)

    def turn_filter(step, _):
        rows = pl.ds(pl.multiple_of(8 * step, 8), 8)
        for c in range(2):
            got = swap_blocks([azf_in[c, rows, LANES * k : LANES * (k + 1)] for k in range(16)], 1)
            for k1 in range(16):
                a_ref[c, k1, rows, :] = got[k1]
        return 0

    lax.fori_loop(0, BINS // 8, turn_filter, 0)

    def by_bin(values):
        tall = values.T
        return jnp.concatenate([tall[16 * u : 16 * (u + 1)] for u in range(8)], axis=1)

    shift_ref[...] = by_bin(shift_in[...])
    frac = by_bin(frac_in[...])
    for tap in range(TAPS):
        weight = jnp.zeros(frac.shape, F32)
        for row in range(16):
            weight = jnp.where(frac == row, ktab[tap, row], weight)
        w_ref[tap] = weight

    def main_copy(t, q, src, dst, size):
        return pltpu.make_async_remote_copy(
            src_ref=t_ref.at[t, pl.ds(src, size)],
            dst_ref=g_ref.at[chip, pl.ds(dst, size)],
            send_sem=p_send.at[t, q],
            recv_sem=p_recv.at[chip],
            device_id=device(z, 4 * chunk_of(t) + q, core),
            device_id_type=MESH,
        )

    def main_recv(other, src, dst, size):
        return pltpu.make_async_remote_copy(
            src_ref=t_ref.at[0, pl.ds(src, size)],
            dst_ref=g_ref.at[other, pl.ds(dst, size)],
            send_sem=p_send.at[0, 0],
            recv_sem=p_recv.at[other],
            device_id=core_partner,
            device_id_type=MESH,
        )

    def main_own(src, dst, size):
        return pltpu.make_async_copy(
            t_ref.at[CHUNKS - 1, pl.ds(src, size)], g_ref.at[chip, pl.ds(dst, size)], own_sem
        )

    def windows(q, act):
        pl.when(q == 0)(lambda: act(0, BELOW, PAIR - BELOW))
        pl.when(q == 3)(lambda: act(CHUNK - BELOW - 2 * BINS, 0, PAIR - ABOVE))
        middle = jnp.logical_and(q > 0, q < 3)
        pl.when(middle)(lambda: act(pl.multiple_of(2 * BINS * q - BELOW, 8), 0, PAIR))

    def halo_targets(chunk):
        down_chip = lax.rem(4 * chunk + CHIPS - 1, CHIPS)
        up_chip = lax.rem(4 * chunk + 4, CHIPS)
        down_plane = jnp.where(chunk == 0, z - 1, z)
        up_plane = jnp.where(chunk == CHUNKS - 1, z + 1, z)
        return down_plane, down_chip, up_plane, up_chip

    DOWN = (0, PAIR - ABOVE, ABOVE)
    UP = (CHUNK - BELOW, 0, BELOW)

    def halo_copy(t, which, plane, to):
        src, dst, size = (DOWN, UP)[which]
        return pltpu.make_async_remote_copy(
            src_ref=t_ref.at[t, pl.ds(src, size)],
            dst_ref=g_ref.at[chip, pl.ds(dst, size)],
            send_sem=h_send.at[t, which],
            recv_sem=h_recv.at[chip],
            device_id=device(plane, to, core),
            device_id_type=MESH,
        )

    def halo_mine(t, which):
        src, dst, size = (DOWN, UP)[which]
        return pltpu.make_async_copy(
            t_ref.at[t, pl.ds(src, size)], g_ref.at[chip, pl.ds(dst, size)], halo_own
        )

    def halo_recv(other, which):
        src, dst, size = (DOWN, UP)[which]
        return pltpu.make_async_remote_copy(
            src_ref=t_ref.at[0, pl.ds(src, size)],
            dst_ref=g_ref.at[other, pl.ds(dst, size)],
            send_sem=h_send.at[0, which],
            recv_sem=h_recv.at[other],
            device_id=core_partner,
            device_id_type=MESH,
        )

    def each_halo(t, remote, local):
        down_plane, down_chip, up_plane, up_chip = halo_targets(chunk_of(t))
        for which, plane, to in ((0, down_plane, down_chip), (1, up_plane, up_chip)):
            inside = jnp.logical_and(plane >= 0, plane < PLANES)
            me = jnp.logical_and(plane == z, to == chip)
            pl.when(jnp.logical_and(inside, jnp.logical_not(me)))(
                functools.partial(remote, t, which, plane, to)
            )
            pl.when(me)(functools.partial(local, t, which))

    def each_main(t, act):
        for off in range(4):
            q = lax.rem(q_me + off, 4)
            to_me = jnp.logical_and(t == CHUNKS - 1, off == 0)

            def remote(q=q):
                windows(q, functools.partial(act, t, q))

            pl.when(jnp.logical_not(to_me))(remote)

    def wait_block(block, _):
        def wait_z(off, _):
            z_copy(block, off).wait_recv()
            return 0

        lax.fori_loop(1, PLANES, wait_z, 0)
        z_mine(block).wait()
        return 0

    def plane_step(t, _):
        @pl.when(t == 0)
        def _():
            lax.fori_loop(0, 3, wait_block, 0)

        @pl.when(t == 2)
        def _():
            wait_block(3, 0)

        pair = lax.div(t, 2)
        half = lax.rem(t, 2)
        chunk = chunk_of(t)
        for row in range(CHUNK_ROWS):
            parts = []
            for c in range(2):
                for r in range(2):
                    start = size * chunk + CHUNK_ROWS * c + row
                    parts.append(z_ref[r, pl.ds(start, PLANES, stride=PIECE), :])
                for r in range(2):
                    start = size * (2 * half + r) + CHUNK_ROWS * c + row
                    parts.append(z_ref[2 + pair, pl.ds(start, PLANES, stride=PIECE), :])
            t_ref[t, LANES * row : LANES * (row + 1), :] = times_right(
                jnp.concatenate(parts, axis=0).T, planes[...]
            )
        each_main(t, lambda *a: main_copy(*a).start())

        def local(t, which):
            halo_mine(t, which).start()
            halo_mine(t, which).wait()

        each_halo(t, lambda *a: halo_copy(*a).start(), local)
        return 0

    lax.fori_loop(0, CHUNKS, plane_step, 0)

    def own(src, dst, size):
        main_own(src, dst, size).start()
        main_own(src, dst, size).wait()

    windows(q_me, own)

    def core_copy(row):
        return pltpu.make_async_remote_copy(
            src_ref=g_ref.at[pl.ds(4 * row, 4), pl.ds(pl.multiple_of(BINS * (1 - core), 8), WINDOW)],
            dst_ref=o_ref.at[pl.ds(4 * row, 4)],
            send_sem=fwd_send.at[row],
            recv_sem=fwd_recv.at[row],
            device_id=core_partner,
            device_id_type=MESH,
        )

    takes_up = jnp.logical_and(q_me == 0, jnp.logical_or(y > 0, has_below))
    takes_down = jnp.logical_and(q_me == 3, jnp.logical_or(y < 3, has_above))
    other_plane = jnp.where(q_me == 0, y == 0, y == 3)

    def gather(t, _):
        row = lax.rem(y + CHUNKS - chunk_of(t) + y, CHUNKS)

        def one(k, _):
            other = 4 * row + k
            mine = other == chip
            pl.when(jnp.logical_not(mine))(
                lambda: windows(q_me, lambda *a: main_recv(other, *a).wait_recv())
            )
            remote = jnp.logical_or(other_plane, jnp.logical_not(mine))
            pl.when(jnp.logical_and(takes_up, remote))(lambda: halo_recv(other, 1).wait_recv())
            pl.when(jnp.logical_and(takes_down, remote))(lambda: halo_recv(other, 0).wait_recv())
            return 0

        lax.fori_loop(0, 4, one, 0)
        core_copy(row).start()
        return 0

    lax.fori_loop(0, CHUNKS, gather, 0)

    part = WINDOW // 2

    def turn_rows(read):
        def body(step, _):
            rows = pl.ds(pl.multiple_of(part * step, 8), part)
            got = swap_blocks([read(k, part * step) for k in range(CHIPS)], 8)
            for k1 in range(16):
                h_ref[k1, rows, :] = got[k1]
            return 0

        lax.fori_loop(0, WINDOW // part, body, 0)

    group = 4

    def transform(from_core, add):
        def body(step, _):
            high, low = split(h_ref[pl.ds(group * step, group)].reshape(group * WINDOW, LANES))
            d = jnp.dot(
                jnp.concatenate([high, low, high], axis=1), az_fwd[from_core], preferred_element_type=F32
            )
            for k in range(group):
                for c in range(2):
                    piece = d[WINDOW * k : WINDOW * (k + 1), LANES * c : LANES * (c + 1)]
                    if add:
                        piece = piece + d_ref[group * step + k, c]
                    d_ref[group * step + k, c] = piece
            return 0

        lax.fori_loop(0, 16 // group, body, 0)

    turn_rows(lambda k, start: g_ref[k, pl.ds(pl.multiple_of(BINS * core + start, 8), part), :])
    transform(core, False)

    def wait_core(row, _):
        core_copy(row).wait_recv()
        return 0

    lax.fori_loop(0, 4, wait_core, 0)
    turn_rows(lambda k, start: o_ref[k, pl.ds(pl.multiple_of(start, 8), part), :])
    transform(1 - core, True)

    def migrate(k1, slot):
        shift = shift_ref[pl.ds(k1, 1), :]
        weights = [w_ref[tap, pl.ds(k1, 1), :] for tap in range(TAPS)]
        moved = []
        for c in range(2):
            x = d_ref[k1, c]
            near = jnp.where((shift & 16) != 0, x[16:80], x[0:64])
            x = jnp.concatenate([near, x[64:80]], axis=0)
            m, e = m_ref.at[slot, c], e_ref.at[slot, c]
            m[0:72] = jnp.where((shift & 8) != 0, x[8:80], x[0:72])
            e[0:64] = jnp.where((shift & 4) != 0, m[4:68], m[0:64])
            m[0:62] = jnp.where((shift & 2) != 0, e[2:64], e[0:62])
            e[0:61] = jnp.where((shift & 1) != 0, m[1:62], m[0:61])
            total = weights[0] * e[5 : 5 + BINS]
            for tap in range(1, TAPS):
                total = total + weights[tap] * e[5 + tap : 5 + tap + BINS]
            moved.append(total)
        return jnp.concatenate(cmul(moved[0], moved[1], a_ref[0, k1], a_ref[1, k1]), axis=1)

    def per_group(step, _):
        ks = [group * step + k for k in range(group)]
        s = times_right(jnp.concatenate([migrate(k1, k) for k, k1 in enumerate(ks)], axis=0), az_back[...])
        for k, k1 in enumerate(ks):
            rows = slice(BINS * k, BINS * (k + 1))
            f_ref[0, k1], f_ref[1, k1] = cmul(
                s[rows, :LANES], s[rows, LANES:], az_twist[0, pl.ds(k1, 1), :], az_twist[1, pl.ds(k1, 1), :]
            )
        return 0

    lax.fori_loop(0, 16 // group, per_group, 0)

    def finish(step, _):
        rows = pl.ds(pl.multiple_of(8 * step, 8), 8)
        got = fft_list([(f_ref[0, k1, rows, :], f_ref[1, k1, rows, :]) for k1 in range(16)], 1)
        for tile in range(16):
            out_ref[0, rows, LANES * tile : LANES * (tile + 1)] = got[tile][0]
            out_ref[1, rows, LANES * tile : LANES * (tile + 1)] = got[tile][1]
        return 0

    lax.fori_loop(0, BINS // 8, finish, 0)

    for r in range(LANE_PULSES):
        for which in range(2):
            x_copy(r, which).wait_send()
            core_swap(r, which).wait_send()

    def wait_sends(t, _):
        def wait_z_send(off, _):
            z_copy(t, off).wait_send()
            return 0

        lax.fori_loop(1, PLANES, wait_z_send, 0)
        each_main(t, lambda *a: main_copy(*a).wait_send())
        each_halo(t, lambda *a: halo_copy(*a).wait_send(), lambda *a: None)
        core_copy(t).wait_send()
        return 0

    lax.fori_loop(0, CHUNKS, wait_sends, 0)


ANY = pl.BlockSpec(memory_space=pl.ANY)
DMA = pltpu.SemaphoreType.DMA


def shards(raw, range_filter, azimuth_filter, shifts, frac_index, kernel_table):
    order = filter_order()
    tables = [
        table_first(),
        table_last(),
        table_twist(),
        right_factor(table_columns(np.arange(LANES), order, -1)),
        right_factor(table_columns(order, np.arange(LANES), 1)),
        table_planes(),
        table_azimuth(),
        table_back(),
        table_back_twist(),
    ]
    operands = [
        raw.reshape(2, 2, 8, 48, LANES).transpose(0, 1, 3, 2, 4).reshape(2, 2, 384, LANES),
        range_filter.reshape(2, ROWS, LANES).transpose(1, 0, 2).reshape(2 * ROWS, LANES),
        azimuth_filter,
        shifts.reshape(16, LANES),
        frac_index.reshape(16, LANES),
        kernel_table.T,
    ]

    def like(array, shape=None):
        return pltpu.VMEM(array.shape if shape is None else shape, array.dtype)

    loads = [like(a) for a in operands[1:5]] + [pltpu.SMEM(operands[5].shape, F32)]
    loads += [like(a) for a in tables]
    loads[5 + 5] = like(tables[5], tables[5].shape[1:])
    scratch = [
        pltpu.VMEM((2, 2, 384, LANES), F32),
        pltpu.VMEM((LANE_PULSES, 2, 48, LANES), F32),
        pltpu.VMEM((LANE_PULSES, 2, 48, LANES), F32),
        pltpu.VMEM((LANE_PULSES, 2, 48, LANES), F32),
        pltpu.VMEM((LANE_PULSES, 2, 48, LANES), F32),
        pltpu.VMEM((LANE_PULSES, 2, ROWS, LANES), F32),
        pltpu.VMEM((2, ROWS, LANES), F32),
        pltpu.VMEM((LANE_PULSES, 6 * ROWS, LANES), BF16),
        pltpu.VMEM((CHUNKS, PLANES, PIECE, LANES), F32),
        pltpu.VMEM((CHUNKS, PLANES * PIECE, LANES), F32),
        pltpu.VMEM((CHUNKS, CHUNK, LANES), F32),
        pltpu.VMEM((CHIPS, PAIR, LANES), F32),
        pltpu.VMEM((CHIPS, WINDOW, LANES), F32),
        pltpu.VMEM((16, LANES), jnp.int32),
        pltpu.VMEM((TAPS, 16, LANES), F32),
        pltpu.VMEM((2, 16, BINS, LANES), F32),
        pltpu.VMEM((16, WINDOW, LANES), F32),
        pltpu.VMEM((16, 2, WINDOW, LANES), F32),
        pltpu.VMEM((4, 2, WINDOW, LANES), F32),
        pltpu.VMEM((4, 2, WINDOW, LANES), F32),
        pltpu.VMEM((2, 16, BINS, LANES), F32),
        DMA((2,)), DMA((4, 2)), DMA((4, 2)), DMA((4, 2)), DMA((4, 2)),
        DMA((CHUNKS, PLANES)), DMA((CHUNKS, PLANES)), DMA((CHUNKS,)),
        DMA((CHUNKS, 4)), DMA((CHIPS,)), DMA((CHUNKS, 2)), DMA((CHIPS,)), DMA, DMA, DMA((4,)), DMA((4,)),
    ]
    return pl.pallas_call(
        kernel,
        out_shape=jax.ShapeDtypeStruct((2, BINS, PULSES), F32),
        in_specs=[ANY] * (len(operands) + len(tables)),
        out_specs=pl.BlockSpec(memory_space=pltpu.VMEM),
        scratch_shapes=loads + [DMA((len(loads),))] + scratch,
        compiler_params=pltpu.CompilerParams(
            vmem_limit_bytes=60 * 2**20, collective_id=0, has_side_effects=True
        ),
    )(*operands, *tables)


def solution(mesh):
    in_specs = (P(None, "pulse", "rng"), P(), P(None, ("pulse", "rng"), None), P(), P(), P())
    out_specs = P(None, ("pulse", "rng"), None)
    return jax.shard_map(shards, mesh=mesh, in_specs=in_specs, out_specs=out_specs, check_vma=False)
```

```python
import functools
import math

import jax
import jax.numpy as jnp
import ml_dtypes
import numpy as np
from jax import lax
from jax.experimental import pallas as pl
from jax.experimental.pallas import tpu as pltpu
from jax.sharding import PartitionSpec as P

MESH = pl.DeviceIdType.MESH
F32 = jnp.float32
BF16 = jnp.bfloat16

PULSES = 2048
SAMPLES = 24576
ROWS = 192
LANES = 128
PLANES = 16
PEERS = 32
CHIPS = 16
LANE_PULSES = 4
BINS = 48
CHUNKS = 4
CHUNK_ROWS = 3
CHUNK = CHUNK_ROWS * LANES
PIECE = 2 * CHUNK_ROWS * LANE_PULSES
BELOW = 8
ABOVE = 24
WINDOW = BELOW + BINS + ABOVE
PAIR = BELOW + 2 * BINS + ABOVE
TAPS = 8
ORDER = ((2, 1, 3, 0), (2, 3, 1, 0))


def turn(product, period, sign):
    angle = sign * 2.0 * math.pi * (product % period) / period
    return np.cos(angle), np.sin(angle)


def halves(table):
    high = table.astype(ml_dtypes.bfloat16)
    low = (table - high.astype(np.float64)).astype(ml_dtypes.bfloat16)
    return high, low


def left_factor(table):
    high, low = halves(table)
    return np.concatenate([high, high, low], axis=1)


def right_factor(table):
    high, low = halves(table)
    return np.concatenate([high, high, low], axis=-2)


def lane_bins():
    lanes = np.arange(LANES)
    return 8 * (lanes % 16) + lanes // 16


def table_first():
    ids = np.arange(ROWS)
    re, im = turn(np.outer(ids, ids), ROWS, -1)
    return left_factor(np.block([[re, -im], [im, re]]))


def table_last():
    ids = np.arange(ROWS)
    re, im = turn(np.outer(ids, ids), ROWS, 1)
    full = np.stack([np.concatenate([re, -im], axis=1), np.concatenate([im, re], axis=1)]) / SAMPLES
    full = full.reshape(2, PLANES, CHUNKS, CHUNK_ROWS, 2 * ROWS).transpose(2, 1, 0, 3, 4)
    return left_factor(full.reshape(2 * ROWS, 2 * ROWS)).reshape(CHUNKS, 2 * ROWS // CHUNKS, -1)


def filter_order():
    lanes = np.arange(LANES)
    return 2 * (lanes % 64) + lanes // 64


def table_columns(rows, cols, sign, scale=1.0):
    re, im = turn(np.outer(rows, cols), LANES, sign)
    return np.block([[re, im], [-im, re]]) * scale


def table_twist():
    re, im = turn(np.outer(np.arange(ROWS), np.arange(LANES)), SAMPLES, -1)
    return np.stack([re, im]).astype(np.float32)


def table_planes():
    place = np.arange(PEERS)[:, None, None, None]
    r = np.arange(LANE_PULSES)[None, :, None, None]
    z = np.arange(PLANES)[None, None, :, None]
    k1 = np.arange(16)[None, None, None, :]
    re, im = turn((128 * z + 4 * place + r) * k1, PULSES, -1)
    full = np.zeros((PEERS, 2, LANE_PULSES, PLANES, 16, 2, LANE_PULSES))
    for q in range(LANE_PULSES):
        full[:, 0, q, :, :, 0, q] = re[:, q]
        full[:, 1, q, :, :, 0, q] = -im[:, q]
        full[:, 0, q, :, :, 1, q] = im[:, q]
        full[:, 1, q, :, :, 1, q] = re[:, q]
    return right_factor(full.reshape(PEERS, 128, 128))


def table_azimuth():
    place = np.arange(PEERS)[:, None, None]
    r = np.arange(LANE_PULSES)[None, :, None]
    re, im = turn((4 * place + r) * lane_bins()[None, None, :], LANES, -1)
    full = np.zeros((PEERS, 2, LANE_PULSES, 2, LANES))
    full[:, 0, :, 0] = re
    full[:, 1, :, 0] = -im
    full[:, 0, :, 1] = im
    full[:, 1, :, 1] = re
    by_core = full.reshape(CHIPS, 2, 8, 2 * LANES).transpose(1, 0, 2, 3)
    return right_factor(by_core.reshape(2, LANES, 2 * LANES))


def table_back():
    return right_factor(table_columns(lane_bins(), np.arange(LANES), 1, 1.0 / PULSES))


def table_back_twist():
    re, im = turn(np.outer(np.arange(16), np.arange(LANES)), PULSES, 1)
    return np.stack([re, im]).astype(np.float32)


def split(values):
    high = values.astype(BF16)
    low = (values - high.astype(F32)).astype(BF16)
    return high, low


def times_left(table, values):
    high, low = split(values)
    return jnp.dot(table, jnp.concatenate([high, low, high], axis=0), preferred_element_type=F32)


def times_right(values, table):
    high, low = split(values)
    return jnp.dot(jnp.concatenate([high, low, high], axis=1), table, preferred_element_type=F32)


def cmul(a_re, a_im, b_re, b_im):
    return a_re * b_re - a_im * b_im, a_re * b_im + a_im * b_re


def fft_list(values, sign):
    count = len(values)
    if count == 1:
        return values
    even = fft_list(values[0::2], sign)
    odd = fft_list(values[1::2], sign)
    low, high = [], []
    for k in range(count // 2):
        re, im = odd[k]
        if 4 * k == count:
            re, im = (-im, re) if sign > 0 else (im, -re)
        elif k:
            w_re = math.cos(2.0 * math.pi * k / count)
            w_im = sign * math.sin(2.0 * math.pi * k / count)
            re, im = re * w_re - im * w_im, re * w_im + im * w_re
        low.append((even[k][0] + re, even[k][1] + im))
        high.append((even[k][0] - re, even[k][1] - im))
    return low + high


def swap_blocks(arrays, width):
    arrays = list(arrays)
    lane = lax.broadcasted_iota(jnp.int32, arrays[0].shape, 1)
    for bit in (1, 2, 4, 8):
        keep = (lane // width) & bit == 0
        for a in range(16):
            if a & bit:
                continue
            first, second = arrays[a], arrays[a + bit]
            arrays[a] = jnp.where(keep, first, pltpu.roll(second, bit * width, 1))
            arrays[a + bit] = jnp.where(keep, pltpu.roll(first, LANES - bit * width, 1), second)
    return arrays


def kernel(
    raw_hbm, filt_hbm, azf_hbm, shift_hbm, frac_hbm, ktab_hbm,
    first_hbm, last_hbm, twist_hbm, fwd_hbm, back_hbm, planes_hbm, az_fwd_hbm, az_back_hbm, az_twist_hbm,
    out_ref,
    filt_in, azf_in, shift_in, frac_in, ktab, first, last, twist, fwd, back, planes, az_fwd, az_back, az_twist,
    load_sem,
    tiles, to_like, to_relay, relay, to_core, x_ref, filt, v_ref, y_ref, z_ref, t_ref, g_ref, o_ref,
    shift_ref, w_ref, a_ref, h_ref, d_ref, m_ref, e_ref, f_ref,
    tile_sem, x_send, x_recv, core_send, core_recv, z_send, z_recv, z_own,
    p_send, p_recv, h_send, h_recv, own_sem, halo_own, fwd_send, fwd_recv,
):
    pulse = lax.axis_index("pulse")
    lane = lax.axis_index("rng")
    z = lax.div(pulse, 8)
    y = lax.rem(lax.div(pulse, 2), 4)
    xh = lax.div(lane, 2)
    core = lax.rem(lane, 2)
    q_me = 2 * lax.rem(pulse, 2) + xh
    chip = 4 * y + q_me
    has_below = z > 0
    has_above = z < PLANES - 1

    def device(plane, other_chip, other_core):
        return (8 * plane + lax.div(other_chip, 2), 2 * lax.rem(other_chip, 2) + other_core)

    x_partner = (pulse, 2 * (1 - xh) + core)
    core_partner = (pulse, 2 * xh + 1 - core)

    barrier = pltpu.get_barrier_semaphore()

    def greet(to):
        pl.semaphore_signal(barrier, inc=1, device_id=to, device_id_type=MESH)

    greet(x_partner)
    greet(core_partner)

    def greet_z(off, _):
        greet(device(lax.rem(z + off, PLANES), chip, core))
        return 0

    def greet_plane(off, _):
        greet(device(z, lax.rem(chip + off, CHIPS), core))
        return 0

    def greet_all(plane):
        def body(other, _):
            greet(device(plane, other, core))
            return 0

        lax.fori_loop(0, CHIPS, body, 0)

    lax.fori_loop(1, PLANES, greet_z, 0)
    lax.fori_loop(1, CHIPS, greet_plane, 0)
    pl.when(jnp.logical_and(chip == 0, has_below))(lambda: greet_all(z - 1))
    pl.when(jnp.logical_and(chip == CHIPS - 1, has_above))(lambda: greet_all(z + 1))

    place = 2 * chip + core
    loads = [
        (filt_hbm, filt_in), (first_hbm, first), (twist_hbm, twist), (fwd_hbm, fwd), (back_hbm, back),
        (last_hbm, last), (planes_hbm.at[place], planes), (azf_hbm, azf_in), (shift_hbm, shift_in),
        (frac_hbm, frac_in), (ktab_hbm, ktab), (az_fwd_hbm, az_fwd), (az_back_hbm, az_back),
        (az_twist_hbm, az_twist),
    ]
    loads = [pltpu.make_async_copy(src, dst, load_sem.at[k]) for k, (src, dst) in enumerate(loads)]
    tile_loads = [
        pltpu.make_async_copy(raw_hbm.at[:, 1 - xh], tiles.at[1], tile_sem.at[1]),
        pltpu.make_async_copy(raw_hbm.at[:, xh], tiles.at[0], tile_sem.at[0]),
    ]
    for load in tile_loads + loads:
        load.start()

    def blank(start, size):
        def body(other, _):
            g_ref[other, start : start + size, :] = jnp.zeros((size, LANES), F32)
            return 0

        lax.fori_loop(0, CHIPS, body, 0)

    pl.when(jnp.logical_and(chip == 0, z == 0))(lambda: blank(0, BELOW))
    pl.when(jnp.logical_and(chip == CHIPS - 1, z == PLANES - 1))(lambda: blank(PAIR - ABOVE, ABOVE))

    my_quarter = 2 * xh + core
    x_quarter = 2 * (1 - xh) + core

    def quarter_rows(quarter):
        return pl.ds(pl.multiple_of(48 * quarter, 8), 48)

    for load in tile_loads:
        load.wait()
    for r in range(LANE_PULSES):
        like = pl.ds(4 * core + r, 48, stride=8)
        other = pl.ds(4 * (1 - core) + r, 48, stride=8)
        for c in range(2):
            to_like[r, c] = tiles[1, c, like, :]
            to_relay[r, c] = tiles[1, c, other, :]
            to_core[r, c] = tiles[0, c, other, :]
            x_ref[r, c, quarter_rows(my_quarter), :] = tiles[0, c, like, :]

    pl.semaphore_wait(
        barrier,
        2 + PLANES - 1 + CHIPS - 1 + jnp.where(has_below, 1, 0) + jnp.where(has_above, 1, 0),
    )

    def x_copy(r, which):
        return pltpu.make_async_remote_copy(
            src_ref=(to_like, to_relay)[which].at[r],
            dst_ref=x_ref.at[r, :, quarter_rows(my_quarter)] if which == 0 else relay.at[r],
            send_sem=x_send.at[r, which],
            recv_sem=x_recv.at[r, which],
            device_id=x_partner,
            device_id_type=MESH,
        )

    def core_swap(r, which):
        return pltpu.make_async_remote_copy(
            src_ref=(to_core, relay)[which].at[r],
            dst_ref=x_ref.at[r, :, quarter_rows((my_quarter, x_quarter)[which])],
            send_sem=core_send.at[r, which],
            recv_sem=core_recv.at[r, which],
            device_id=core_partner,
            device_id_type=MESH,
        )

    def send_pulse(r):
        x_copy(r, 1).start()
        x_copy(r, 0).start()
        core_swap(r, 0).start()

    send_pulse(0)

    for load in loads:
        load.wait()
    for c in range(2):
        cols = [filt_in[pl.ds(2 * u + c, 64, stride=6), :].T for u in range(3)]
        tall = jnp.concatenate(cols, axis=0)
        filt[c] = jnp.concatenate([tall[:ROWS], tall[ROWS:]], axis=1)

    def compress(r):
        x_copy(r, 1).wait_recv()
        core_swap(r, 1).start()
        x_copy(r, 0).wait_recv()
        pl.when(r < LANE_PULSES - 1)(lambda: send_pulse(r + 1))
        core_swap(r, 0).wait_recv()
        core_swap(r, 1).wait_recv()
        twist_re, twist_im = twist[0], twist[1]
        v = times_left(first[...], jnp.concatenate([x_ref[r, 0], x_ref[r, 1]], axis=0))
        re, im = cmul(v[:ROWS], v[ROWS:], twist_re, twist_im)
        s = times_right(jnp.concatenate([re, im], axis=1), fwd[...])
        re, im = cmul(s[:, :LANES], s[:, LANES:], filt[0], filt[1])
        s = times_right(jnp.concatenate([re, im], axis=1), back[...])
        re, im = cmul(s[:, :LANES], s[:, LANES:], twist_re, -twist_im)
        high, low = split(jnp.concatenate([re, im], axis=0))
        v_ref[r, 0 : 2 * ROWS] = high
        v_ref[r, 2 * ROWS : 4 * ROWS] = low
        v_ref[r, 4 * ROWS : 6 * ROWS] = high

    def chunk_of(t):
        one, three = jnp.where(core == 0, t == 1, t == 2), jnp.where(core == 0, t == 2, t == 1)
        step = jnp.where(t == 0, 2, jnp.where(one, 1, jnp.where(three, 3, 0)))
        return lax.rem(y + step, CHUNKS)

    def z_copy(block, off):
        to = lax.rem(z + off, PLANES)
        return pltpu.make_async_remote_copy(
            src_ref=y_ref.at[block, to],
            dst_ref=z_ref.at[block, pl.ds(pl.multiple_of(PIECE * z, 8), PIECE)],
            send_sem=z_send.at[block, off],
            recv_sem=z_recv.at[block, off],
            device_id=device(to, chip, core),
            device_id_type=MESH,
        )

    def z_mine(block):
        return pltpu.make_async_copy(
            y_ref.at[block, z], z_ref.at[block, pl.ds(pl.multiple_of(PIECE * z, 8), PIECE)], z_own.at[block]
        )

    def send_block(block):
        def start(step, _):
            near = PLANES // 2 - step
            z_copy(block, near).start()
            z_copy(block, PLANES - near).start()
            return 0

        z_copy(block, PLANES // 2).start()
        lax.fori_loop(1, PLANES // 2, start, 0)
        z_mine(block).start()

    def sent_block(block):
        def wait_z_send(off, _):
            z_copy(block, off).wait_send()
            return 0

        lax.fori_loop(1, PLANES, wait_z_send, 0)

    size = 2 * CHUNK_ROWS

    def one_pulse(r, _):
        compress(r)
        for chunk in range(CHUNKS):
            out = jnp.dot(last[chunk], v_ref[r], preferred_element_type=F32)
            for to in range(PLANES):
                y_ref[r, to, size * chunk : size * (chunk + 1), :] = out[size * to : size * (to + 1)]
        send_block(r)
        return 0

    def two_chunks(pair, _):
        both = jnp.concatenate([v_ref[2], v_ref[3]], axis=1)
        for half in range(2):
            out = jnp.dot(last[chunk_of(2 * pair + half)], both, preferred_element_type=F32)
            for r in range(2):
                place = size * (2 * half + r)
                for to in range(PLANES):
                    y_ref[2 + pair, to, place : place + size, :] = out[
                        size * to : size * (to + 1), LANES * r : LANES * (r + 1)
                    ]
        return 0

    def later_pulse(r, _):
        compress(r)
        return 0

    lax.fori_loop(0, 2, one_pulse, 0)
    lax.fori_loop(2, 4, later_pulse, 0)
    lax.fori_loop(0, 2, two_chunks, 0)

    def turn_filter(step, _):
        rows = pl.ds(pl.multiple_of(8 * step, 8), 8)
        for c in range(2):
            got = swap_blocks([azf_in[c, rows, LANES * k : LANES * (k + 1)] for k in range(16)], 1)
            for k1 in range(16):
                a_ref[c, k1, rows, :] = got[k1]
        return 0

    lax.fori_loop(0, BINS // 8, turn_filter, 0)

    def by_bin(values):
        tall = values.T
        return jnp.concatenate([tall[16 * u : 16 * (u + 1)] for u in range(8)], axis=1)

    shift_ref[...] = by_bin(shift_in[...])
    frac = by_bin(frac_in[...])
    for tap in range(TAPS):
        weight = jnp.zeros(frac.shape, F32)
        for row in range(16):
            weight = jnp.where(frac == row, ktab[tap, row], weight)
        w_ref[tap] = weight

    def next_block(block, _):
        sent_block(block)
        send_block(block + 2)
        return 0

    lax.fori_loop(0, 2, next_block, 0)

    def main_copy(t, q, src, dst, size):
        return pltpu.make_async_remote_copy(
            src_ref=t_ref.at[t, pl.ds(src, size)],
            dst_ref=g_ref.at[chip, pl.ds(dst, size)],
            send_sem=p_send.at[t, q],
            recv_sem=p_recv.at[chip],
            device_id=device(z, 4 * chunk_of(t) + q, core),
            device_id_type=MESH,
        )

    def main_recv(other, src, dst, size):
        return pltpu.make_async_remote_copy(
            src_ref=t_ref.at[0, pl.ds(src, size)],
            dst_ref=g_ref.at[other, pl.ds(dst, size)],
            send_sem=p_send.at[0, 0],
            recv_sem=p_recv.at[other],
            device_id=core_partner,
            device_id_type=MESH,
        )

    def main_own(src, dst, size):
        return pltpu.make_async_copy(
            t_ref.at[CHUNKS - 1, pl.ds(src, size)], g_ref.at[chip, pl.ds(dst, size)], own_sem
        )

    def windows(q, act):
        pl.when(q == 0)(lambda: act(0, BELOW, PAIR - BELOW))
        pl.when(q == 3)(lambda: act(CHUNK - BELOW - 2 * BINS, 0, PAIR - ABOVE))
        middle = jnp.logical_and(q > 0, q < 3)
        pl.when(middle)(lambda: act(pl.multiple_of(2 * BINS * q - BELOW, 8), 0, PAIR))

    def halo_targets(chunk):
        down_chip = lax.rem(4 * chunk + CHIPS - 1, CHIPS)
        up_chip = lax.rem(4 * chunk + 4, CHIPS)
        down_plane = jnp.where(chunk == 0, z - 1, z)
        up_plane = jnp.where(chunk == CHUNKS - 1, z + 1, z)
        return down_plane, down_chip, up_plane, up_chip

    DOWN = (0, PAIR - ABOVE, ABOVE)
    UP = (CHUNK - BELOW, 0, BELOW)

    def halo_copy(t, which, plane, to):
        src, dst, size = (DOWN, UP)[which]
        return pltpu.make_async_remote_copy(
            src_ref=t_ref.at[t, pl.ds(src, size)],
            dst_ref=g_ref.at[chip, pl.ds(dst, size)],
            send_sem=h_send.at[t, which],
            recv_sem=h_recv.at[chip],
            device_id=device(plane, to, core),
            device_id_type=MESH,
        )

    def halo_mine(t, which):
        src, dst, size = (DOWN, UP)[which]
        return pltpu.make_async_copy(
            t_ref.at[t, pl.ds(src, size)], g_ref.at[chip, pl.ds(dst, size)], halo_own
        )

    def halo_recv(other, which):
        src, dst, size = (DOWN, UP)[which]
        return pltpu.make_async_remote_copy(
            src_ref=t_ref.at[0, pl.ds(src, size)],
            dst_ref=g_ref.at[other, pl.ds(dst, size)],
            send_sem=h_send.at[0, which],
            recv_sem=h_recv.at[other],
            device_id=core_partner,
            device_id_type=MESH,
        )

    def each_halo(t, remote, local):
        down_plane, down_chip, up_plane, up_chip = halo_targets(chunk_of(t))
        for which, plane, to in ((0, down_plane, down_chip), (1, up_plane, up_chip)):
            inside = jnp.logical_and(plane >= 0, plane < PLANES)
            me = jnp.logical_and(plane == z, to == chip)
            pl.when(jnp.logical_and(inside, jnp.logical_not(me)))(
                functools.partial(remote, t, which, plane, to)
            )
            pl.when(me)(functools.partial(local, t, which))

    def each_main(t, act):
        for off in range(4):
            q = lax.rem(q_me + off, 4)
            to_me = jnp.logical_and(t == CHUNKS - 1, off == 0)

            def remote(q=q):
                windows(q, functools.partial(act, t, q))

            pl.when(jnp.logical_not(to_me))(remote)

    def wait_block(block, _):
        def wait_z(off, _):
            z_copy(block, off).wait_recv()
            return 0

        lax.fori_loop(1, PLANES, wait_z, 0)
        z_mine(block).wait()
        return 0

    def plane_step(t, _):
        @pl.when(t == 0)
        def _():
            lax.fori_loop(0, 3, wait_block, 0)

        @pl.when(t == 2)
        def _():
            wait_block(3, 0)

        pair = lax.div(t, 2)
        half = lax.rem(t, 2)
        chunk = chunk_of(t)
        for row in range(CHUNK_ROWS):
            parts = []
            for c in range(2):
                for r in range(2):
                    start = size * chunk + CHUNK_ROWS * c + row
                    parts.append(z_ref[r, pl.ds(start, PLANES, stride=PIECE), :])
                for r in range(2):
                    start = size * (2 * half + r) + CHUNK_ROWS * c + row
                    parts.append(z_ref[2 + pair, pl.ds(start, PLANES, stride=PIECE), :])
            t_ref[t, LANES * row : LANES * (row + 1), :] = times_right(
                jnp.concatenate(parts, axis=0).T, planes[...]
            )
        each_main(t, lambda *a: main_copy(*a).start())

        def local(t, which):
            halo_mine(t, which).start()
            halo_mine(t, which).wait()

        each_halo(t, lambda *a: halo_copy(*a).start(), local)
        return 0

    lax.fori_loop(0, CHUNKS, plane_step, 0)

    def own(src, dst, size):
        main_own(src, dst, size).start()
        main_own(src, dst, size).wait()

    windows(q_me, own)

    def core_copy(row):
        return pltpu.make_async_remote_copy(
            src_ref=g_ref.at[pl.ds(4 * row, 4), pl.ds(pl.multiple_of(BINS * (1 - core), 8), WINDOW)],
            dst_ref=o_ref.at[pl.ds(4 * row, 4)],
            send_sem=fwd_send.at[row],
            recv_sem=fwd_recv.at[row],
            device_id=core_partner,
            device_id_type=MESH,
        )

    takes_up = jnp.logical_and(q_me == 0, jnp.logical_or(y > 0, has_below))
    takes_down = jnp.logical_and(q_me == 3, jnp.logical_or(y < 3, has_above))
    other_plane = jnp.where(q_me == 0, y == 0, y == 3)

    def gather(t, _):
        row = lax.rem(y + CHUNKS - chunk_of(t) + y, CHUNKS)

        def one(k, _):
            other = 4 * row + k
            mine = other == chip
            pl.when(jnp.logical_not(mine))(
                lambda: windows(q_me, lambda *a: main_recv(other, *a).wait_recv())
            )
            remote = jnp.logical_or(other_plane, jnp.logical_not(mine))
            pl.when(jnp.logical_and(takes_up, remote))(lambda: halo_recv(other, 1).wait_recv())
            pl.when(jnp.logical_and(takes_down, remote))(lambda: halo_recv(other, 0).wait_recv())
            return 0

        lax.fori_loop(0, 4, one, 0)
        core_copy(row).start()
        return 0

    lax.fori_loop(0, CHUNKS, gather, 0)

    part = WINDOW // 2

    def turn_rows(read):
        def body(step, _):
            rows = pl.ds(pl.multiple_of(part * step, 8), part)
            got = swap_blocks([read(k, part * step) for k in range(CHIPS)], 8)
            for k1 in range(16):
                h_ref[k1, rows, :] = got[k1]
            return 0

        lax.fori_loop(0, WINDOW // part, body, 0)

    group = 4

    def transform(from_core, add):
        def body(step, _):
            high, low = split(h_ref[pl.ds(group * step, group)].reshape(group * WINDOW, LANES))
            d = jnp.dot(
                jnp.concatenate([high, low, high], axis=1), az_fwd[from_core], preferred_element_type=F32
            )
            for k in range(group):
                for c in range(2):
                    piece = d[WINDOW * k : WINDOW * (k + 1), LANES * c : LANES * (c + 1)]
                    if add:
                        piece = piece + d_ref[group * step + k, c]
                    d_ref[group * step + k, c] = piece
            return 0

        lax.fori_loop(0, 16 // group, body, 0)

    turn_rows(lambda k, start: g_ref[k, pl.ds(pl.multiple_of(BINS * core + start, 8), part), :])
    transform(core, False)

    def wait_core(row, _):
        core_copy(row).wait_recv()
        return 0

    lax.fori_loop(0, 4, wait_core, 0)
    turn_rows(lambda k, start: o_ref[k, pl.ds(pl.multiple_of(start, 8), part), :])
    transform(1 - core, True)

    def migrate(k1, slot):
        shift = shift_ref[pl.ds(k1, 1), :]
        weights = [w_ref[tap, pl.ds(k1, 1), :] for tap in range(TAPS)]
        moved = []
        for c in range(2):
            x = d_ref[k1, c]
            near = jnp.where((shift & 16) != 0, x[16:80], x[0:64])
            x = jnp.concatenate([near, x[64:80]], axis=0)
            m, e = m_ref.at[slot, c], e_ref.at[slot, c]
            m[0:72] = jnp.where((shift & 8) != 0, x[8:80], x[0:72])
            e[0:64] = jnp.where((shift & 4) != 0, m[4:68], m[0:64])
            m[0:62] = jnp.where((shift & 2) != 0, e[2:64], e[0:62])
            e[0:61] = jnp.where((shift & 1) != 0, m[1:62], m[0:61])
            total = weights[0] * e[5 : 5 + BINS]
            for tap in range(1, TAPS):
                total = total + weights[tap] * e[5 + tap : 5 + tap + BINS]
            moved.append(total)
        return jnp.concatenate(cmul(moved[0], moved[1], a_ref[0, k1], a_ref[1, k1]), axis=1)

    def per_group(step, _):
        ks = [group * step + k for k in range(group)]
        s = times_right(jnp.concatenate([migrate(k1, k) for k, k1 in enumerate(ks)], axis=0), az_back[...])
        for k, k1 in enumerate(ks):
            rows = slice(BINS * k, BINS * (k + 1))
            f_ref[0, k1], f_ref[1, k1] = cmul(
                s[rows, :LANES], s[rows, LANES:], az_twist[0, pl.ds(k1, 1), :], az_twist[1, pl.ds(k1, 1), :]
            )
        return 0

    lax.fori_loop(0, 16 // group, per_group, 0)

    def finish(step, _):
        rows = pl.ds(pl.multiple_of(8 * step, 8), 8)
        got = fft_list([(f_ref[0, k1, rows, :], f_ref[1, k1, rows, :]) for k1 in range(16)], 1)
        for tile in range(16):
            out_ref[0, rows, LANES * tile : LANES * (tile + 1)] = got[tile][0]
            out_ref[1, rows, LANES * tile : LANES * (tile + 1)] = got[tile][1]
        return 0

    lax.fori_loop(0, BINS // 8, finish, 0)

    for r in range(LANE_PULSES):
        for which in range(2):
            x_copy(r, which).wait_send()
            core_swap(r, which).wait_send()

    def wait_sends(t, _):
        pl.when(t >= 2)(lambda: sent_block(t))
        each_main(t, lambda *a: main_copy(*a).wait_send())
        each_halo(t, lambda *a: halo_copy(*a).wait_send(), lambda *a: None)
        core_copy(t).wait_send()
        return 0

    lax.fori_loop(0, CHUNKS, wait_sends, 0)


ANY = pl.BlockSpec(memory_space=pl.ANY)
DMA = pltpu.SemaphoreType.DMA


def shards(raw, range_filter, azimuth_filter, shifts, frac_index, kernel_table):
    order = filter_order()
    tables = [
        table_first(),
        table_last(),
        table_twist(),
        right_factor(table_columns(np.arange(LANES), order, -1)),
        right_factor(table_columns(order, np.arange(LANES), 1)),
        table_planes(),
        table_azimuth(),
        table_back(),
        table_back_twist(),
    ]
    operands = [
        raw.reshape(2, 2, 8, 48, LANES).transpose(0, 1, 3, 2, 4).reshape(2, 2, 384, LANES),
        range_filter.reshape(2, ROWS, LANES).transpose(1, 0, 2).reshape(2 * ROWS, LANES),
        azimuth_filter,
        shifts.reshape(16, LANES),
        frac_index.reshape(16, LANES),
        kernel_table.T,
    ]

    def like(array, shape=None):
        return pltpu.VMEM(array.shape if shape is None else shape, array.dtype)

    loads = [like(a) for a in operands[1:5]] + [pltpu.SMEM(operands[5].shape, F32)]
    loads += [like(a) for a in tables]
    loads[5 + 5] = like(tables[5], tables[5].shape[1:])
    scratch = [
        pltpu.VMEM((2, 2, 384, LANES), F32),
        pltpu.VMEM((LANE_PULSES, 2, 48, LANES), F32),
        pltpu.VMEM((LANE_PULSES, 2, 48, LANES), F32),
        pltpu.VMEM((LANE_PULSES, 2, 48, LANES), F32),
        pltpu.VMEM((LANE_PULSES, 2, 48, LANES), F32),
        pltpu.VMEM((LANE_PULSES, 2, ROWS, LANES), F32),
        pltpu.VMEM((2, ROWS, LANES), F32),
        pltpu.VMEM((LANE_PULSES, 6 * ROWS, LANES), BF16),
        pltpu.VMEM((CHUNKS, PLANES, PIECE, LANES), F32),
        pltpu.VMEM((CHUNKS, PLANES * PIECE, LANES), F32),
        pltpu.VMEM((CHUNKS, CHUNK, LANES), F32),
        pltpu.VMEM((CHIPS, PAIR, LANES), F32),
        pltpu.VMEM((CHIPS, WINDOW, LANES), F32),
        pltpu.VMEM((16, LANES), jnp.int32),
        pltpu.VMEM((TAPS, 16, LANES), F32),
        pltpu.VMEM((2, 16, BINS, LANES), F32),
        pltpu.VMEM((16, WINDOW, LANES), F32),
        pltpu.VMEM((16, 2, WINDOW, LANES), F32),
        pltpu.VMEM((4, 2, WINDOW, LANES), F32),
        pltpu.VMEM((4, 2, WINDOW, LANES), F32),
        pltpu.VMEM((2, 16, BINS, LANES), F32),
        DMA((2,)), DMA((4, 2)), DMA((4, 2)), DMA((4, 2)), DMA((4, 2)),
        DMA((CHUNKS, PLANES)), DMA((CHUNKS, PLANES)), DMA((CHUNKS,)),
        DMA((CHUNKS, 4)), DMA((CHIPS,)), DMA((CHUNKS, 2)), DMA((CHIPS,)), DMA, DMA, DMA((4,)), DMA((4,)),
    ]
    return pl.pallas_call(
        kernel,
        out_shape=jax.ShapeDtypeStruct((2, BINS, PULSES), F32),
        in_specs=[ANY] * (len(operands) + len(tables)),
        out_specs=pl.BlockSpec(memory_space=pltpu.VMEM),
        scratch_shapes=loads + [DMA((len(loads),))] + scratch,
        compiler_params=pltpu.CompilerParams(
            vmem_limit_bytes=60 * 2**20, collective_id=0, has_side_effects=True
        ),
    )(*operands, *tables)


def solution(mesh):
    in_specs = (P(None, "pulse", "rng"), P(), P(None, ("pulse", "rng"), None), P(), P(), P())
    out_specs = P(None, ("pulse", "rng"), None)
    return jax.shard_map(shards, mesh=mesh, in_specs=in_specs, out_specs=out_specs, check_vma=False)
```

```python
import functools
import math

import jax
import jax.numpy as jnp
import ml_dtypes
import numpy as np
from jax import lax
from jax.experimental import pallas as pl
from jax.experimental.pallas import tpu as pltpu
from jax.sharding import PartitionSpec as P

MESH = pl.DeviceIdType.MESH
F32 = jnp.float32
BF16 = jnp.bfloat16

PULSES = 2048
SAMPLES = 24576
ROWS = 192
LANES = 128
PLANES = 16
PEERS = 32
CHIPS = 16
LANE_PULSES = 4
BINS = 48
CHUNKS = 4
CHUNK_ROWS = 3
CHUNK = CHUNK_ROWS * LANES
PIECE = 2 * CHUNK_ROWS * LANE_PULSES
BELOW = 8
ABOVE = 24
WINDOW = BELOW + BINS + ABOVE
PAIR = BELOW + 2 * BINS + ABOVE
TAPS = 8
ORDER = ((2, 1, 3, 0), (2, 3, 1, 0))


def turn(product, period, sign):
    angle = sign * 2.0 * math.pi * (product % period) / period
    return np.cos(angle), np.sin(angle)


def halves(table):
    high = table.astype(ml_dtypes.bfloat16)
    low = (table - high.astype(np.float64)).astype(ml_dtypes.bfloat16)
    return high, low


def left_factor(table):
    high, low = halves(table)
    return np.concatenate([high, high, low], axis=1)


def right_factor(table):
    high, low = halves(table)
    return np.concatenate([high, high, low], axis=-2)


def lane_bins():
    lanes = np.arange(LANES)
    return 8 * (lanes % 16) + lanes // 16


def table_first():
    ids = np.arange(ROWS)
    re, im = turn(np.outer(ids, ids), ROWS, -1)
    return left_factor(np.block([[re, -im], [im, re]]))


def table_last():
    ids = np.arange(ROWS)
    re, im = turn(np.outer(ids, ids), ROWS, 1)
    full = np.stack([np.concatenate([re, -im], axis=1), np.concatenate([im, re], axis=1)]) / SAMPLES
    full = full.reshape(2, PLANES, CHUNKS, CHUNK_ROWS, 2 * ROWS).transpose(2, 1, 0, 3, 4)
    return left_factor(full.reshape(2 * ROWS, 2 * ROWS)).reshape(CHUNKS, 2 * ROWS // CHUNKS, -1)


def filter_order():
    lanes = np.arange(LANES)
    return 2 * (lanes % 64) + lanes // 64


def table_columns(rows, cols, sign, scale=1.0):
    re, im = turn(np.outer(rows, cols), LANES, sign)
    return np.block([[re, im], [-im, re]]) * scale


def table_twist():
    re, im = turn(np.outer(np.arange(ROWS), np.arange(LANES)), SAMPLES, -1)
    return np.stack([re, im]).astype(np.float32)


def table_planes():
    place = np.arange(PEERS)[:, None, None, None]
    r = np.arange(LANE_PULSES)[None, :, None, None]
    z = np.arange(PLANES)[None, None, :, None]
    k1 = np.arange(16)[None, None, None, :]
    re, im = turn((128 * z + 4 * place + r) * k1, PULSES, -1)
    full = np.zeros((PEERS, 2, LANE_PULSES, PLANES, 16, 2, LANE_PULSES))
    for q in range(LANE_PULSES):
        full[:, 0, q, :, :, 0, q] = re[:, q]
        full[:, 1, q, :, :, 0, q] = -im[:, q]
        full[:, 0, q, :, :, 1, q] = im[:, q]
        full[:, 1, q, :, :, 1, q] = re[:, q]
    return right_factor(full.reshape(PEERS, 128, 128))


def table_azimuth():
    place = np.arange(PEERS)[:, None, None]
    r = np.arange(LANE_PULSES)[None, :, None]
    re, im = turn((4 * place + r) * lane_bins()[None, None, :], LANES, -1)
    full = np.zeros((PEERS, 2, LANE_PULSES, 2, LANES))
    full[:, 0, :, 0] = re
    full[:, 1, :, 0] = -im
    full[:, 0, :, 1] = im
    full[:, 1, :, 1] = re
    by_core = full.reshape(CHIPS, 2, 8, 2 * LANES).transpose(1, 0, 2, 3)
    return right_factor(by_core.reshape(2, LANES, 2 * LANES))


def table_back():
    return right_factor(table_columns(lane_bins(), np.arange(LANES), 1, 1.0 / PULSES))


def table_back_twist():
    re, im = turn(np.outer(np.arange(16), np.arange(LANES)), PULSES, 1)
    return np.stack([re, im]).astype(np.float32)


def split(values):
    high = values.astype(BF16)
    low = (values - high.astype(F32)).astype(BF16)
    return high, low


def times_left(table, values):
    high, low = split(values)
    return jnp.dot(table, jnp.concatenate([high, low, high], axis=0), preferred_element_type=F32)


def times_right(values, table):
    high, low = split(values)
    return jnp.dot(jnp.concatenate([high, low, high], axis=1), table, preferred_element_type=F32)


def cmul(a_re, a_im, b_re, b_im):
    return a_re * b_re - a_im * b_im, a_re * b_im + a_im * b_re


def fft_list(values, sign):
    count = len(values)
    if count == 1:
        return values
    even = fft_list(values[0::2], sign)
    odd = fft_list(values[1::2], sign)
    low, high = [], []
    for k in range(count // 2):
        re, im = odd[k]
        if 4 * k == count:
            re, im = (-im, re) if sign > 0 else (im, -re)
        elif k:
            w_re = math.cos(2.0 * math.pi * k / count)
            w_im = sign * math.sin(2.0 * math.pi * k / count)
            re, im = re * w_re - im * w_im, re * w_im + im * w_re
        low.append((even[k][0] + re, even[k][1] + im))
        high.append((even[k][0] - re, even[k][1] - im))
    return low + high


def swap_blocks(arrays, width):
    arrays = list(arrays)
    lane = lax.broadcasted_iota(jnp.int32, arrays[0].shape, 1)
    for bit in (1, 2, 4, 8):
        keep = (lane // width) & bit == 0
        for a in range(16):
            if a & bit:
                continue
            first, second = arrays[a], arrays[a + bit]
            arrays[a] = jnp.where(keep, first, pltpu.roll(second, bit * width, 1))
            arrays[a + bit] = jnp.where(keep, pltpu.roll(first, LANES - bit * width, 1), second)
    return arrays


def kernel(
    raw_hbm, filt_hbm, azf_hbm, shift_hbm, frac_hbm, ktab_hbm,
    first_hbm, last_hbm, twist_hbm, fwd_hbm, back_hbm, planes_hbm, az_fwd_hbm, az_back_hbm, az_twist_hbm,
    out_hbm,
    filt_in, azf_in, shift_in, frac_in, ktab, first, last, twist, fwd, back, planes, az_fwd, az_back, az_twist,
    load_sem,
    tiles, to_like, to_relay, relay, to_core, x_ref, filt, v_ref, y_ref, z_ref, t_ref, g_ref, o_ref,
    shift_ref, w_ref, a_ref, h_ref, d_ref, m_ref, e_ref, f_ref,
    tile_sem, x_send, x_recv, core_send, core_recv, z_send, z_recv,
    p_send, p_recv, h_send, h_recv, fwd_send, fwd_recv, out_sem,
):
    pulse = lax.axis_index("pulse")
    lane = lax.axis_index("rng")
    z = lax.div(pulse, 8)
    y = lax.rem(lax.div(pulse, 2), 4)
    xh = lax.div(lane, 2)
    core = lax.rem(lane, 2)
    q_me = 2 * lax.rem(pulse, 2) + xh
    chip = 4 * y + q_me
    has_below = z > 0
    has_above = z < PLANES - 1

    def device(plane, other_chip, other_core):
        return (8 * plane + lax.div(other_chip, 2), 2 * lax.rem(other_chip, 2) + other_core)

    x_partner = (pulse, 2 * (1 - xh) + core)
    core_partner = (pulse, 2 * xh + 1 - core)

    place = 2 * chip + core
    loads = [
        (filt_hbm, filt_in), (first_hbm, first), (twist_hbm, twist), (fwd_hbm, fwd), (back_hbm, back),
        (last_hbm, last), (planes_hbm.at[place], planes), (azf_hbm, azf_in), (shift_hbm, shift_in),
        (frac_hbm, frac_in), (ktab_hbm, ktab), (az_fwd_hbm, az_fwd), (az_back_hbm, az_back),
        (az_twist_hbm, az_twist),
    ]
    loads = [pltpu.make_async_copy(src, dst, load_sem.at[k]) for k, (src, dst) in enumerate(loads)]
    tile_loads = [
        pltpu.make_async_copy(raw_hbm.at[:, 1 - xh], tiles.at[1], tile_sem.at[1]),
        pltpu.make_async_copy(raw_hbm.at[:, xh], tiles.at[0], tile_sem.at[0]),
    ]
    for load in tile_loads:
        load.start()

    barrier = pltpu.get_barrier_semaphore()

    def greet(to):
        pl.semaphore_signal(barrier, inc=1, device_id=to, device_id_type=MESH)

    greet(x_partner)
    greet(core_partner)

    def greet_z(off, _):
        greet(device(lax.rem(z + off, PLANES), chip, core))
        return 0

    def greet_plane(off, _):
        greet(device(z, lax.rem(chip + off, CHIPS), core))
        return 0

    def greet_all(plane):
        def body(other, _):
            greet(device(plane, other, core))
            return 0

        lax.fori_loop(0, CHIPS, body, 0)

    lax.fori_loop(1, PLANES, greet_z, 0)
    lax.fori_loop(1, CHIPS, greet_plane, 0)
    pl.when(jnp.logical_and(chip == 0, has_below))(lambda: greet_all(z - 1))
    pl.when(jnp.logical_and(chip == CHIPS - 1, has_above))(lambda: greet_all(z + 1))

    for load in loads:
        load.start()

    def blank(start, size):
        def body(other, _):
            g_ref[other, start : start + size, :] = jnp.zeros((size, LANES), F32)
            return 0

        lax.fori_loop(0, CHIPS, body, 0)

    pl.when(jnp.logical_and(chip == 0, z == 0))(lambda: blank(0, BELOW))
    pl.when(jnp.logical_and(chip == CHIPS - 1, z == PLANES - 1))(lambda: blank(PAIR - ABOVE, ABOVE))

    my_quarter = 2 * xh + core
    x_quarter = 2 * (1 - xh) + core

    def quarter_rows(quarter):
        return pl.ds(pl.multiple_of(48 * quarter, 8), 48)

    for load in tile_loads:
        load.wait()
    def sort_pulse(r):
        like = pl.ds(4 * core + r, 48, stride=8)
        other = pl.ds(4 * (1 - core) + r, 48, stride=8)
        for c in range(2):
            to_like[r, c] = tiles[1, c, like, :]
            to_relay[r, c] = tiles[1, c, other, :]
            to_core[r, c] = tiles[0, c, other, :]
            x_ref[r, c, quarter_rows(my_quarter), :] = tiles[0, c, like, :]

    sort_pulse(0)
    pl.semaphore_wait(
        barrier,
        2 + PLANES - 1 + CHIPS - 1 + jnp.where(has_below, 1, 0) + jnp.where(has_above, 1, 0),
    )

    def x_copy(r, which):
        return pltpu.make_async_remote_copy(
            src_ref=(to_like, to_relay)[which].at[r],
            dst_ref=x_ref.at[r, :, quarter_rows(my_quarter)] if which == 0 else relay.at[r],
            send_sem=x_send.at[r, which],
            recv_sem=x_recv.at[r, which],
            device_id=x_partner,
            device_id_type=MESH,
        )

    def core_swap(r, which):
        return pltpu.make_async_remote_copy(
            src_ref=(to_core, relay)[which].at[r],
            dst_ref=x_ref.at[r, :, quarter_rows((my_quarter, x_quarter)[which])],
            send_sem=core_send.at[r, which],
            recv_sem=core_recv.at[r, which],
            device_id=core_partner,
            device_id_type=MESH,
        )

    def send_pulse(r):
        x_copy(r, 1).start()
        x_copy(r, 0).start()
        core_swap(r, 0).start()

    send_pulse(0)
    for r in range(1, LANE_PULSES):
        sort_pulse(r)

    for load in loads:
        load.wait()
    for c in range(2):
        cols = [filt_in[pl.ds(2 * u + c, 64, stride=6), :].T for u in range(3)]
        tall = jnp.concatenate(cols, axis=0)
        filt[c] = jnp.concatenate([tall[:ROWS], tall[ROWS:]], axis=1)

    def compress(r):
        x_copy(r, 1).wait_recv()
        core_swap(r, 1).start()
        x_copy(r, 0).wait_recv()
        pl.when(r < LANE_PULSES - 1)(lambda: send_pulse(r + 1))
        core_swap(r, 0).wait_recv()
        core_swap(r, 1).wait_recv()
        twist_re, twist_im = twist[0], twist[1]
        v = times_left(first[...], jnp.concatenate([x_ref[r, 0], x_ref[r, 1]], axis=0))
        re, im = cmul(v[:ROWS], v[ROWS:], twist_re, twist_im)
        s = times_right(jnp.concatenate([re, im], axis=1), fwd[...])
        re, im = cmul(s[:, :LANES], s[:, LANES:], filt[0], filt[1])
        s = times_right(jnp.concatenate([re, im], axis=1), back[...])
        re, im = cmul(s[:, :LANES], s[:, LANES:], twist_re, -twist_im)
        high, low = split(jnp.concatenate([re, im], axis=0))
        v_ref[r, 0 : 2 * ROWS] = high
        v_ref[r, 2 * ROWS : 4 * ROWS] = low
        v_ref[r, 4 * ROWS : 6 * ROWS] = high

    def chunk_of(t):
        one, three = jnp.where(core == 0, t == 1, t == 2), jnp.where(core == 0, t == 2, t == 1)
        step = jnp.where(t == 0, 2, jnp.where(one, 1, jnp.where(three, 3, 0)))
        return lax.rem(y + step, CHUNKS)

    def z_copy(block, off):
        to = lax.rem(z + off, PLANES)
        return pltpu.make_async_remote_copy(
            src_ref=y_ref.at[block, to],
            dst_ref=z_ref.at[block, pl.ds(pl.multiple_of(PIECE * z, 8), PIECE)],
            send_sem=z_send.at[block],
            recv_sem=z_recv.at[block],
            device_id=device(to, chip, core),
            device_id_type=MESH,
        )

    def z_mine(block):
        return pltpu.make_async_copy(
            y_ref.at[block, z], z_ref.at[block, pl.ds(pl.multiple_of(PIECE * z, 8), PIECE)], z_recv.at[block]
        )

    def send_block(block):
        def start(step, _):
            near = PLANES // 2 - step
            z_copy(block, near).start()
            z_copy(block, PLANES - near).start()
            return 0

        z_copy(block, PLANES // 2).start()
        lax.fori_loop(1, PLANES // 2, start, 0)
        z_mine(block).start()

    def wait_for(ref, sem):
        pltpu.make_async_copy(ref, ref, sem).wait()

    def sent_block(block):
        wait_for(y_ref.at[block, pl.ds(0, PLANES - 1)], z_send.at[block])

    size = 2 * CHUNK_ROWS

    def one_pulse(r, _):
        compress(r)
        for chunk in range(CHUNKS):
            out = jnp.dot(last[chunk], v_ref[r], preferred_element_type=F32)
            for to in range(PLANES):
                y_ref[r, to, size * chunk : size * (chunk + 1), :] = out[size * to : size * (to + 1)]
        send_block(r)
        return 0

    def two_chunks(pair, _):
        both = jnp.concatenate([v_ref[2], v_ref[3]], axis=1)
        for half in range(2):
            out = jnp.dot(last[chunk_of(2 * pair + half)], both, preferred_element_type=F32)
            for r in range(2):
                place = size * (2 * half + r)
                for to in range(PLANES):
                    y_ref[2 + pair, to, place : place + size, :] = out[
                        size * to : size * (to + 1), LANES * r : LANES * (r + 1)
                    ]
        return 0

    def later_pulse(r, _):
        compress(r)
        return 0

    lax.fori_loop(0, 2, one_pulse, 0)
    lax.fori_loop(2, 4, later_pulse, 0)
    lax.fori_loop(0, 2, two_chunks, 0)

    def turn_filter(step, _):
        rows = pl.ds(pl.multiple_of(8 * step, 8), 8)
        for c in range(2):
            got = swap_blocks([azf_in[c, rows, LANES * k : LANES * (k + 1)] for k in range(16)], 1)
            for k1 in range(16):
                a_ref[c, k1, rows, :] = got[k1]
        return 0

    lax.fori_loop(0, BINS // 8, turn_filter, 0)

    def by_bin(values):
        tall = values.T
        return jnp.concatenate([tall[16 * u : 16 * (u + 1)] for u in range(8)], axis=1)

    shift_ref[...] = by_bin(shift_in[...])
    frac = by_bin(frac_in[...])
    for tap in range(TAPS):
        weight = jnp.zeros(frac.shape, F32)
        for row in range(16):
            weight = jnp.where(frac == row, ktab[tap, row], weight)
        w_ref[tap] = weight

    for r in range(LANE_PULSES):
        for which in range(2):
            x_copy(r, which).wait_send()
            core_swap(r, which).wait_send()

    def next_block(block, _):
        sent_block(block)
        send_block(block + 2)
        return 0

    lax.fori_loop(0, 2, next_block, 0)

    def main_copy(t, q, src, dst, size):
        return pltpu.make_async_remote_copy(
            src_ref=t_ref.at[t, pl.ds(src, size)],
            dst_ref=g_ref.at[chip, pl.ds(dst, size)],
            send_sem=p_send.at[t, q],
            recv_sem=p_recv.at[y],
            device_id=device(z, 4 * chunk_of(t) + q, core),
            device_id_type=MESH,
        )

    def main_own(src, dst, size):
        return pltpu.make_async_copy(
            t_ref.at[CHUNKS - 1, pl.ds(src, size)], g_ref.at[chip, pl.ds(dst, size)], p_recv.at[y]
        )

    def windows(q, act):
        pl.when(q == 0)(lambda: act(0, BELOW, PAIR - BELOW))
        pl.when(q == 3)(lambda: act(CHUNK - BELOW - 2 * BINS, 0, PAIR - ABOVE))
        middle = jnp.logical_and(q > 0, q < 3)
        pl.when(middle)(lambda: act(pl.multiple_of(2 * BINS * q - BELOW, 8), 0, PAIR))

    def halo_targets(chunk):
        down_chip = lax.rem(4 * chunk + CHIPS - 1, CHIPS)
        up_chip = lax.rem(4 * chunk + 4, CHIPS)
        down_plane = jnp.where(chunk == 0, z - 1, z)
        up_plane = jnp.where(chunk == CHUNKS - 1, z + 1, z)
        return down_plane, down_chip, up_plane, up_chip

    DOWN = (0, PAIR - ABOVE, ABOVE)
    UP = (CHUNK - BELOW, 0, BELOW)

    def halo_copy(t, which, plane, to):
        src, dst, size = (DOWN, UP)[which]
        return pltpu.make_async_remote_copy(
            src_ref=t_ref.at[t, pl.ds(src, size)],
            dst_ref=g_ref.at[chip, pl.ds(dst, size)],
            send_sem=h_send.at[t, which],
            recv_sem=h_recv.at[y],
            device_id=device(plane, to, core),
            device_id_type=MESH,
        )

    def halo_mine(t, which):
        src, dst, size = (DOWN, UP)[which]
        return pltpu.make_async_copy(
            t_ref.at[t, pl.ds(src, size)], g_ref.at[chip, pl.ds(dst, size)], h_recv.at[y]
        )

    def each_halo(t, remote, local):
        down_plane, down_chip, up_plane, up_chip = halo_targets(chunk_of(t))
        for which, plane, to in ((0, down_plane, down_chip), (1, up_plane, up_chip)):
            inside = jnp.logical_and(plane >= 0, plane < PLANES)
            me = jnp.logical_and(plane == z, to == chip)
            pl.when(jnp.logical_and(inside, jnp.logical_not(me)))(
                functools.partial(remote, t, which, plane, to)
            )
            pl.when(me)(functools.partial(local, t, which))

    def each_main(t, act):
        for off in range(4):
            q = lax.rem(q_me + off, 4)
            to_me = jnp.logical_and(t == CHUNKS - 1, off == 0)

            def remote(q=q):
                windows(q, functools.partial(act, t, q))

            pl.when(jnp.logical_not(to_me))(remote)

    def wait_block(block, _):
        wait_for(z_ref.at[block], z_recv.at[block])
        return 0

    def sent_chunk(t, _):
        each_main(t, lambda *a: main_copy(*a).wait_send())
        each_halo(t, lambda *a: halo_copy(*a).wait_send(), lambda *a: None)
        return 0

    def plane_step(t, _):
        @pl.when(t == 0)
        def _():
            lax.fori_loop(0, 3, wait_block, 0)

        @pl.when(t == 2)
        def _():
            lax.fori_loop(0, 2, sent_chunk, 0)
            wait_block(3, 0)

        pair = lax.div(t, 2)
        half = lax.rem(t, 2)
        chunk = chunk_of(t)
        for row in range(CHUNK_ROWS):
            parts = []
            for c in range(2):
                for r in range(2):
                    start = size * chunk + CHUNK_ROWS * c + row
                    parts.append(z_ref[r, pl.ds(start, PLANES, stride=PIECE), :])
                for r in range(2):
                    start = size * (2 * half + r) + CHUNK_ROWS * c + row
                    parts.append(z_ref[2 + pair, pl.ds(start, PLANES, stride=PIECE), :])
            t_ref[t, LANES * row : LANES * (row + 1), :] = times_right(
                jnp.concatenate(parts, axis=0).T, planes[...]
            )
        each_main(t, lambda *a: main_copy(*a).start())

        each_halo(t, lambda *a: halo_copy(*a).start(), lambda *a: halo_mine(*a).start())
        return 0

    lax.fori_loop(0, CHUNKS, plane_step, 0)

    windows(q_me, lambda *a: main_own(*a).start())

    def core_copy(row):
        return pltpu.make_async_remote_copy(
            src_ref=g_ref.at[pl.ds(4 * row, 4), pl.ds(pl.multiple_of(BINS * (1 - core), 8), WINDOW)],
            dst_ref=o_ref.at[pl.ds(4 * row, 4)],
            send_sem=fwd_send.at[row],
            recv_sem=fwd_recv.at[row],
            device_id=core_partner,
            device_id_type=MESH,
        )

    takes_up = jnp.logical_and(q_me == 0, jnp.logical_or(y > 0, has_below))
    takes_down = jnp.logical_and(q_me == 3, jnp.logical_or(y < 3, has_above))

    def gather(t, _):
        row = lax.rem(y + CHUNKS - chunk_of(t) + y, CHUNKS)

        def rows_of(start, size):
            return g_ref.at[pl.ds(4 * row, 4), pl.ds(start, size)]

        windows(q_me, lambda src, dst, size: wait_for(rows_of(dst, size), p_recv.at[row]))
        pl.when(takes_up)(lambda: wait_for(rows_of(0, BELOW), h_recv.at[row]))
        pl.when(takes_down)(lambda: wait_for(rows_of(PAIR - ABOVE, ABOVE), h_recv.at[row]))
        core_copy(row).start()
        return 0

    lax.fori_loop(0, CHUNKS, gather, 0)

    part = WINDOW // 2

    def turn_rows(read):
        def body(step, _):
            rows = pl.ds(pl.multiple_of(part * step, 8), part)
            got = swap_blocks([read(k, part * step) for k in range(CHIPS)], 8)
            for k1 in range(16):
                h_ref[k1, rows, :] = got[k1]
            return 0

        lax.fori_loop(0, WINDOW // part, body, 0)

    group = 4

    def transform(from_core, add):
        def body(step, _):
            high, low = split(h_ref[pl.ds(group * step, group)].reshape(group * WINDOW, LANES))
            d = jnp.dot(
                jnp.concatenate([high, low, high], axis=1), az_fwd[from_core], preferred_element_type=F32
            )
            for k in range(group):
                for c in range(2):
                    piece = d[WINDOW * k : WINDOW * (k + 1), LANES * c : LANES * (c + 1)]
                    if add:
                        piece = piece + d_ref[group * step + k, c]
                    d_ref[group * step + k, c] = piece
            return 0

        lax.fori_loop(0, 16 // group, body, 0)

    turn_rows(lambda k, start: g_ref[k, pl.ds(pl.multiple_of(BINS * core + start, 8), part), :])
    transform(core, False)

    def wait_core(row, _):
        core_copy(row).wait_recv()
        return 0

    lax.fori_loop(2, 4, sent_chunk, 0)
    for block in (2, 3):
        sent_block(block)
    lax.fori_loop(0, 4, wait_core, 0)
    turn_rows(lambda k, start: o_ref[k, pl.ds(pl.multiple_of(start, 8), part), :])
    transform(1 - core, True)

    def migrate(k1, slot):
        shift = shift_ref[pl.ds(k1, 1), :]
        weights = [w_ref[tap, pl.ds(k1, 1), :] for tap in range(TAPS)]
        moved = []
        for c in range(2):
            x = d_ref[k1, c]
            near = jnp.where((shift & 16) != 0, x[16:80], x[0:64])
            x = jnp.concatenate([near, x[64:80]], axis=0)
            m, e = m_ref.at[slot, c], e_ref.at[slot, c]
            m[0:72] = jnp.where((shift & 8) != 0, x[8:80], x[0:72])
            e[0:64] = jnp.where((shift & 4) != 0, m[4:68], m[0:64])
            m[0:62] = jnp.where((shift & 2) != 0, e[2:64], e[0:62])
            e[0:61] = jnp.where((shift & 1) != 0, m[1:62], m[0:61])
            total = weights[0] * e[5 : 5 + BINS]
            for tap in range(1, TAPS):
                total = total + weights[tap] * e[5 + tap : 5 + tap + BINS]
            moved.append(total)
        return jnp.concatenate(cmul(moved[0], moved[1], a_ref[0, k1], a_ref[1, k1]), axis=1)

    def result_copy(step):
        some = pl.ds(group * step, group)
        return pltpu.make_async_copy(f_ref.at[:, some], out_hbm.at[:, some], out_sem.at[step])

    def per_group(step, _):
        ks = [group * step + k for k in range(group)]
        s = times_right(jnp.concatenate([migrate(k1, k) for k, k1 in enumerate(ks)], axis=0), az_back[...])
        for k, k1 in enumerate(ks):
            rows = slice(BINS * k, BINS * (k + 1))
            f_ref[0, k1], f_ref[1, k1] = cmul(
                s[rows, :LANES], s[rows, LANES:], az_twist[0, pl.ds(k1, 1), :], az_twist[1, pl.ds(k1, 1), :]
            )
        result_copy(step).start()
        return 0

    lax.fori_loop(0, 16 // group, per_group, 0)

    def sent_core(row, _):
        core_copy(row).wait_send()
        return 0

    lax.fori_loop(0, 4, sent_core, 0)
    for step in range(16 // group):
        result_copy(step).wait()


FINISH_ROWS = 16


def finish_kernel(f_ref, out_ref):
    for half in range(FINISH_ROWS // 8):
        rows = slice(8 * half, 8 * (half + 1))
        got = fft_list([(f_ref[0, k1, rows, :], f_ref[1, k1, rows, :]) for k1 in range(16)], 1)
        for tile in range(16):
            for c in range(2):
                out_ref[c, rows, LANES * tile : LANES * (tile + 1)] = got[tile][c]


ANY = pl.BlockSpec(memory_space=pl.ANY)
DMA = pltpu.SemaphoreType.DMA


def shards(raw, range_filter, azimuth_filter, shifts, frac_index, kernel_table):
    order = filter_order()
    tables = [
        table_first(),
        table_last(),
        table_twist(),
        right_factor(table_columns(np.arange(LANES), order, -1)),
        right_factor(table_columns(order, np.arange(LANES), 1)),
        table_planes(),
        table_azimuth(),
        table_back(),
        table_back_twist(),
    ]
    operands = [
        raw.reshape(2, 2, 8, 48, LANES).transpose(0, 1, 3, 2, 4).reshape(2, 2, 384, LANES),
        range_filter.reshape(2, ROWS, LANES).transpose(1, 0, 2).reshape(2 * ROWS, LANES),
        azimuth_filter,
        shifts.reshape(16, LANES),
        frac_index.reshape(16, LANES),
        kernel_table.T,
    ]

    def like(array, shape=None):
        return pltpu.VMEM(array.shape if shape is None else shape, array.dtype)

    loads = [like(a) for a in operands[1:5]] + [pltpu.SMEM(operands[5].shape, F32)]
    loads += [like(a) for a in tables]
    loads[5 + 5] = like(tables[5], tables[5].shape[1:])
    scratch = [
        pltpu.VMEM((2, 2, 384, LANES), F32),
        pltpu.VMEM((LANE_PULSES, 2, 48, LANES), F32),
        pltpu.VMEM((LANE_PULSES, 2, 48, LANES), F32),
        pltpu.VMEM((LANE_PULSES, 2, 48, LANES), F32),
        pltpu.VMEM((LANE_PULSES, 2, 48, LANES), F32),
        pltpu.VMEM((LANE_PULSES, 2, ROWS, LANES), F32),
        pltpu.VMEM((2, ROWS, LANES), F32),
        pltpu.VMEM((LANE_PULSES, 6 * ROWS, LANES), BF16),
        pltpu.VMEM((CHUNKS, PLANES, PIECE, LANES), F32),
        pltpu.VMEM((CHUNKS, PLANES * PIECE, LANES), F32),
        pltpu.VMEM((CHUNKS, CHUNK, LANES), F32),
        pltpu.VMEM((CHIPS, PAIR, LANES), F32),
        pltpu.VMEM((CHIPS, WINDOW, LANES), F32),
        pltpu.VMEM((16, LANES), jnp.int32),
        pltpu.VMEM((TAPS, 16, LANES), F32),
        pltpu.VMEM((2, 16, BINS, LANES), F32),
        pltpu.VMEM((16, WINDOW, LANES), F32),
        pltpu.VMEM((16, 2, WINDOW, LANES), F32),
        pltpu.VMEM((4, 2, WINDOW, LANES), F32),
        pltpu.VMEM((4, 2, WINDOW, LANES), F32),
        pltpu.VMEM((2, 16, BINS, LANES), F32),
        DMA((2,)), DMA((4, 2)), DMA((4, 2)), DMA((4, 2)), DMA((4, 2)),
        DMA((4,)), DMA((4,)),
        DMA((CHUNKS, 4)), DMA((4,)), DMA((CHUNKS, 2)), DMA((4,)), DMA((4,)), DMA((4,)), DMA((4,)),
    ]
    turned = pl.pallas_call(
        kernel,
        out_shape=jax.ShapeDtypeStruct((2, 16, BINS, LANES), F32),
        in_specs=[ANY] * (len(operands) + len(tables)),
        out_specs=ANY,
        scratch_shapes=loads + [DMA((len(loads),))] + scratch,
        compiler_params=pltpu.CompilerParams(
            vmem_limit_bytes=60 * 2**20, collective_id=0, has_side_effects=True
        ),
    )(*operands, *tables)
    return pl.pallas_call(
        finish_kernel,
        out_shape=jax.ShapeDtypeStruct((2, BINS, PULSES), F32),
        grid=(BINS // FINISH_ROWS,),
        in_specs=[pl.BlockSpec((2, 16, FINISH_ROWS, LANES), lambda i: (0, 0, i, 0))],
        out_specs=pl.BlockSpec((2, FINISH_ROWS, PULSES), lambda i: (0, i, 0)),
    )(turned)


def solution(mesh):
    in_specs = (P(None, "pulse", "rng"), P(), P(None, ("pulse", "rng"), None), P(), P(), P())
    out_specs = P(None, ("pulse", "rng"), None)
    return jax.shard_map(shards, mesh=mesh, in_specs=in_specs, out_specs=out_specs, check_vma=False)
```

```python
import functools
import math

import jax
import jax.numpy as jnp
import ml_dtypes
import numpy as np
from jax import lax
from jax.experimental import pallas as pl
from jax.experimental.pallas import tpu as pltpu
from jax.sharding import PartitionSpec as P

MESH = pl.DeviceIdType.MESH
F32 = jnp.float32
BF16 = jnp.bfloat16

PULSES = 2048
SAMPLES = 24576
ROWS = 192
LANES = 128
PLANES = 16
PEERS = 32
CHIPS = 16
LANE_PULSES = 4
BINS = 48
CHUNKS = 4
CHUNK_ROWS = 3
CHUNK = CHUNK_ROWS * LANES
BLOCKS = (24, 24, 32, 16)
BELOW = 8
ABOVE = 24
WINDOW = BELOW + BINS + ABOVE
PAIR = BELOW + 2 * BINS + ABOVE
TAPS = 8
NEAR = 4
ORDER = ((2, 1, 3, 0), (2, 3, 1, 0))


def turn(product, period, sign):
    angle = sign * 2.0 * math.pi * (product % period) / period
    return np.cos(angle), np.sin(angle)


def halves(table):
    high = table.astype(ml_dtypes.bfloat16)
    low = (table - high.astype(np.float64)).astype(ml_dtypes.bfloat16)
    return high, low


def left_factor(table):
    high, low = halves(table)
    return np.concatenate([high, high, low], axis=1)


def right_factor(table):
    high, low = halves(table)
    return np.concatenate([high, high, low], axis=-2)


def lane_bins():
    lanes = np.arange(LANES)
    return 8 * (lanes % 16) + lanes // 16


def table_first():
    ids = np.arange(ROWS)
    re, im = turn(np.outer(ids, ids), ROWS, -1)
    return left_factor(np.block([[re, -im], [im, re]]))


def table_last():
    ids = np.arange(ROWS)
    re, im = turn(np.outer(ids, ids), ROWS, 1)
    full = np.stack([np.concatenate([re, -im], axis=1), np.concatenate([im, re], axis=1)]) / SAMPLES
    full = full.reshape(2, PLANES, CHUNKS, CHUNK_ROWS, 2 * ROWS).transpose(2, 1, 0, 3, 4)
    return left_factor(full.reshape(2 * ROWS, 2 * ROWS)).reshape(CHUNKS, 2 * ROWS // CHUNKS, -1)


def filter_order():
    lanes = np.arange(LANES)
    return 2 * (lanes % 64) + lanes // 64


def table_columns(rows, cols, sign, scale=1.0):
    re, im = turn(np.outer(rows, cols), LANES, sign)
    return np.block([[re, im], [-im, re]]) * scale


def table_twist():
    re, im = turn(np.outer(np.arange(ROWS), np.arange(LANES)), SAMPLES, -1)
    return np.stack([re, im]).astype(np.float32)


def table_planes():
    place = np.arange(PEERS)[:, None, None, None]
    r = np.arange(LANE_PULSES)[None, :, None, None]
    z = np.arange(PLANES)[None, None, :, None]
    k1 = np.arange(16)[None, None, None, :]
    re, im = turn((128 * z + 4 * place + r) * k1, PULSES, -1)
    full = np.zeros((PEERS, 2, LANE_PULSES, PLANES, 16, 2, LANE_PULSES))
    for q in range(LANE_PULSES):
        full[:, 0, q, :, :, 0, q] = re[:, q]
        full[:, 1, q, :, :, 0, q] = -im[:, q]
        full[:, 0, q, :, :, 1, q] = im[:, q]
        full[:, 1, q, :, :, 1, q] = re[:, q]
    return right_factor(full.reshape(PEERS, 128, 128))


def table_azimuth():
    place = np.arange(PEERS)[:, None, None]
    r = np.arange(LANE_PULSES)[None, :, None]
    re, im = turn((4 * place + r) * lane_bins()[None, None, :], LANES, -1)
    full = np.zeros((PEERS, 2, LANE_PULSES, 2, LANES))
    full[:, 0, :, 0] = re
    full[:, 1, :, 0] = -im
    full[:, 0, :, 1] = im
    full[:, 1, :, 1] = re
    by_core = full.reshape(CHIPS, 2, 8, 2 * LANES).transpose(1, 0, 2, 3)
    return right_factor(by_core.reshape(2, LANES, 2 * LANES))


def table_back():
    return right_factor(table_columns(lane_bins(), np.arange(LANES), 1, 1.0 / PULSES))


def table_back_twist():
    re, im = turn(np.outer(np.arange(16), np.arange(LANES)), PULSES, 1)
    return np.stack([re, im]).astype(np.float32)


def split(values):
    high = values.astype(BF16)
    low = (values - high.astype(F32)).astype(BF16)
    return high, low


def times_left(table, values):
    high, low = split(values)
    return jnp.dot(table, jnp.concatenate([high, low, high], axis=0), preferred_element_type=F32)


def times_right(values, table):
    high, low = split(values)
    return jnp.dot(jnp.concatenate([high, low, high], axis=1), table, preferred_element_type=F32)


def cmul(a_re, a_im, b_re, b_im):
    return a_re * b_re - a_im * b_im, a_re * b_im + a_im * b_re


def fft_list(values, sign):
    count = len(values)
    if count == 1:
        return values
    even = fft_list(values[0::2], sign)
    odd = fft_list(values[1::2], sign)
    low, high = [], []
    for k in range(count // 2):
        re, im = odd[k]
        if 4 * k == count:
            re, im = (-im, re) if sign > 0 else (im, -re)
        elif k:
            w_re = math.cos(2.0 * math.pi * k / count)
            w_im = sign * math.sin(2.0 * math.pi * k / count)
            re, im = re * w_re - im * w_im, re * w_im + im * w_re
        low.append((even[k][0] + re, even[k][1] + im))
        high.append((even[k][0] - re, even[k][1] - im))
    return low + high


def swap_blocks(arrays, width):
    arrays = list(arrays)
    lane = lax.broadcasted_iota(jnp.int32, arrays[0].shape, 1)
    for bit in (1, 2, 4, 8):
        keep = (lane // width) & bit == 0
        for a in range(16):
            if a & bit:
                continue
            first, second = arrays[a], arrays[a + bit]
            arrays[a] = jnp.where(keep, first, pltpu.roll(second, bit * width, 1))
            arrays[a + bit] = jnp.where(keep, pltpu.roll(first, LANES - bit * width, 1), second)
    return arrays


def kernel(
    raw_hbm, filt_hbm, azf_hbm, shift_hbm, frac_hbm, ktab_hbm,
    first_hbm, last_hbm, twist_hbm, fwd_hbm, back_hbm, planes_hbm, az_fwd_hbm, az_back_hbm, az_twist_hbm,
    out_hbm,
    filt_in, azf_in, shift_in, frac_in, ktab, first, last, twist, fwd, back, planes, az_fwd, az_back, az_twist,
    load_sem,
    tiles, to_like, to_cross, to_core, x_ref, filt, v_ref, y0, y1, y2, y3, z0, z1, z2, z3, t_ref, g_ref, o_ref,
    shift_ref, w_ref, a_ref, h_ref, d_ref, m_ref, e_ref, f_ref,
    tile_sem, x_send, x_recv, z_send, z_recv,
    p_send, p_recv, h_send, h_recv, fwd_send, fwd_recv, out_sem,
):
    pulse = lax.axis_index("pulse")
    lane = lax.axis_index("rng")
    z = lax.div(pulse, 8)
    y = lax.rem(lax.div(pulse, 2), 4)
    xh = lax.div(lane, 2)
    core = lax.rem(lane, 2)
    q_me = 2 * lax.rem(pulse, 2) + xh
    chip = 4 * y + q_me
    has_below = z > 0
    has_above = z < PLANES - 1

    def device(plane, other_chip, other_core):
        return (8 * plane + lax.div(other_chip, 2), 2 * lax.rem(other_chip, 2) + other_core)

    x_partner = (pulse, 2 * (1 - xh) + core)
    x_cross = (pulse, 2 * (1 - xh) + 1 - core)
    core_partner = (pulse, 2 * xh + 1 - core)

    place = 2 * chip + core
    loads = [
        (filt_hbm, filt_in), (first_hbm, first), (twist_hbm, twist), (fwd_hbm, fwd), (back_hbm, back),
        (last_hbm, last), (planes_hbm.at[place], planes), (azf_hbm, azf_in), (shift_hbm, shift_in),
        (frac_hbm, frac_in), (ktab_hbm, ktab), (az_fwd_hbm, az_fwd), (az_back_hbm, az_back),
        (az_twist_hbm, az_twist),
    ]
    loads = [pltpu.make_async_copy(src, dst, load_sem.at[k]) for k, (src, dst) in enumerate(loads)]
    tile_loads = [
        pltpu.make_async_copy(raw_hbm.at[:, 1 - xh], tiles.at[1], tile_sem.at[1]),
        pltpu.make_async_copy(raw_hbm.at[:, xh], tiles.at[0], tile_sem.at[0]),
    ]
    for load in tile_loads:
        load.start()

    barrier = pltpu.get_barrier_semaphore()

    def greet(to):
        pl.semaphore_signal(barrier, inc=1, device_id=to, device_id_type=MESH)

    greet(x_partner)
    greet(x_cross)
    greet(core_partner)

    def greet_z(off, _):
        greet(device(lax.rem(z + off, PLANES), chip, core))
        return 0

    def greet_plane(off, _):
        greet(device(z, lax.rem(chip + off, CHIPS), core))
        return 0

    def greet_all(plane):
        def body(other, _):
            greet(device(plane, other, core))
            return 0

        lax.fori_loop(0, CHIPS, body, 0)

    lax.fori_loop(1, PLANES, greet_z, 0)
    lax.fori_loop(1, CHIPS, greet_plane, 0)
    pl.when(jnp.logical_and(chip == 0, has_below))(lambda: greet_all(z - 1))
    pl.when(jnp.logical_and(chip == CHIPS - 1, has_above))(lambda: greet_all(z + 1))

    for load in loads:
        load.start()

    def blank(start, size):
        def body(other, _):
            g_ref[other, start : start + size, :] = jnp.zeros((size, LANES), F32)
            return 0

        lax.fori_loop(0, CHIPS, body, 0)

    pl.when(jnp.logical_and(chip == 0, z == 0))(lambda: blank(0, BELOW))
    pl.when(jnp.logical_and(chip == CHIPS - 1, z == PLANES - 1))(lambda: blank(PAIR - ABOVE, ABOVE))

    my_quarter = 2 * xh + core

    def quarter_rows(quarter):
        return pl.ds(pl.multiple_of(48 * quarter, 8), 48)

    for load in tile_loads:
        load.wait()
    def sort_pulse(r):
        like = pl.ds(4 * core + r, 48, stride=8)
        other = pl.ds(4 * (1 - core) + r, 48, stride=8)
        for c in range(2):
            to_like[r, c] = tiles[1, c, like, :]
            to_cross[r, c] = tiles[1, c, other, :]
            to_core[r, c] = tiles[0, c, other, :]
            x_ref[r, c, quarter_rows(my_quarter), :] = tiles[0, c, like, :]

    sort_pulse(0)
    pl.semaphore_wait(
        barrier,
        3 + PLANES - 1 + CHIPS - 1 + jnp.where(has_below, 1, 0) + jnp.where(has_above, 1, 0),
    )

    def pulse_copy(r, which):
        return pltpu.make_async_remote_copy(
            src_ref=(to_like, to_cross, to_core)[which].at[r],
            dst_ref=x_ref.at[r, :, quarter_rows(my_quarter)],
            send_sem=x_send.at[r, which],
            recv_sem=x_recv.at[r, which],
            device_id=(x_partner, x_cross, core_partner)[which],
            device_id_type=MESH,
        )

    def send_pulse(r):
        for which in range(3):
            pulse_copy(r, which).start()

    send_pulse(0)
    for r in range(1, LANE_PULSES):
        sort_pulse(r)

    for load in loads:
        load.wait()
    for c in range(2):
        cols = [filt_in[pl.ds(2 * u + c, 64, stride=6), :].T for u in range(3)]
        tall = jnp.concatenate(cols, axis=0)
        filt[c] = jnp.concatenate([tall[:ROWS], tall[ROWS:]], axis=1)

    def compress(r):
        for which in range(3):
            pulse_copy(r, which).wait_recv()
        pl.when(r < LANE_PULSES - 1)(lambda: send_pulse(r + 1))
        twist_re, twist_im = twist[0], twist[1]
        v = times_left(first[...], jnp.concatenate([x_ref[r, 0], x_ref[r, 1]], axis=0))
        re, im = cmul(v[:ROWS], v[ROWS:], twist_re, twist_im)
        s = times_right(jnp.concatenate([re, im], axis=1), fwd[...])
        re, im = cmul(s[:, :LANES], s[:, LANES:], filt[0], filt[1])
        s = times_right(jnp.concatenate([re, im], axis=1), back[...])
        re, im = cmul(s[:, :LANES], s[:, LANES:], twist_re, -twist_im)
        high, low = split(jnp.concatenate([re, im], axis=0))
        v_ref[r, 0 : 2 * ROWS] = high
        v_ref[r, 2 * ROWS : 4 * ROWS] = low
        v_ref[r, 4 * ROWS : 6 * ROWS] = high

    ys, zs = (y0, y1, y2, y3), (z0, z1, z2, z3)

    def chunk_of(t):
        if t in (0, 3):
            return lax.rem(y + (2 if t == 0 else 0), CHUNKS)
        return lax.rem(y + jnp.where(core == t - 1, 1, 3), CHUNKS)

    def z_mine_rows(block):
        return pl.ds(pl.multiple_of(BLOCKS[block] * z, 8), BLOCKS[block])

    def z_copy(block, off):
        to = lax.rem(z + off, PLANES)
        return pltpu.make_async_remote_copy(
            src_ref=ys[block].at[to],
            dst_ref=zs[block].at[z_mine_rows(block)],
            send_sem=z_send.at[block],
            recv_sem=z_recv.at[block],
            device_id=device(to, chip, core),
            device_id_type=MESH,
        )

    def z_mine(block):
        return pltpu.make_async_copy(ys[block].at[z], zs[block].at[z_mine_rows(block)], z_recv.at[block])

    def send_to(block, first, last):
        def start(step, _):
            near = last - step
            z_copy(block, near).start()
            z_copy(block, PLANES - near).start()
            return 0

        lax.fori_loop(0, last - first + 1, start, 0)

    def send_far(block):
        z_copy(block, PLANES // 2).start()
        send_to(block, NEAR + 1, PLANES // 2 - 1)
        z_mine(block).start()

    def send_near(block):
        send_to(block, 1, NEAR)

    def send_block(block):
        send_far(block)
        send_near(block)

    def wait_for(ref, sem):
        pltpu.make_async_copy(ref, ref, sem).wait()

    def sent_block(block):
        wait_for(ys[block].at[pl.ds(0, PLANES - 1)], z_send.at[block])

    size = 2 * CHUNK_ROWS

    def place_of(t, r, c, row):
        if t == 3:
            return 3, 6 * (r - 2) + 3 * c + row
        if t < 2:
            return 2, 12 * t + 6 * (r - 2) + 3 * c + row
        if row < 2:
            return 2, 24 + 4 * (r - 2) + 2 * c + row
        return 3, 12 + 2 * (r - 2) + c

    for r in range(2):
        compress(r)
        for chunk in range(CHUNKS):
            out = jnp.dot(last[chunk], v_ref[r], preferred_element_type=F32)
            for to in range(PLANES):
                ys[r][to, size * chunk : size * (chunk + 1), :] = out[size * to : size * (to + 1)]
        send_block(r)

    def later_pulse(r, _):
        compress(r)
        return 0

    lax.fori_loop(2, 4, later_pulse, 0)
    both = jnp.concatenate([v_ref[2], v_ref[3]], axis=1)
    for t in range(CHUNKS):
        out = jnp.dot(last[chunk_of(t)], both, preferred_element_type=F32)
        for r in (2, 3):
            lanes = slice(LANES * (r - 2), LANES * (r - 1))
            pieces = [(0, 6)] if t != 2 else [(0, 2), (2, 3), (3, 5), (5, 6)]
            for first_row, end in pieces:
                block, place = place_of(t, r, first_row // 3, first_row % 3)
                for to in range(PLANES):
                    ys[block][to, place : place + end - first_row, :] = out[
                        size * to + first_row : size * to + end, lanes
                    ]

    def turn_filter(step, _):
        rows = pl.ds(pl.multiple_of(8 * step, 8), 8)
        for c in range(2):
            got = swap_blocks([azf_in[c, rows, LANES * k : LANES * (k + 1)] for k in range(16)], 1)
            for k1 in range(16):
                a_ref[c, k1, rows, :] = got[k1]
        return 0

    lax.fori_loop(0, BINS // 8, turn_filter, 0)

    def by_bin(values):
        tall = values.T
        return jnp.concatenate([tall[16 * u : 16 * (u + 1)] for u in range(8)], axis=1)

    shift_ref[...] = by_bin(shift_in[...])
    frac = by_bin(frac_in[...])
    for tap in range(TAPS):
        weight = jnp.zeros(frac.shape, F32)
        for row in range(16):
            weight = jnp.where(frac == row, ktab[tap, row], weight)
        w_ref[tap] = weight

    for r in range(LANE_PULSES):
        for which in range(3):
            pulse_copy(r, which).wait_send()

    sent_block(0)
    send_block(2)
    sent_block(1)
    send_far(3)
    sent_block(2)
    send_near(3)

    def window(q):
        if q == 0:
            return 0, BELOW, PAIR - BELOW
        if q == 3:
            return CHUNK - BELOW - 2 * BINS, 0, PAIR - ABOVE
        return 2 * BINS * q - BELOW, 0, PAIR

    def main_copy(t, q):
        src, dst, size = window(q)
        return pltpu.make_async_remote_copy(
            src_ref=t_ref.at[t, pl.ds(src, size)],
            dst_ref=g_ref.at[chip, pl.ds(dst, size)],
            send_sem=p_send.at[t, q],
            recv_sem=p_recv.at[y],
            device_id=device(z, 4 * chunk_of(t) + q, core),
            device_id_type=MESH,
        )

    def main_own(q):
        src, dst, size = window(q)
        return pltpu.make_async_copy(
            t_ref.at[CHUNKS - 1, pl.ds(src, size)], g_ref.at[chip, pl.ds(dst, size)], p_recv.at[y]
        )

    def each_main(t, qs, act, local):
        for q in qs:
            if t < CHUNKS - 1:
                act(main_copy(t, q))
            else:
                pl.when(q_me != q)(functools.partial(lambda q: act(main_copy(t, q)), q))
                if local:
                    pl.when(q_me == q)(functools.partial(lambda q: local(main_own(q)), q))

    def on_window(act):
        for q in range(4):
            pl.when(q_me == q)(functools.partial(lambda q: act(*window(q)), q))

    def halo_targets(chunk):
        down_chip = lax.rem(4 * chunk + CHIPS - 1, CHIPS)
        up_chip = lax.rem(4 * chunk + 4, CHIPS)
        down_plane = jnp.where(chunk == 0, z - 1, z)
        up_plane = jnp.where(chunk == CHUNKS - 1, z + 1, z)
        return down_plane, down_chip, up_plane, up_chip

    DOWN = (0, PAIR - ABOVE, ABOVE)
    UP = (CHUNK - BELOW, 0, BELOW)

    def halo_copy(t, which, plane, to):
        src, dst, size = (DOWN, UP)[which]
        return pltpu.make_async_remote_copy(
            src_ref=t_ref.at[t, pl.ds(src, size)],
            dst_ref=g_ref.at[chip, pl.ds(dst, size)],
            send_sem=h_send.at[t, which],
            recv_sem=h_recv.at[y],
            device_id=device(plane, to, core),
            device_id_type=MESH,
        )

    def halo_mine(t, which):
        src, dst, size = (DOWN, UP)[which]
        return pltpu.make_async_copy(
            t_ref.at[t, pl.ds(src, size)], g_ref.at[chip, pl.ds(dst, size)], h_recv.at[y]
        )

    def each_halo(t, whichs, act, local):
        down_plane, down_chip, up_plane, up_chip = halo_targets(chunk_of(t))
        for which, plane, to in ((0, down_plane, down_chip), (1, up_plane, up_chip)):
            if which not in whichs:
                continue
            inside = jnp.logical_and(plane >= 0, plane < PLANES)
            me = jnp.logical_and(plane == z, to == chip)
            pl.when(jnp.logical_and(inside, jnp.logical_not(me)))(
                functools.partial(lambda *a: act(halo_copy(*a)), t, which, plane, to)
            )
            if local:
                pl.when(me)(functools.partial(lambda *a: local(halo_mine(*a)), t, which))

    def wait_block(block):
        wait_for(zs[block], z_recv.at[block])

    def start(copy):
        copy.start()

    def sent_chunk(t):
        each_main(t, range(4), lambda copy: copy.wait_send(), None)
        each_halo(t, (0, 1), lambda copy: copy.wait_send(), None)

    def turn_chunk(t, rows):
        chunk = chunk_of(t)
        for row in rows:
            parts = []
            for c in range(2):
                for r in range(2):
                    place = size * chunk + CHUNK_ROWS * c + row
                    parts.append(zs[r][pl.ds(place, PLANES, stride=BLOCKS[r]), :])
                for r in (2, 3):
                    block, place = place_of(t, r, c, row)
                    parts.append(zs[block][pl.ds(place, PLANES, stride=BLOCKS[block]), :])
            t_ref[t, LANES * row : LANES * (row + 1), :] = times_right(
                jnp.concatenate(parts, axis=0).T, planes[...]
            )

    for block in range(3):
        wait_block(block)
    for t in range(2):
        turn_chunk(t, range(CHUNK_ROWS))
        each_main(t, range(4), start, start)
        each_halo(t, (0, 1), start, start)
    turn_chunk(2, range(2))
    each_main(2, (0, 1), start, start)
    each_halo(2, (0,), start, start)
    for t in range(2):
        sent_chunk(t)
    wait_block(3)
    turn_chunk(2, (2,))
    each_main(2, (2, 3), start, start)
    each_halo(2, (1,), start, start)
    turn_chunk(3, range(CHUNK_ROWS))
    each_main(3, range(4), start, start)
    each_halo(3, (0, 1), start, start)

    def core_copy(row):
        return pltpu.make_async_remote_copy(
            src_ref=g_ref.at[pl.ds(4 * row, 4), pl.ds(pl.multiple_of(BINS * (1 - core), 8), WINDOW)],
            dst_ref=o_ref.at[pl.ds(4 * row, 4)],
            send_sem=fwd_send.at[row],
            recv_sem=fwd_recv.at[row],
            device_id=core_partner,
            device_id_type=MESH,
        )

    takes_up = jnp.logical_and(q_me == 0, jnp.logical_or(y > 0, has_below))
    takes_down = jnp.logical_and(q_me == 3, jnp.logical_or(y < 3, has_above))

    def gather(t):
        row = lax.rem(2 * y + CHUNKS - chunk_of(t), CHUNKS)

        def rows_of(first_row, count):
            return g_ref.at[pl.ds(4 * row, 4), pl.ds(first_row, count)]

        on_window(lambda src, dst, count: wait_for(rows_of(dst, count), p_recv.at[row]))
        pl.when(takes_up)(lambda: wait_for(rows_of(0, BELOW), h_recv.at[row]))
        pl.when(takes_down)(lambda: wait_for(rows_of(PAIR - ABOVE, ABOVE), h_recv.at[row]))
        core_copy(row).start()

    for t in range(CHUNKS):
        gather(t)

    part = WINDOW // 2

    def turn_rows(read):
        def body(step, _):
            rows = pl.ds(pl.multiple_of(part * step, 8), part)
            got = swap_blocks([read(k, part * step) for k in range(CHIPS)], 8)
            for k1 in range(16):
                h_ref[k1, rows, :] = got[k1]
            return 0

        lax.fori_loop(0, WINDOW // part, body, 0)

    group = 4

    def transform(from_core, add):
        def body(step, _):
            high, low = split(h_ref[pl.ds(group * step, group)].reshape(group * WINDOW, LANES))
            d = jnp.dot(
                jnp.concatenate([high, low, high], axis=1), az_fwd[from_core], preferred_element_type=F32
            )
            for k in range(group):
                for c in range(2):
                    piece = d[WINDOW * k : WINDOW * (k + 1), LANES * c : LANES * (c + 1)]
                    if add:
                        piece = piece + d_ref[group * step + k, c]
                    d_ref[group * step + k, c] = piece
            return 0

        lax.fori_loop(0, 16 // group, body, 0)

    turn_rows(lambda k, start: g_ref[k, pl.ds(pl.multiple_of(BINS * core + start, 8), part), :])
    transform(core, False)

    def wait_core(row, _):
        core_copy(row).wait_recv()
        return 0

    for t in (2, 3):
        sent_chunk(t)
    sent_block(3)
    lax.fori_loop(0, 4, wait_core, 0)
    turn_rows(lambda k, start: o_ref[k, pl.ds(pl.multiple_of(start, 8), part), :])
    transform(1 - core, True)

    def migrate(k1, slot):
        shift = shift_ref[pl.ds(k1, 1), :]
        weights = [w_ref[tap, pl.ds(k1, 1), :] for tap in range(TAPS)]
        moved = []
        for c in range(2):
            x = d_ref[k1, c]
            near = jnp.where((shift & 16) != 0, x[16:80], x[0:64])
            x = jnp.concatenate([near, x[64:80]], axis=0)
            m, e = m_ref.at[slot, c], e_ref.at[slot, c]
            m[0:72] = jnp.where((shift & 8) != 0, x[8:80], x[0:72])
            e[0:64] = jnp.where((shift & 4) != 0, m[4:68], m[0:64])
            m[0:62] = jnp.where((shift & 2) != 0, e[2:64], e[0:62])
            e[0:61] = jnp.where((shift & 1) != 0, m[1:62], m[0:61])
            total = weights[0] * e[5 : 5 + BINS]
            for tap in range(1, TAPS):
                total = total + weights[tap] * e[5 + tap : 5 + tap + BINS]
            moved.append(total)
        return jnp.concatenate(cmul(moved[0], moved[1], a_ref[0, k1], a_ref[1, k1]), axis=1)

    def result_copy(step):
        some = pl.ds(group * step, group)
        return pltpu.make_async_copy(f_ref.at[:, some], out_hbm.at[:, some], out_sem.at[step])

    def per_group(step, _):
        ks = [group * step + k for k in range(group)]
        s = times_right(jnp.concatenate([migrate(k1, k) for k, k1 in enumerate(ks)], axis=0), az_back[...])
        for k, k1 in enumerate(ks):
            rows = slice(BINS * k, BINS * (k + 1))
            f_ref[0, k1], f_ref[1, k1] = cmul(
                s[rows, :LANES], s[rows, LANES:], az_twist[0, pl.ds(k1, 1), :], az_twist[1, pl.ds(k1, 1), :]
            )
        result_copy(step).start()
        return 0

    lax.fori_loop(0, 16 // group, per_group, 0)

    def sent_core(row, _):
        core_copy(row).wait_send()
        return 0

    lax.fori_loop(0, 4, sent_core, 0)
    for step in range(16 // group):
        result_copy(step).wait()


def finish_kernel(f_hbm, out_hbm, f_ref, out_ref, in_sem, out_sem):
    def fetch(step):
        rows = slice(8 * step, 8 * (step + 1))
        return pltpu.make_async_copy(f_hbm.at[:, :, rows], f_ref.at[:, :, rows], in_sem.at[step])

    def store(step):
        rows = slice(8 * step, 8 * (step + 1))
        return pltpu.make_async_copy(out_ref.at[:, rows], out_hbm.at[:, rows], out_sem.at[step])

    for step in range(BINS // 8):
        fetch(step).start()
    for step in range(BINS // 8):
        rows = slice(8 * step, 8 * (step + 1))
        fetch(step).wait()
        got = fft_list([(f_ref[0, k1, rows, :], f_ref[1, k1, rows, :]) for k1 in range(16)], 1)
        for tile in range(16):
            for c in range(2):
                out_ref[c, rows, LANES * tile : LANES * (tile + 1)] = got[tile][c]
        store(step).start()
    for step in range(BINS // 8):
        store(step).wait()


IN_HBM = pl.BlockSpec(memory_space=pltpu.HBM)
DMA = pltpu.SemaphoreType.DMA


def shards(raw, range_filter, azimuth_filter, shifts, frac_index, kernel_table):
    order = filter_order()
    tables = [
        table_first(),
        table_last(),
        table_twist(),
        right_factor(table_columns(np.arange(LANES), order, -1)),
        right_factor(table_columns(order, np.arange(LANES), 1)),
        table_planes(),
        table_azimuth(),
        table_back(),
        table_back_twist(),
    ]
    operands = [
        raw.reshape(2, 2, 8, 48, LANES).transpose(0, 1, 3, 2, 4).reshape(2, 2, 384, LANES),
        range_filter.reshape(2, ROWS, LANES).transpose(1, 0, 2).reshape(2 * ROWS, LANES),
        azimuth_filter,
        shifts.reshape(16, LANES),
        frac_index.reshape(16, LANES),
        kernel_table.T,
    ]

    def like(array, shape=None):
        return pltpu.VMEM(array.shape if shape is None else shape, array.dtype)

    loads = [like(a) for a in operands[1:5]] + [pltpu.SMEM(operands[5].shape, F32)]
    loads += [like(a) for a in tables]
    loads[5 + 5] = like(tables[5], tables[5].shape[1:])
    scratch = [
        pltpu.VMEM((2, 2, 384, LANES), F32),
        pltpu.VMEM((LANE_PULSES, 2, 48, LANES), F32),
        pltpu.VMEM((LANE_PULSES, 2, 48, LANES), F32),
        pltpu.VMEM((LANE_PULSES, 2, 48, LANES), F32),
        pltpu.VMEM((LANE_PULSES, 2, ROWS, LANES), F32),
        pltpu.VMEM((2, ROWS, LANES), F32),
        pltpu.VMEM((LANE_PULSES, 6 * ROWS, LANES), BF16),
        *[pltpu.VMEM((PLANES, rows, LANES), F32) for rows in BLOCKS],
        *[pltpu.VMEM((PLANES * rows, LANES), F32) for rows in BLOCKS],
        pltpu.VMEM((CHUNKS, CHUNK, LANES), F32),
        pltpu.VMEM((CHIPS, PAIR, LANES), F32),
        pltpu.VMEM((CHIPS, WINDOW, LANES), F32),
        pltpu.VMEM((16, LANES), jnp.int32),
        pltpu.VMEM((TAPS, 16, LANES), F32),
        pltpu.VMEM((2, 16, BINS, LANES), F32),
        pltpu.VMEM((16, WINDOW, LANES), F32),
        pltpu.VMEM((16, 2, WINDOW, LANES), F32),
        pltpu.VMEM((4, 2, WINDOW, LANES), F32),
        pltpu.VMEM((4, 2, WINDOW, LANES), F32),
        pltpu.VMEM((2, 16, BINS, LANES), F32),
        DMA((2,)), DMA((4, 3)), DMA((4, 3)),
        DMA((4,)), DMA((4,)),
        DMA((CHUNKS, 4)), DMA((4,)), DMA((CHUNKS, 2)), DMA((4,)), DMA((4,)), DMA((4,)), DMA((4,)),
    ]
    turned = pl.pallas_call(
        kernel,
        out_shape=jax.ShapeDtypeStruct((2, 16, BINS, LANES), F32),
        in_specs=[IN_HBM] * (len(operands) + len(tables)),
        out_specs=IN_HBM,
        scratch_shapes=loads + [DMA((len(loads),))] + scratch,
        compiler_params=pltpu.CompilerParams(
            vmem_limit_bytes=60 * 2**20, collective_id=0, has_side_effects=True
        ),
    )(*operands, *tables)
    return pl.pallas_call(
        finish_kernel,
        out_shape=jax.ShapeDtypeStruct((2, BINS, PULSES), F32),
        in_specs=[IN_HBM],
        out_specs=IN_HBM,
        scratch_shapes=[
            pltpu.VMEM((2, 16, BINS, LANES), F32),
            pltpu.VMEM((2, BINS, PULSES), F32),
            DMA((BINS // 8,)),
            DMA((BINS // 8,)),
        ],
        compiler_params=pltpu.CompilerParams(vmem_limit_bytes=60 * 2**20),
    )(turned)


def solution(mesh):
    in_specs = (P(None, "pulse", "rng"), P(), P(None, ("pulse", "rng"), None), P(), P(), P())
    out_specs = P(None, ("pulse", "rng"), None)
    return jax.shard_map(shards, mesh=mesh, in_specs=in_specs, out_specs=out_specs, check_vma=False)
```

```python
import functools
import math

import jax
import jax.numpy as jnp
import ml_dtypes
import numpy as np
from jax import lax
from jax.experimental import pallas as pl
from jax.experimental.pallas import tpu as pltpu
from jax.sharding import PartitionSpec as P

MESH = pl.DeviceIdType.MESH
F32 = jnp.float32
BF16 = jnp.bfloat16

PULSES = 2048
SAMPLES = 24576
ROWS = 192
LANES = 128
PLANES = 16
PEERS = 32
CHIPS = 16
LANE_PULSES = 4
BINS = 48
CHUNKS = 4
CHUNK_ROWS = 3
CHUNK = CHUNK_ROWS * LANES
PIECE = 2 * CHUNK_ROWS * LANE_PULSES
BELOW = 8
ABOVE = 24
WINDOW = BELOW + BINS + ABOVE
PAIR = BELOW + 2 * BINS + ABOVE
TAPS = 8
NEAR = 4
ORDER = ((2, 1, 3, 0), (2, 3, 1, 0))


def turn(product, period, sign):
    angle = sign * 2.0 * math.pi * (product % period) / period
    return np.cos(angle), np.sin(angle)


def halves(table):
    high = table.astype(ml_dtypes.bfloat16)
    low = (table - high.astype(np.float64)).astype(ml_dtypes.bfloat16)
    return high, low


def left_factor(table):
    high, low = halves(table)
    return np.concatenate([high, high, low], axis=1)


def right_factor(table):
    high, low = halves(table)
    return np.concatenate([high, high, low], axis=-2)


def lane_bins():
    lanes = np.arange(LANES)
    return 8 * (lanes % 16) + lanes // 16


def table_first():
    ids = np.arange(ROWS)
    re, im = turn(np.outer(ids, ids), ROWS, -1)
    return left_factor(np.block([[re, -im], [im, re]]))


def table_last():
    ids = np.arange(ROWS)
    re, im = turn(np.outer(ids, ids), ROWS, 1)
    full = np.stack([np.concatenate([re, -im], axis=1), np.concatenate([im, re], axis=1)]) / SAMPLES
    full = full.reshape(2, PLANES, CHUNKS, CHUNK_ROWS, 2 * ROWS).transpose(2, 1, 0, 3, 4)
    return left_factor(full.reshape(2 * ROWS, 2 * ROWS)).reshape(CHUNKS, 2 * ROWS // CHUNKS, -1)


def filter_order():
    lanes = np.arange(LANES)
    return 2 * (lanes % 64) + lanes // 64


def table_columns(rows, cols, sign, scale=1.0):
    re, im = turn(np.outer(rows, cols), LANES, sign)
    return np.block([[re, im], [-im, re]]) * scale


def table_twist():
    re, im = turn(np.outer(np.arange(ROWS), np.arange(LANES)), SAMPLES, -1)
    return np.stack([re, im]).astype(np.float32)


def table_planes():
    place = np.arange(PEERS)[:, None, None, None]
    r = np.arange(LANE_PULSES)[None, :, None, None]
    z = np.arange(PLANES)[None, None, :, None]
    k1 = np.arange(16)[None, None, None, :]
    re, im = turn((128 * z + 4 * place + r) * k1, PULSES, -1)
    full = np.zeros((PEERS, 2, LANE_PULSES, PLANES, 16, 2, LANE_PULSES))
    for q in range(LANE_PULSES):
        full[:, 0, q, :, :, 0, q] = re[:, q]
        full[:, 1, q, :, :, 0, q] = -im[:, q]
        full[:, 0, q, :, :, 1, q] = im[:, q]
        full[:, 1, q, :, :, 1, q] = re[:, q]
    return right_factor(full.reshape(PEERS, 128, 128))


def table_azimuth():
    place = np.arange(PEERS)[:, None, None]
    r = np.arange(LANE_PULSES)[None, :, None]
    re, im = turn((4 * place + r) * lane_bins()[None, None, :], LANES, -1)
    full = np.zeros((PEERS, 2, LANE_PULSES, 2, LANES))
    full[:, 0, :, 0] = re
    full[:, 1, :, 0] = -im
    full[:, 0, :, 1] = im
    full[:, 1, :, 1] = re
    by_core = full.reshape(CHIPS, 2, 8, 2 * LANES).transpose(1, 0, 2, 3)
    return right_factor(by_core.reshape(2, LANES, 2 * LANES))


def table_back():
    return right_factor(table_columns(lane_bins(), np.arange(LANES), 1, 1.0 / PULSES))


def table_back_twist():
    re, im = turn(np.outer(np.arange(16), np.arange(LANES)), PULSES, 1)
    return np.stack([re, im]).astype(np.float32)


def split(values):
    high = values.astype(BF16)
    low = (values - high.astype(F32)).astype(BF16)
    return high, low


def times_left(table, values):
    high, low = split(values)
    return jnp.dot(table, jnp.concatenate([high, low, high], axis=0), preferred_element_type=F32)


def times_right(values, table):
    high, low = split(values)
    return jnp.dot(jnp.concatenate([high, low, high], axis=1), table, preferred_element_type=F32)


def cmul(a_re, a_im, b_re, b_im):
    return a_re * b_re - a_im * b_im, a_re * b_im + a_im * b_re


def fft_list(values, sign):
    count = len(values)
    if count == 1:
        return values
    even = fft_list(values[0::2], sign)
    odd = fft_list(values[1::2], sign)
    low, high = [], []
    for k in range(count // 2):
        re, im = odd[k]
        if 4 * k == count:
            re, im = (-im, re) if sign > 0 else (im, -re)
        elif k:
            w_re = math.cos(2.0 * math.pi * k / count)
            w_im = sign * math.sin(2.0 * math.pi * k / count)
            re, im = re * w_re - im * w_im, re * w_im + im * w_re
        low.append((even[k][0] + re, even[k][1] + im))
        high.append((even[k][0] - re, even[k][1] - im))
    return low + high


def swap_blocks(arrays, width):
    arrays = list(arrays)
    lane = lax.broadcasted_iota(jnp.int32, arrays[0].shape, 1)
    for bit in (1, 2, 4, 8):
        keep = (lane // width) & bit == 0
        for a in range(16):
            if a & bit:
                continue
            first, second = arrays[a], arrays[a + bit]
            arrays[a] = jnp.where(keep, first, pltpu.roll(second, bit * width, 1))
            arrays[a + bit] = jnp.where(keep, pltpu.roll(first, LANES - bit * width, 1), second)
    return arrays


def kernel(
    raw_hbm, filt_hbm, azf_hbm, shift_hbm, frac_hbm, ktab_hbm,
    first_hbm, last_hbm, twist_hbm, fwd_hbm, back_hbm, planes_hbm, az_fwd_hbm, az_back_hbm, az_twist_hbm,
    out_hbm,
    filt_in, azf_in, shift_in, frac_in, ktab, first, last, twist, fwd, back, planes, az_fwd, az_back, az_twist,
    load_sem,
    tiles, to_like, to_cross, to_core, x_ref, filt, v_ref, y_ref, z_ref, t_ref, g_ref, o_ref,
    shift_ref, w_ref, a_ref, h_ref, d_ref, m_ref, e_ref, f_ref,
    tile_sem, x_send, x_recv, z_send, z_recv,
    p_send, p_recv, h_send, h_recv, fwd_send, fwd_recv, out_sem,
):
    pulse = lax.axis_index("pulse")
    lane = lax.axis_index("rng")
    z = lax.div(pulse, 8)
    y = lax.rem(lax.div(pulse, 2), 4)
    xh = lax.div(lane, 2)
    core = lax.rem(lane, 2)
    q_me = 2 * lax.rem(pulse, 2) + xh
    chip = 4 * y + q_me
    has_below = z > 0
    has_above = z < PLANES - 1

    def device(plane, other_chip, other_core):
        return (8 * plane + lax.div(other_chip, 2), 2 * lax.rem(other_chip, 2) + other_core)

    x_partner = (pulse, 2 * (1 - xh) + core)
    x_cross = (pulse, 2 * (1 - xh) + 1 - core)
    core_partner = (pulse, 2 * xh + 1 - core)

    place = 2 * chip + core
    loads = [
        (filt_hbm, filt_in), (first_hbm, first), (twist_hbm, twist), (fwd_hbm, fwd), (back_hbm, back),
        (last_hbm, last), (planes_hbm.at[place], planes), (azf_hbm, azf_in), (shift_hbm, shift_in),
        (frac_hbm, frac_in), (ktab_hbm, ktab), (az_fwd_hbm, az_fwd), (az_back_hbm, az_back),
        (az_twist_hbm, az_twist),
    ]
    loads = [pltpu.make_async_copy(src, dst, load_sem.at[k]) for k, (src, dst) in enumerate(loads)]
    tile_loads = [
        pltpu.make_async_copy(raw_hbm.at[:, 1 - xh], tiles.at[1], tile_sem.at[1]),
        pltpu.make_async_copy(raw_hbm.at[:, xh], tiles.at[0], tile_sem.at[0]),
    ]
    for load in tile_loads:
        load.start()

    barrier = pltpu.get_barrier_semaphore()

    def greet(to):
        pl.semaphore_signal(barrier, inc=1, device_id=to, device_id_type=MESH)

    greet(x_partner)
    greet(x_cross)
    greet(core_partner)

    def greet_z(off, _):
        greet(device(lax.rem(z + off, PLANES), chip, core))
        return 0

    def greet_plane(off, _):
        greet(device(z, lax.rem(chip + off, CHIPS), core))
        return 0

    def greet_all(plane):
        def body(other, _):
            greet(device(plane, other, core))
            return 0

        lax.fori_loop(0, CHIPS, body, 0)

    lax.fori_loop(1, PLANES, greet_z, 0)
    lax.fori_loop(1, CHIPS, greet_plane, 0)
    pl.when(jnp.logical_and(chip == 0, has_below))(lambda: greet_all(z - 1))
    pl.when(jnp.logical_and(chip == CHIPS - 1, has_above))(lambda: greet_all(z + 1))

    for load in loads:
        load.start()

    def blank(start, size):
        def body(other, _):
            g_ref[other, start : start + size, :] = jnp.zeros((size, LANES), F32)
            return 0

        lax.fori_loop(0, CHIPS, body, 0)

    pl.when(jnp.logical_and(chip == 0, z == 0))(lambda: blank(0, BELOW))
    pl.when(jnp.logical_and(chip == CHIPS - 1, z == PLANES - 1))(lambda: blank(PAIR - ABOVE, ABOVE))

    my_quarter = 2 * xh + core

    def quarter_rows(quarter):
        return pl.ds(pl.multiple_of(48 * quarter, 8), 48)

    for load in tile_loads:
        load.wait()
    def sort_pulse(r):
        like = pl.ds(4 * core + r, 48, stride=8)
        other = pl.ds(4 * (1 - core) + r, 48, stride=8)
        for c in range(2):
            to_like[r, c] = tiles[1, c, like, :]
            to_cross[r, c] = tiles[1, c, other, :]
            to_core[r, c] = tiles[0, c, other, :]
            x_ref[r, c, quarter_rows(my_quarter), :] = tiles[0, c, like, :]

    sort_pulse(0)
    pl.semaphore_wait(
        barrier,
        3 + PLANES - 1 + CHIPS - 1 + jnp.where(has_below, 1, 0) + jnp.where(has_above, 1, 0),
    )

    def pulse_copy(r, which):
        return pltpu.make_async_remote_copy(
            src_ref=(to_like, to_cross, to_core)[which].at[r],
            dst_ref=x_ref.at[r, :, quarter_rows(my_quarter)],
            send_sem=x_send.at[r, which],
            recv_sem=x_recv.at[r, which],
            device_id=(x_partner, x_cross, core_partner)[which],
            device_id_type=MESH,
        )

    def send_pulse(r):
        for which in range(3):
            pulse_copy(r, which).start()

    send_pulse(0)
    for r in range(1, LANE_PULSES):
        sort_pulse(r)

    for load in loads:
        load.wait()
    for c in range(2):
        cols = [filt_in[pl.ds(2 * u + c, 64, stride=6), :].T for u in range(3)]
        tall = jnp.concatenate(cols, axis=0)
        filt[c] = jnp.concatenate([tall[:ROWS], tall[ROWS:]], axis=1)

    def compress(r):
        for which in range(3):
            pulse_copy(r, which).wait_recv()
        pl.when(r < LANE_PULSES - 1)(lambda: send_pulse(r + 1))
        twist_re, twist_im = twist[0], twist[1]
        v = times_left(first[...], jnp.concatenate([x_ref[r, 0], x_ref[r, 1]], axis=0))
        re, im = cmul(v[:ROWS], v[ROWS:], twist_re, twist_im)
        s = times_right(jnp.concatenate([re, im], axis=1), fwd[...])
        re, im = cmul(s[:, :LANES], s[:, LANES:], filt[0], filt[1])
        s = times_right(jnp.concatenate([re, im], axis=1), back[...])
        re, im = cmul(s[:, :LANES], s[:, LANES:], twist_re, -twist_im)
        high, low = split(jnp.concatenate([re, im], axis=0))
        v_ref[r, 0 : 2 * ROWS] = high
        v_ref[r, 2 * ROWS : 4 * ROWS] = low
        v_ref[r, 4 * ROWS : 6 * ROWS] = high

    def chunk_of(t):
        one, three = jnp.where(core == 0, t == 1, t == 2), jnp.where(core == 0, t == 2, t == 1)
        step = jnp.where(t == 0, 2, jnp.where(one, 1, jnp.where(three, 3, 0)))
        return lax.rem(y + step, CHUNKS)

    def z_copy(block, off):
        to = lax.rem(z + off, PLANES)
        return pltpu.make_async_remote_copy(
            src_ref=y_ref.at[block, to],
            dst_ref=z_ref.at[block, pl.ds(pl.multiple_of(PIECE * z, 8), PIECE)],
            send_sem=z_send.at[block],
            recv_sem=z_recv.at[block],
            device_id=device(to, chip, core),
            device_id_type=MESH,
        )

    def z_mine(block):
        return pltpu.make_async_copy(
            y_ref.at[block, z], z_ref.at[block, pl.ds(pl.multiple_of(PIECE * z, 8), PIECE)], z_recv.at[block]
        )

    def send_to(block, first, last):
        def start(step, _):
            near = last - step
            z_copy(block, near).start()
            z_copy(block, PLANES - near).start()
            return 0

        lax.fori_loop(0, last - first + 1, start, 0)

    def send_far(block):
        z_copy(block, PLANES // 2).start()
        send_to(block, NEAR + 1, PLANES // 2 - 1)
        z_mine(block).start()

    def send_near(block):
        send_to(block, 1, NEAR)

    def send_block(block):
        send_far(block)
        send_near(block)

    def wait_for(ref, sem):
        pltpu.make_async_copy(ref, ref, sem).wait()

    def sent_block(block):
        wait_for(y_ref.at[block, pl.ds(0, PLANES - 1)], z_send.at[block])

    size = 2 * CHUNK_ROWS

    def one_pulse(r, _):
        compress(r)
        for chunk in range(CHUNKS):
            out = jnp.dot(last[chunk], v_ref[r], preferred_element_type=F32)
            for to in range(PLANES):
                y_ref[r, to, size * chunk : size * (chunk + 1), :] = out[size * to : size * (to + 1)]
        send_block(r)
        return 0

    def two_chunks(pair, _):
        both = jnp.concatenate([v_ref[2], v_ref[3]], axis=1)
        for half in range(2):
            out = jnp.dot(last[chunk_of(2 * pair + half)], both, preferred_element_type=F32)
            for r in range(2):
                place = size * (2 * half + r)
                for to in range(PLANES):
                    y_ref[2 + pair, to, place : place + size, :] = out[
                        size * to : size * (to + 1), LANES * r : LANES * (r + 1)
                    ]
        return 0

    def later_pulse(r, _):
        compress(r)
        return 0

    lax.fori_loop(0, 2, one_pulse, 0)
    lax.fori_loop(2, 4, later_pulse, 0)
    lax.fori_loop(0, 2, two_chunks, 0)

    def turn_filter(step, _):
        rows = pl.ds(pl.multiple_of(8 * step, 8), 8)
        for c in range(2):
            got = swap_blocks([azf_in[c, rows, LANES * k : LANES * (k + 1)] for k in range(16)], 1)
            for k1 in range(16):
                a_ref[c, k1, rows, :] = got[k1]
        return 0

    lax.fori_loop(0, BINS // 8, turn_filter, 0)

    def by_bin(values):
        tall = values.T
        return jnp.concatenate([tall[16 * u : 16 * (u + 1)] for u in range(8)], axis=1)

    shift_ref[...] = by_bin(shift_in[...])
    frac = by_bin(frac_in[...])
    for tap in range(TAPS):
        weight = jnp.zeros(frac.shape, F32)
        for row in range(16):
            weight = jnp.where(frac == row, ktab[tap, row], weight)
        w_ref[tap] = weight

    for r in range(LANE_PULSES):
        for which in range(3):
            pulse_copy(r, which).wait_send()

    sent_block(0)
    send_block(2)
    sent_block(1)
    send_far(3)
    sent_block(2)
    send_near(3)

    def main_copy(t, q, src, dst, size):
        return pltpu.make_async_remote_copy(
            src_ref=t_ref.at[t, pl.ds(src, size)],
            dst_ref=g_ref.at[chip, pl.ds(dst, size)],
            send_sem=p_send.at[t, q],
            recv_sem=p_recv.at[y],
            device_id=device(z, 4 * chunk_of(t) + q, core),
            device_id_type=MESH,
        )

    def main_own(src, dst, size):
        return pltpu.make_async_copy(
            t_ref.at[CHUNKS - 1, pl.ds(src, size)], g_ref.at[chip, pl.ds(dst, size)], p_recv.at[y]
        )

    def windows(q, act):
        pl.when(q == 0)(lambda: act(0, BELOW, PAIR - BELOW))
        pl.when(q == 3)(lambda: act(CHUNK - BELOW - 2 * BINS, 0, PAIR - ABOVE))
        middle = jnp.logical_and(q > 0, q < 3)
        pl.when(middle)(lambda: act(pl.multiple_of(2 * BINS * q - BELOW, 8), 0, PAIR))

    def halo_targets(chunk):
        down_chip = lax.rem(4 * chunk + CHIPS - 1, CHIPS)
        up_chip = lax.rem(4 * chunk + 4, CHIPS)
        down_plane = jnp.where(chunk == 0, z - 1, z)
        up_plane = jnp.where(chunk == CHUNKS - 1, z + 1, z)
        return down_plane, down_chip, up_plane, up_chip

    DOWN = (0, PAIR - ABOVE, ABOVE)
    UP = (CHUNK - BELOW, 0, BELOW)

    def halo_copy(t, which, plane, to):
        src, dst, size = (DOWN, UP)[which]
        return pltpu.make_async_remote_copy(
            src_ref=t_ref.at[t, pl.ds(src, size)],
            dst_ref=g_ref.at[chip, pl.ds(dst, size)],
            send_sem=h_send.at[t, which],
            recv_sem=h_recv.at[y],
            device_id=device(plane, to, core),
            device_id_type=MESH,
        )

    def halo_mine(t, which):
        src, dst, size = (DOWN, UP)[which]
        return pltpu.make_async_copy(
            t_ref.at[t, pl.ds(src, size)], g_ref.at[chip, pl.ds(dst, size)], h_recv.at[y]
        )

    def each_halo(t, remote, local):
        down_plane, down_chip, up_plane, up_chip = halo_targets(chunk_of(t))
        for which, plane, to in ((0, down_plane, down_chip), (1, up_plane, up_chip)):
            inside = jnp.logical_and(plane >= 0, plane < PLANES)
            me = jnp.logical_and(plane == z, to == chip)
            pl.when(jnp.logical_and(inside, jnp.logical_not(me)))(
                functools.partial(remote, t, which, plane, to)
            )
            pl.when(me)(functools.partial(local, t, which))

    def each_main(t, act):
        for off in range(4):
            q = lax.rem(q_me + off, 4)
            to_me = jnp.logical_and(t == CHUNKS - 1, off == 0)

            def remote(q=q):
                windows(q, functools.partial(act, t, q))

            pl.when(jnp.logical_not(to_me))(remote)

    def wait_block(block, _):
        wait_for(z_ref.at[block], z_recv.at[block])
        return 0

    def sent_chunk(t, _):
        each_main(t, lambda *a: main_copy(*a).wait_send())
        each_halo(t, lambda *a: halo_copy(*a).wait_send(), lambda *a: None)
        return 0

    def plane_step(t, _):
        @pl.when(t == 0)
        def _():
            lax.fori_loop(0, 3, wait_block, 0)

        @pl.when(t == 2)
        def _():
            lax.fori_loop(0, 2, sent_chunk, 0)
            wait_block(3, 0)

        pair = lax.div(t, 2)
        half = lax.rem(t, 2)
        chunk = chunk_of(t)
        for row in range(CHUNK_ROWS):
            parts = []
            for c in range(2):
                for r in range(2):
                    start = size * chunk + CHUNK_ROWS * c + row
                    parts.append(z_ref[r, pl.ds(start, PLANES, stride=PIECE), :])
                for r in range(2):
                    start = size * (2 * half + r) + CHUNK_ROWS * c + row
                    parts.append(z_ref[2 + pair, pl.ds(start, PLANES, stride=PIECE), :])
            t_ref[t, LANES * row : LANES * (row + 1), :] = times_right(
                jnp.concatenate(parts, axis=0).T, planes[...]
            )
        each_main(t, lambda *a: main_copy(*a).start())

        each_halo(t, lambda *a: halo_copy(*a).start(), lambda *a: halo_mine(*a).start())
        return 0

    lax.fori_loop(0, CHUNKS, plane_step, 0)

    windows(q_me, lambda *a: main_own(*a).start())

    def core_copy(row):
        return pltpu.make_async_remote_copy(
            src_ref=g_ref.at[pl.ds(4 * row, 4), pl.ds(pl.multiple_of(BINS * (1 - core), 8), WINDOW)],
            dst_ref=o_ref.at[pl.ds(4 * row, 4)],
            send_sem=fwd_send.at[row],
            recv_sem=fwd_recv.at[row],
            device_id=core_partner,
            device_id_type=MESH,
        )

    takes_up = jnp.logical_and(q_me == 0, jnp.logical_or(y > 0, has_below))
    takes_down = jnp.logical_and(q_me == 3, jnp.logical_or(y < 3, has_above))

    def gather(t, _):
        row = lax.rem(y + CHUNKS - chunk_of(t) + y, CHUNKS)

        def rows_of(start, size):
            return g_ref.at[pl.ds(4 * row, 4), pl.ds(start, size)]

        windows(q_me, lambda src, dst, size: wait_for(rows_of(dst, size), p_recv.at[row]))
        pl.when(takes_up)(lambda: wait_for(rows_of(0, BELOW), h_recv.at[row]))
        pl.when(takes_down)(lambda: wait_for(rows_of(PAIR - ABOVE, ABOVE), h_recv.at[row]))
        core_copy(row).start()
        return 0

    lax.fori_loop(0, CHUNKS, gather, 0)

    part = WINDOW // 2

    def turn_rows(read):
        def body(step, _):
            rows = pl.ds(pl.multiple_of(part * step, 8), part)
            got = swap_blocks([read(k, part * step) for k in range(CHIPS)], 8)
            for k1 in range(16):
                h_ref[k1, rows, :] = got[k1]
            return 0

        lax.fori_loop(0, WINDOW // part, body, 0)

    group = 4

    def transform(from_core, add):
        def body(step, _):
            high, low = split(h_ref[pl.ds(group * step, group)].reshape(group * WINDOW, LANES))
            d = jnp.dot(
                jnp.concatenate([high, low, high], axis=1), az_fwd[from_core], preferred_element_type=F32
            )
            for k in range(group):
                for c in range(2):
                    piece = d[WINDOW * k : WINDOW * (k + 1), LANES * c : LANES * (c + 1)]
                    if add:
                        piece = piece + d_ref[group * step + k, c]
                    d_ref[group * step + k, c] = piece
            return 0

        lax.fori_loop(0, 16 // group, body, 0)

    turn_rows(lambda k, start: g_ref[k, pl.ds(pl.multiple_of(BINS * core + start, 8), part), :])
    transform(core, False)

    def wait_core(row, _):
        core_copy(row).wait_recv()
        return 0

    lax.fori_loop(2, 4, sent_chunk, 0)
    sent_block(3)
    lax.fori_loop(0, 4, wait_core, 0)
    turn_rows(lambda k, start: o_ref[k, pl.ds(pl.multiple_of(start, 8), part), :])
    transform(1 - core, True)

    def migrate(k1, slot):
        shift = shift_ref[pl.ds(k1, 1), :]
        weights = [w_ref[tap, pl.ds(k1, 1), :] for tap in range(TAPS)]
        moved = []
        for c in range(2):
            x = d_ref[k1, c]
            near = jnp.where((shift & 16) != 0, x[16:80], x[0:64])
            x = jnp.concatenate([near, x[64:80]], axis=0)
            m, e = m_ref.at[slot, c], e_ref.at[slot, c]
            m[0:72] = jnp.where((shift & 8) != 0, x[8:80], x[0:72])
            e[0:64] = jnp.where((shift & 4) != 0, m[4:68], m[0:64])
            m[0:62] = jnp.where((shift & 2) != 0, e[2:64], e[0:62])
            e[0:61] = jnp.where((shift & 1) != 0, m[1:62], m[0:61])
            total = weights[0] * e[5 : 5 + BINS]
            for tap in range(1, TAPS):
                total = total + weights[tap] * e[5 + tap : 5 + tap + BINS]
            moved.append(total)
        return jnp.concatenate(cmul(moved[0], moved[1], a_ref[0, k1], a_ref[1, k1]), axis=1)

    def result_copy(step):
        some = pl.ds(group * step, group)
        return pltpu.make_async_copy(f_ref.at[:, some], out_hbm.at[:, some], out_sem.at[step])

    def per_group(step, _):
        ks = [group * step + k for k in range(group)]
        s = times_right(jnp.concatenate([migrate(k1, k) for k, k1 in enumerate(ks)], axis=0), az_back[...])
        for k, k1 in enumerate(ks):
            rows = slice(BINS * k, BINS * (k + 1))
            f_ref[0, k1], f_ref[1, k1] = cmul(
                s[rows, :LANES], s[rows, LANES:], az_twist[0, pl.ds(k1, 1), :], az_twist[1, pl.ds(k1, 1), :]
            )
        result_copy(step).start()
        return 0

    lax.fori_loop(0, 16 // group, per_group, 0)

    def sent_core(row, _):
        core_copy(row).wait_send()
        return 0

    lax.fori_loop(0, 4, sent_core, 0)
    for step in range(16 // group):
        result_copy(step).wait()


def finish_kernel(f_hbm, out_hbm, f_ref, out_ref, in_sem, out_sem):
    def fetch(step):
        rows = slice(8 * step, 8 * (step + 1))
        return pltpu.make_async_copy(f_hbm.at[:, :, rows], f_ref.at[:, :, rows], in_sem.at[step])

    def store(step):
        rows = slice(8 * step, 8 * (step + 1))
        return pltpu.make_async_copy(out_ref.at[:, rows], out_hbm.at[:, rows], out_sem.at[step])

    for step in range(BINS // 8):
        fetch(step).start()
    for step in range(BINS // 8):
        rows = slice(8 * step, 8 * (step + 1))
        fetch(step).wait()
        got = fft_list([(f_ref[0, k1, rows, :], f_ref[1, k1, rows, :]) for k1 in range(16)], 1)
        for tile in range(16):
            for c in range(2):
                out_ref[c, rows, LANES * tile : LANES * (tile + 1)] = got[tile][c]
        store(step).start()
    for step in range(BINS // 8):
        store(step).wait()


IN_HBM = pl.BlockSpec(memory_space=pltpu.HBM)
DMA = pltpu.SemaphoreType.DMA


def shards(raw, range_filter, azimuth_filter, shifts, frac_index, kernel_table):
    order = filter_order()
    tables = [
        table_first(),
        table_last(),
        table_twist(),
        right_factor(table_columns(np.arange(LANES), order, -1)),
        right_factor(table_columns(order, np.arange(LANES), 1)),
        table_planes(),
        table_azimuth(),
        table_back(),
        table_back_twist(),
    ]
    operands = [
        raw.reshape(2, 2, 8, 48, LANES).transpose(0, 1, 3, 2, 4).reshape(2, 2, 384, LANES),
        range_filter.reshape(2, ROWS, LANES).transpose(1, 0, 2).reshape(2 * ROWS, LANES),
        azimuth_filter,
        shifts.reshape(16, LANES),
        frac_index.reshape(16, LANES),
        kernel_table.T,
    ]

    def like(array, shape=None):
        return pltpu.VMEM(array.shape if shape is None else shape, array.dtype)

    loads = [like(a) for a in operands[1:5]] + [pltpu.SMEM(operands[5].shape, F32)]
    loads += [like(a) for a in tables]
    loads[5 + 5] = like(tables[5], tables[5].shape[1:])
    scratch = [
        pltpu.VMEM((2, 2, 384, LANES), F32),
        pltpu.VMEM((LANE_PULSES, 2, 48, LANES), F32),
        pltpu.VMEM((LANE_PULSES, 2, 48, LANES), F32),
        pltpu.VMEM((LANE_PULSES, 2, 48, LANES), F32),
        pltpu.VMEM((LANE_PULSES, 2, ROWS, LANES), F32),
        pltpu.VMEM((2, ROWS, LANES), F32),
        pltpu.VMEM((LANE_PULSES, 6 * ROWS, LANES), BF16),
        pltpu.VMEM((CHUNKS, PLANES, PIECE, LANES), F32),
        pltpu.VMEM((CHUNKS, PLANES * PIECE, LANES), F32),
        pltpu.VMEM((CHUNKS, CHUNK, LANES), F32),
        pltpu.VMEM((CHIPS, PAIR, LANES), F32),
        pltpu.VMEM((CHIPS, WINDOW, LANES), F32),
        pltpu.VMEM((16, LANES), jnp.int32),
        pltpu.VMEM((TAPS, 16, LANES), F32),
        pltpu.VMEM((2, 16, BINS, LANES), F32),
        pltpu.VMEM((16, WINDOW, LANES), F32),
        pltpu.VMEM((16, 2, WINDOW, LANES), F32),
        pltpu.VMEM((4, 2, WINDOW, LANES), F32),
        pltpu.VMEM((4, 2, WINDOW, LANES), F32),
        pltpu.VMEM((2, 16, BINS, LANES), F32),
        DMA((2,)), DMA((4, 3)), DMA((4, 3)),
        DMA((4,)), DMA((4,)),
        DMA((CHUNKS, 4)), DMA((4,)), DMA((CHUNKS, 2)), DMA((4,)), DMA((4,)), DMA((4,)), DMA((4,)),
    ]
    turned = pl.pallas_call(
        kernel,
        out_shape=jax.ShapeDtypeStruct((2, 16, BINS, LANES), F32),
        in_specs=[IN_HBM] * (len(operands) + len(tables)),
        out_specs=IN_HBM,
        scratch_shapes=loads + [DMA((len(loads),))] + scratch,
        compiler_params=pltpu.CompilerParams(
            vmem_limit_bytes=60 * 2**20, collective_id=0, has_side_effects=True
        ),
    )(*operands, *tables)
    return pl.pallas_call(
        finish_kernel,
        out_shape=jax.ShapeDtypeStruct((2, BINS, PULSES), F32),
        in_specs=[IN_HBM],
        out_specs=IN_HBM,
        scratch_shapes=[
            pltpu.VMEM((2, 16, BINS, LANES), F32),
            pltpu.VMEM((2, BINS, PULSES), F32),
            DMA((BINS // 8,)),
            DMA((BINS // 8,)),
        ],
        compiler_params=pltpu.CompilerParams(vmem_limit_bytes=60 * 2**20),
    )(turned)


def solution(mesh):
    in_specs = (P(None, "pulse", "rng"), P(), P(None, ("pulse", "rng"), None), P(), P(), P())
    out_specs = P(None, ("pulse", "rng"), None)
    return jax.shard_map(shards, mesh=mesh, in_specs=in_specs, out_specs=out_specs, check_vma=False)
```

```python
import functools
import math

import jax
import jax.numpy as jnp
import ml_dtypes
import numpy as np
from jax import lax
from jax.experimental import pallas as pl
from jax.experimental.pallas import tpu as pltpu
from jax.sharding import PartitionSpec as P

MESH = pl.DeviceIdType.MESH
F32 = jnp.float32
BF16 = jnp.bfloat16

PULSES = 2048
SAMPLES = 24576
ROWS = 192
LANES = 128
PLANES = 16
PEERS = 32
CHIPS = 16
LANE_PULSES = 4
BINS = 48
CHUNKS = 4
CHUNK_ROWS = 3
CHUNK = CHUNK_ROWS * LANES
BLOCKS = (24, 24, 16, 16, 16)
BELOW = 8
ABOVE = 24
WINDOW = BELOW + BINS + ABOVE
PAIR = BELOW + 2 * BINS + ABOVE
TAPS = 8
ORDER = ((2, 1, 3, 0), (2, 3, 1, 0))


def turn(product, period, sign):
    angle = sign * 2.0 * math.pi * (product % period) / period
    return np.cos(angle), np.sin(angle)


def halves(table):
    high = table.astype(ml_dtypes.bfloat16)
    low = (table - high.astype(np.float64)).astype(ml_dtypes.bfloat16)
    return high, low


def left_factor(table):
    high, low = halves(table)
    return np.concatenate([high, high, low], axis=1)


def right_factor(table):
    high, low = halves(table)
    return np.concatenate([high, high, low], axis=-2)


def lane_bins():
    lanes = np.arange(LANES)
    return 8 * (lanes % 16) + lanes // 16


def table_first():
    ids = np.arange(ROWS)
    re, im = turn(np.outer(ids, ids), ROWS, -1)
    return left_factor(np.block([[re, -im], [im, re]]))


def table_last():
    ids = np.arange(ROWS)
    re, im = turn(np.outer(ids, ids), ROWS, 1)
    full = np.stack([np.concatenate([re, -im], axis=1), np.concatenate([im, re], axis=1)]) / SAMPLES
    full = full.reshape(2, PLANES, CHUNKS, CHUNK_ROWS, 2 * ROWS).transpose(2, 1, 0, 3, 4)
    return left_factor(full.reshape(2 * ROWS, 2 * ROWS)).reshape(CHUNKS, 2 * ROWS // CHUNKS, -1)


def filter_order():
    lanes = np.arange(LANES)
    return 2 * (lanes % 64) + lanes // 64


def table_columns(rows, cols, sign, scale=1.0):
    re, im = turn(np.outer(rows, cols), LANES, sign)
    return np.block([[re, im], [-im, re]]) * scale


def table_twist():
    re, im = turn(np.outer(np.arange(ROWS), np.arange(LANES)), SAMPLES, -1)
    return np.stack([re, im]).astype(np.float32)


def table_planes():
    place = np.arange(PEERS)[:, None, None, None]
    r = np.arange(LANE_PULSES)[None, :, None, None]
    z = np.arange(PLANES)[None, None, :, None]
    k1 = np.arange(16)[None, None, None, :]
    re, im = turn((128 * z + 4 * place + r) * k1, PULSES, -1)
    full = np.zeros((PEERS, 2, LANE_PULSES, PLANES, 16, 2, LANE_PULSES))
    for q in range(LANE_PULSES):
        full[:, 0, q, :, :, 0, q] = re[:, q]
        full[:, 1, q, :, :, 0, q] = -im[:, q]
        full[:, 0, q, :, :, 1, q] = im[:, q]
        full[:, 1, q, :, :, 1, q] = re[:, q]
    return right_factor(full.reshape(PEERS, 128, 128))


def table_azimuth():
    place = np.arange(PEERS)[:, None, None]
    r = np.arange(LANE_PULSES)[None, :, None]
    re, im = turn((4 * place + r) * lane_bins()[None, None, :], LANES, -1)
    full = np.zeros((PEERS, 2, LANE_PULSES, 2, LANES))
    full[:, 0, :, 0] = re
    full[:, 1, :, 0] = -im
    full[:, 0, :, 1] = im
    full[:, 1, :, 1] = re
    by_core = full.reshape(CHIPS, 2, 8, 2 * LANES).transpose(1, 0, 2, 3)
    return right_factor(by_core.reshape(2, LANES, 2 * LANES))


def table_back():
    return right_factor(table_columns(lane_bins(), np.arange(LANES), 1, 1.0 / PULSES))


def table_back_twist():
    re, im = turn(np.outer(np.arange(16), np.arange(LANES)), PULSES, 1)
    return np.stack([re, im]).astype(np.float32)


def split(values):
    high = values.astype(BF16)
    low = (values - high.astype(F32)).astype(BF16)
    return high, low


def times_left(table, values):
    high, low = split(values)
    return jnp.dot(table, jnp.concatenate([high, low, high], axis=0), preferred_element_type=F32)


def times_right(values, table):
    high, low = split(values)
    return jnp.dot(jnp.concatenate([high, low, high], axis=1), table, preferred_element_type=F32)


def cmul(a_re, a_im, b_re, b_im):
    return a_re * b_re - a_im * b_im, a_re * b_im + a_im * b_re


def fft_list(values, sign):
    count = len(values)
    if count == 1:
        return values
    even = fft_list(values[0::2], sign)
    odd = fft_list(values[1::2], sign)
    low, high = [], []
    for k in range(count // 2):
        re, im = odd[k]
        if 4 * k == count:
            re, im = (-im, re) if sign > 0 else (im, -re)
        elif k:
            w_re = math.cos(2.0 * math.pi * k / count)
            w_im = sign * math.sin(2.0 * math.pi * k / count)
            re, im = re * w_re - im * w_im, re * w_im + im * w_re
        low.append((even[k][0] + re, even[k][1] + im))
        high.append((even[k][0] - re, even[k][1] - im))
    return low + high


def swap_blocks(arrays, width):
    arrays = list(arrays)
    lane = lax.broadcasted_iota(jnp.int32, arrays[0].shape, 1)
    for bit in (1, 2, 4, 8):
        keep = (lane // width) & bit == 0
        for a in range(16):
            if a & bit:
                continue
            first, second = arrays[a], arrays[a + bit]
            arrays[a] = jnp.where(keep, first, pltpu.roll(second, bit * width, 1))
            arrays[a + bit] = jnp.where(keep, pltpu.roll(first, LANES - bit * width, 1), second)
    return arrays


def kernel(
    raw_hbm, filt_hbm, azf_hbm, shift_hbm, frac_hbm, ktab_hbm,
    first_hbm, last_hbm, twist_hbm, fwd_hbm, back_hbm, planes_hbm, az_fwd_hbm, az_back_hbm, az_twist_hbm,
    out_hbm,
    filt_in, azf_in, shift_in, frac_in, ktab, first, last, twist, fwd, back, planes, az_fwd, az_back, az_twist,
    load_sem,
    tiles, to_like, to_cross, to_core, x_ref, filt, v_ref, y0, y1, y2, y3, y4, z0, z1, z2, z3, z4, t_ref, g_ref, o_ref,
    shift_ref, w_ref, a_ref, h_ref, d_ref, m_ref, e_ref, f_ref,
    tile_sem, x_send, x_recv, z_send, z_recv,
    p_send, p_recv, h_send, h_recv, fwd_send, fwd_recv, out_sem,
):
    pulse = lax.axis_index("pulse")
    lane = lax.axis_index("rng")
    z = lax.div(pulse, 8)
    y = lax.rem(lax.div(pulse, 2), 4)
    xh = lax.div(lane, 2)
    core = lax.rem(lane, 2)
    q_me = 2 * lax.rem(pulse, 2) + xh
    chip = 4 * y + q_me
    has_below = z > 0
    has_above = z < PLANES - 1

    def device(plane, other_chip, other_core):
        return (8 * plane + lax.div(other_chip, 2), 2 * lax.rem(other_chip, 2) + other_core)

    x_partner = (pulse, 2 * (1 - xh) + core)
    x_cross = (pulse, 2 * (1 - xh) + 1 - core)
    core_partner = (pulse, 2 * xh + 1 - core)

    place = 2 * chip + core
    loads = [
        (filt_hbm, filt_in), (first_hbm, first), (twist_hbm, twist), (fwd_hbm, fwd), (back_hbm, back),
        (last_hbm, last), (planes_hbm.at[place], planes), (azf_hbm, azf_in), (shift_hbm, shift_in),
        (frac_hbm, frac_in), (ktab_hbm, ktab), (az_fwd_hbm, az_fwd), (az_back_hbm, az_back),
        (az_twist_hbm, az_twist),
    ]
    loads = [pltpu.make_async_copy(src, dst, load_sem.at[k]) for k, (src, dst) in enumerate(loads)]
    tile_loads = [
        pltpu.make_async_copy(raw_hbm.at[:, 1 - xh], tiles.at[1], tile_sem.at[1]),
        pltpu.make_async_copy(raw_hbm.at[:, xh], tiles.at[0], tile_sem.at[0]),
    ]
    for load in tile_loads:
        load.start()

    barrier = pltpu.get_barrier_semaphore()

    def greet(to):
        pl.semaphore_signal(barrier, inc=1, device_id=to, device_id_type=MESH)

    greet(x_partner)
    greet(x_cross)
    greet(core_partner)

    def greet_z(off, _):
        greet(device(lax.rem(z + off, PLANES), chip, core))
        return 0

    def greet_plane(off, _):
        greet(device(z, lax.rem(chip + off, CHIPS), core))
        return 0

    def greet_all(plane):
        def body(other, _):
            greet(device(plane, other, core))
            return 0

        lax.fori_loop(0, CHIPS, body, 0)

    lax.fori_loop(1, PLANES, greet_z, 0)
    lax.fori_loop(1, CHIPS, greet_plane, 0)
    pl.when(jnp.logical_and(chip == 0, has_below))(lambda: greet_all(z - 1))
    pl.when(jnp.logical_and(chip == CHIPS - 1, has_above))(lambda: greet_all(z + 1))

    for load in loads:
        load.start()

    def blank(start, size):
        def body(other, _):
            g_ref[other, start : start + size, :] = jnp.zeros((size, LANES), F32)
            return 0

        lax.fori_loop(0, CHIPS, body, 0)

    pl.when(jnp.logical_and(chip == 0, z == 0))(lambda: blank(0, BELOW))
    pl.when(jnp.logical_and(chip == CHIPS - 1, z == PLANES - 1))(lambda: blank(PAIR - ABOVE, ABOVE))

    my_quarter = 2 * xh + core

    def quarter_rows(quarter):
        return pl.ds(pl.multiple_of(48 * quarter, 8), 48)

    for load in tile_loads:
        load.wait()
    def sort_pulse(r):
        like = pl.ds(4 * core + r, 48, stride=8)
        other = pl.ds(4 * (1 - core) + r, 48, stride=8)
        for c in range(2):
            to_like[r, c] = tiles[1, c, like, :]
            to_cross[r, c] = tiles[1, c, other, :]
            to_core[r, c] = tiles[0, c, other, :]
            x_ref[r, c, quarter_rows(my_quarter), :] = tiles[0, c, like, :]

    sort_pulse(0)
    pl.semaphore_wait(
        barrier,
        3 + PLANES - 1 + CHIPS - 1 + jnp.where(has_below, 1, 0) + jnp.where(has_above, 1, 0),
    )

    def pulse_copy(r, which):
        return pltpu.make_async_remote_copy(
            src_ref=(to_like, to_cross, to_core)[which].at[r],
            dst_ref=x_ref.at[r, :, quarter_rows(my_quarter)],
            send_sem=x_send.at[r, which],
            recv_sem=x_recv.at[r, which],
            device_id=(x_partner, x_cross, core_partner)[which],
            device_id_type=MESH,
        )

    def send_pulse(r):
        for which in range(3):
            pulse_copy(r, which).start()

    send_pulse(0)
    for r in range(1, LANE_PULSES):
        sort_pulse(r)

    for load in loads:
        load.wait()
    for c in range(2):
        cols = [filt_in[pl.ds(2 * u + c, 64, stride=6), :].T for u in range(3)]
        tall = jnp.concatenate(cols, axis=0)
        filt[c] = jnp.concatenate([tall[:ROWS], tall[ROWS:]], axis=1)

    def wait_pulse(r):
        for which in range(3):
            pulse_copy(r, which).wait_recv()

    def compress(r):
        twist_re, twist_im = twist[0], twist[1]
        v = times_left(first[...], jnp.concatenate([x_ref[r, 0], x_ref[r, 1]], axis=0))
        re, im = cmul(v[:ROWS], v[ROWS:], twist_re, twist_im)
        s = times_right(jnp.concatenate([re, im], axis=1), fwd[...])
        re, im = cmul(s[:, :LANES], s[:, LANES:], filt[0], filt[1])
        s = times_right(jnp.concatenate([re, im], axis=1), back[...])
        re, im = cmul(s[:, :LANES], s[:, LANES:], twist_re, -twist_im)
        high, low = split(jnp.concatenate([re, im], axis=0))
        v_ref[r, 0 : 2 * ROWS] = high
        v_ref[r, 2 * ROWS : 4 * ROWS] = low
        v_ref[r, 4 * ROWS : 6 * ROWS] = high

    ys, zs = (y0, y1, y2, y3, y4), (z0, z1, z2, z3, z4)

    def chunk_of(t):
        if t in (0, 3):
            return lax.rem(y + (2 if t == 0 else 0), CHUNKS)
        return lax.rem(y + jnp.where(core == t - 1, 1, 3), CHUNKS)

    def z_mine_rows(block):
        return pl.ds(pl.multiple_of(BLOCKS[block] * z, 8), BLOCKS[block])

    def z_copy(block, off):
        to = lax.rem(z + off, PLANES)
        return pltpu.make_async_remote_copy(
            src_ref=ys[block].at[to],
            dst_ref=zs[block].at[z_mine_rows(block)],
            send_sem=z_send.at[block],
            recv_sem=z_recv.at[block],
            device_id=device(to, chip, core),
            device_id_type=MESH,
        )

    def z_mine(block):
        return pltpu.make_async_copy(ys[block].at[z], zs[block].at[z_mine_rows(block)], z_recv.at[block])

    def send_block(block):
        def start(step, _):
            near = PLANES // 2 - step
            z_copy(block, near).start()
            z_copy(block, PLANES - near).start()
            return 0

        z_copy(block, PLANES // 2).start()
        lax.fori_loop(1, PLANES // 2, start, 0)
        z_mine(block).start()

    def wait_for(ref, sem):
        pltpu.make_async_copy(ref, ref, sem).wait()

    def sent_block(block):
        wait_for(ys[block].at[pl.ds(0, PLANES - 1)], z_send.at[block])

    size = 2 * CHUNK_ROWS

    def place_of(t, r, c, row):
        rows = {0: (0, 1, 2), 1: (0,) if row == 0 else (1, 2), 2: (0, 1) if row < 2 else (2,), 3: (0, 1, 2)}[t]
        block, start = {(0, 0): (2, 0), (1, 0): (2, 12), (1, 1): (3, 0), (2, 0): (3, 8), (2, 2): (4, 0), (3, 0): (4, 4)}[
            t, rows[0]
        ]
        return block, start + len(rows) * (2 * (r - 2) + c) + row - rows[0]

    for r in range(2):
        wait_pulse(r)
        send_pulse(r + 1)
        compress(r)
        for chunk in range(CHUNKS):
            out = jnp.dot(last[chunk], v_ref[r], preferred_element_type=F32)
            for to in range(PLANES):
                ys[r][to, size * chunk : size * (chunk + 1), :] = out[size * to : size * (to + 1)]
        send_block(r)

    def later_pulse(r, _):
        wait_pulse(r)
        pl.when(r < LANE_PULSES - 1)(lambda: send_pulse(r + 1))
        compress(r)
        return 0

    lax.fori_loop(2, 4, later_pulse, 0)
    both = jnp.concatenate([v_ref[2], v_ref[3]], axis=1)

    def make_chunk(t):
        out = jnp.dot(last[chunk_of(t)], both, preferred_element_type=F32)
        for r in (2, 3):
            lanes = slice(LANES * (r - 2), LANES * (r - 1))
            pieces = {1: [(0, 1), (1, 3), (3, 4), (4, 6)], 2: [(0, 2), (2, 3), (3, 5), (5, 6)]}.get(t, [(0, 6)])
            for first_row, end in pieces:
                block, place = place_of(t, r, first_row // 3, first_row % 3)
                for to in range(PLANES):
                    ys[block][to, place : place + end - first_row, :] = out[
                        size * to + first_row : size * to + end, lanes
                    ]

    for t in range(2):
        make_chunk(t)
    sent_block(0)
    send_block(2)
    for t in (2, 3):
        make_chunk(t)

    def turn_filter(step, _):
        rows = pl.ds(pl.multiple_of(8 * step, 8), 8)
        for c in range(2):
            got = swap_blocks([azf_in[c, rows, LANES * k : LANES * (k + 1)] for k in range(16)], 1)
            for k1 in range(16):
                a_ref[c, k1, rows, :] = got[k1]
        return 0

    lax.fori_loop(0, BINS // 8, turn_filter, 0)

    def by_bin(values):
        tall = values.T
        return jnp.concatenate([tall[16 * u : 16 * (u + 1)] for u in range(8)], axis=1)

    shift_ref[...] = by_bin(shift_in[...])
    frac = by_bin(frac_in[...])
    for tap in range(TAPS):
        weight = jnp.zeros(frac.shape, F32)
        for row in range(16):
            weight = jnp.where(frac == row, ktab[tap, row], weight)
        w_ref[tap] = weight

    for r in range(LANE_PULSES):
        for which in range(3):
            pulse_copy(r, which).wait_send()

    sent_block(1)
    send_block(3)
    sent_block(2)
    send_block(4)

    def window(q):
        if q == 0:
            return 0, BELOW, PAIR - BELOW
        if q == 3:
            return CHUNK - BELOW - 2 * BINS, 0, PAIR - ABOVE
        return 2 * BINS * q - BELOW, 0, PAIR

    def main_copy(t, q):
        src, dst, size = window(q)
        return pltpu.make_async_remote_copy(
            src_ref=t_ref.at[t, pl.ds(src, size)],
            dst_ref=g_ref.at[chip, pl.ds(dst, size)],
            send_sem=p_send.at[t, q],
            recv_sem=p_recv.at[y],
            device_id=device(z, 4 * chunk_of(t) + q, core),
            device_id_type=MESH,
        )

    def main_own(q):
        src, dst, size = window(q)
        return pltpu.make_async_copy(
            t_ref.at[CHUNKS - 1, pl.ds(src, size)], g_ref.at[chip, pl.ds(dst, size)], p_recv.at[y]
        )

    def each_main(t, qs, act, local):
        for q in qs:
            if t < CHUNKS - 1:
                act(main_copy(t, q))
            else:
                pl.when(q_me != q)(functools.partial(lambda q: act(main_copy(t, q)), q))
                if local:
                    pl.when(q_me == q)(functools.partial(lambda q: local(main_own(q)), q))

    def on_window(act):
        for q in range(4):
            pl.when(q_me == q)(functools.partial(lambda q: act(*window(q)), q))

    def halo_targets(chunk):
        down_chip = lax.rem(4 * chunk + CHIPS - 1, CHIPS)
        up_chip = lax.rem(4 * chunk + 4, CHIPS)
        down_plane = jnp.where(chunk == 0, z - 1, z)
        up_plane = jnp.where(chunk == CHUNKS - 1, z + 1, z)
        return down_plane, down_chip, up_plane, up_chip

    DOWN = (0, PAIR - ABOVE, ABOVE)
    UP = (CHUNK - BELOW, 0, BELOW)

    def halo_copy(t, which, plane, to):
        src, dst, size = (DOWN, UP)[which]
        return pltpu.make_async_remote_copy(
            src_ref=t_ref.at[t, pl.ds(src, size)],
            dst_ref=g_ref.at[chip, pl.ds(dst, size)],
            send_sem=h_send.at[t, which],
            recv_sem=h_recv.at[y],
            device_id=device(plane, to, core),
            device_id_type=MESH,
        )

    def halo_mine(t, which):
        src, dst, size = (DOWN, UP)[which]
        return pltpu.make_async_copy(
            t_ref.at[t, pl.ds(src, size)], g_ref.at[chip, pl.ds(dst, size)], h_recv.at[y]
        )

    def each_halo(t, whichs, act, local):
        down_plane, down_chip, up_plane, up_chip = halo_targets(chunk_of(t))
        for which, plane, to in ((0, down_plane, down_chip), (1, up_plane, up_chip)):
            if which not in whichs:
                continue
            inside = jnp.logical_and(plane >= 0, plane < PLANES)
            me = jnp.logical_and(plane == z, to == chip)
            pl.when(jnp.logical_and(inside, jnp.logical_not(me)))(
                functools.partial(lambda *a: act(halo_copy(*a)), t, which, plane, to)
            )
            if local:
                pl.when(me)(functools.partial(lambda *a: local(halo_mine(*a)), t, which))

    def wait_block(block):
        wait_for(zs[block], z_recv.at[block])

    def start(copy):
        copy.start()

    def sent_chunk(t):
        each_main(t, range(4), lambda copy: copy.wait_send(), None)
        each_halo(t, (0, 1), lambda copy: copy.wait_send(), None)

    def turn_chunk(t, rows):
        chunk = chunk_of(t)
        for row in rows:
            parts = []
            for c in range(2):
                for r in range(2):
                    place = size * chunk + CHUNK_ROWS * c + row
                    parts.append(zs[r][pl.ds(place, PLANES, stride=BLOCKS[r]), :])
                for r in (2, 3):
                    block, place = place_of(t, r, c, row)
                    parts.append(zs[block][pl.ds(place, PLANES, stride=BLOCKS[block]), :])
            t_ref[t, LANES * row : LANES * (row + 1), :] = times_right(
                jnp.concatenate(parts, axis=0).T, planes[...]
            )

    for block in range(3):
        wait_block(block)
    turn_chunk(0, range(CHUNK_ROWS))
    each_main(0, range(4), start, start)
    each_halo(0, (0, 1), start, start)
    wait_block(3)
    turn_chunk(1, range(CHUNK_ROWS))
    each_main(1, range(4), start, start)
    each_halo(1, (0, 1), start, start)
    turn_chunk(2, range(2))
    each_main(2, (0, 1), start, start)
    each_halo(2, (0,), start, start)
    sent_chunk(0)
    wait_block(4)
    turn_chunk(2, (2,))
    each_main(2, (2, 3), start, start)
    each_halo(2, (1,), start, start)
    turn_chunk(3, range(CHUNK_ROWS))
    each_main(3, range(4), start, start)
    each_halo(3, (0, 1), start, start)

    def core_copy(row):
        return pltpu.make_async_remote_copy(
            src_ref=g_ref.at[pl.ds(4 * row, 4), pl.ds(pl.multiple_of(BINS * (1 - core), 8), WINDOW)],
            dst_ref=o_ref.at[pl.ds(4 * row, 4)],
            send_sem=fwd_send.at[row],
            recv_sem=fwd_recv.at[row],
            device_id=core_partner,
            device_id_type=MESH,
        )

    takes_up = jnp.logical_and(q_me == 0, jnp.logical_or(y > 0, has_below))
    takes_down = jnp.logical_and(q_me == 3, jnp.logical_or(y < 3, has_above))

    def gather(t):
        row = lax.rem(2 * y + CHUNKS - chunk_of(t), CHUNKS)

        def rows_of(first_row, count):
            return g_ref.at[pl.ds(4 * row, 4), pl.ds(first_row, count)]

        on_window(lambda src, dst, count: wait_for(rows_of(dst, count), p_recv.at[row]))
        pl.when(takes_up)(lambda: wait_for(rows_of(0, BELOW), h_recv.at[row]))
        pl.when(takes_down)(lambda: wait_for(rows_of(PAIR - ABOVE, ABOVE), h_recv.at[row]))
        core_copy(row).start()

    for t in range(CHUNKS):
        gather(t)

    part = WINDOW // 2

    def turn_rows(read):
        def body(step, _):
            rows = pl.ds(pl.multiple_of(part * step, 8), part)
            got = swap_blocks([read(k, part * step) for k in range(CHIPS)], 8)
            for k1 in range(16):
                h_ref[k1, rows, :] = got[k1]
            return 0

        lax.fori_loop(0, WINDOW // part, body, 0)

    group = 4

    def transform(from_core, add):
        def body(step, _):
            high, low = split(h_ref[pl.ds(group * step, group)].reshape(group * WINDOW, LANES))
            d = jnp.dot(
                jnp.concatenate([high, low, high], axis=1), az_fwd[from_core], preferred_element_type=F32
            )
            for k in range(group):
                for c in range(2):
                    piece = d[WINDOW * k : WINDOW * (k + 1), LANES * c : LANES * (c + 1)]
                    if add:
                        piece = piece + d_ref[group * step + k, c]
                    d_ref[group * step + k, c] = piece
            return 0

        lax.fori_loop(0, 16 // group, body, 0)

    turn_rows(lambda k, start: g_ref[k, pl.ds(pl.multiple_of(BINS * core + start, 8), part), :])
    transform(core, False)

    def wait_core(row, _):
        core_copy(row).wait_recv()
        return 0

    for t in (1, 2, 3):
        sent_chunk(t)
    sent_block(3)
    sent_block(4)
    lax.fori_loop(0, 4, wait_core, 0)
    turn_rows(lambda k, start: o_ref[k, pl.ds(pl.multiple_of(start, 8), part), :])
    transform(1 - core, True)

    def migrate(k1, slot):
        shift = shift_ref[pl.ds(k1, 1), :]
        weights = [w_ref[tap, pl.ds(k1, 1), :] for tap in range(TAPS)]
        moved = []
        for c in range(2):
            x = d_ref[k1, c]
            near = jnp.where((shift & 16) != 0, x[16:80], x[0:64])
            x = jnp.concatenate([near, x[64:80]], axis=0)
            m, e = m_ref.at[slot, c], e_ref.at[slot, c]
            m[0:72] = jnp.where((shift & 8) != 0, x[8:80], x[0:72])
            e[0:64] = jnp.where((shift & 4) != 0, m[4:68], m[0:64])
            m[0:62] = jnp.where((shift & 2) != 0, e[2:64], e[0:62])
            e[0:61] = jnp.where((shift & 1) != 0, m[1:62], m[0:61])
            total = weights[0] * e[5 : 5 + BINS]
            for tap in range(1, TAPS):
                total = total + weights[tap] * e[5 + tap : 5 + tap + BINS]
            moved.append(total)
        return jnp.concatenate(cmul(moved[0], moved[1], a_ref[0, k1], a_ref[1, k1]), axis=1)

    def result_copy(step):
        some = pl.ds(group * step, group)
        return pltpu.make_async_copy(f_ref.at[:, some], out_hbm.at[:, some], out_sem.at[step])

    def per_group(step, _):
        ks = [group * step + k for k in range(group)]
        s = times_right(jnp.concatenate([migrate(k1, k) for k, k1 in enumerate(ks)], axis=0), az_back[...])
        for k, k1 in enumerate(ks):
            rows = slice(BINS * k, BINS * (k + 1))
            f_ref[0, k1], f_ref[1, k1] = cmul(
                s[rows, :LANES], s[rows, LANES:], az_twist[0, pl.ds(k1, 1), :], az_twist[1, pl.ds(k1, 1), :]
            )
        result_copy(step).start()
        return 0

    lax.fori_loop(0, 16 // group, per_group, 0)

    def sent_core(row, _):
        core_copy(row).wait_send()
        return 0

    lax.fori_loop(0, 4, sent_core, 0)
    for step in range(16 // group):
        result_copy(step).wait()


def finish_kernel(f_hbm, out_hbm, f_ref, out_ref, in_sem, out_sem):
    def fetch(step):
        rows = slice(8 * step, 8 * (step + 1))
        return pltpu.make_async_copy(f_hbm.at[:, :, rows], f_ref.at[:, :, rows], in_sem.at[step])

    def store(step):
        rows = slice(8 * step, 8 * (step + 1))
        return pltpu.make_async_copy(out_ref.at[:, rows], out_hbm.at[:, rows], out_sem.at[step])

    for step in range(BINS // 8):
        fetch(step).start()
    for step in range(BINS // 8):
        rows = slice(8 * step, 8 * (step + 1))
        fetch(step).wait()
        got = fft_list([(f_ref[0, k1, rows, :], f_ref[1, k1, rows, :]) for k1 in range(16)], 1)
        for tile in range(16):
            for c in range(2):
                out_ref[c, rows, LANES * tile : LANES * (tile + 1)] = got[tile][c]
        store(step).start()
    for step in range(BINS // 8):
        store(step).wait()


IN_HBM = pl.BlockSpec(memory_space=pltpu.HBM)
DMA = pltpu.SemaphoreType.DMA


def shards(raw, range_filter, azimuth_filter, shifts, frac_index, kernel_table):
    order = filter_order()
    tables = [
        table_first(),
        table_last(),
        table_twist(),
        right_factor(table_columns(np.arange(LANES), order, -1)),
        right_factor(table_columns(order, np.arange(LANES), 1)),
        table_planes(),
        table_azimuth(),
        table_back(),
        table_back_twist(),
    ]
    operands = [
        raw.reshape(2, 2, 8, 48, LANES).transpose(0, 1, 3, 2, 4).reshape(2, 2, 384, LANES),
        range_filter.reshape(2, ROWS, LANES).transpose(1, 0, 2).reshape(2 * ROWS, LANES),
        azimuth_filter,
        shifts.reshape(16, LANES),
        frac_index.reshape(16, LANES),
        kernel_table.T,
    ]

    def like(array, shape=None):
        return pltpu.VMEM(array.shape if shape is None else shape, array.dtype)

    loads = [like(a) for a in operands[1:5]] + [pltpu.SMEM(operands[5].shape, F32)]
    loads += [like(a) for a in tables]
    loads[5 + 5] = like(tables[5], tables[5].shape[1:])
    scratch = [
        pltpu.VMEM((2, 2, 384, LANES), F32),
        pltpu.VMEM((LANE_PULSES, 2, 48, LANES), F32),
        pltpu.VMEM((LANE_PULSES, 2, 48, LANES), F32),
        pltpu.VMEM((LANE_PULSES, 2, 48, LANES), F32),
        pltpu.VMEM((LANE_PULSES, 2, ROWS, LANES), F32),
        pltpu.VMEM((2, ROWS, LANES), F32),
        pltpu.VMEM((LANE_PULSES, 6 * ROWS, LANES), BF16),
        *[pltpu.VMEM((PLANES, rows, LANES), F32) for rows in BLOCKS],
        *[pltpu.VMEM((PLANES * rows, LANES), F32) for rows in BLOCKS],
        pltpu.VMEM((CHUNKS, CHUNK, LANES), F32),
        pltpu.VMEM((CHIPS, PAIR, LANES), F32),
        pltpu.VMEM((CHIPS, WINDOW, LANES), F32),
        pltpu.VMEM((16, LANES), jnp.int32),
        pltpu.VMEM((TAPS, 16, LANES), F32),
        pltpu.VMEM((2, 16, BINS, LANES), F32),
        pltpu.VMEM((16, WINDOW, LANES), F32),
        pltpu.VMEM((16, 2, WINDOW, LANES), F32),
        pltpu.VMEM((4, 2, WINDOW, LANES), F32),
        pltpu.VMEM((4, 2, WINDOW, LANES), F32),
        pltpu.VMEM((2, 16, BINS, LANES), F32),
        DMA((2,)), DMA((4, 3)), DMA((4, 3)),
        DMA((len(BLOCKS),)), DMA((len(BLOCKS),)),
        DMA((CHUNKS, 4)), DMA((4,)), DMA((CHUNKS, 2)), DMA((4,)), DMA((4,)), DMA((4,)), DMA((4,)),
    ]
    turned = pl.pallas_call(
        kernel,
        out_shape=jax.ShapeDtypeStruct((2, 16, BINS, LANES), F32),
        in_specs=[IN_HBM] * (len(operands) + len(tables)),
        out_specs=IN_HBM,
        scratch_shapes=loads + [DMA((len(loads),))] + scratch,
        compiler_params=pltpu.CompilerParams(
            vmem_limit_bytes=60 * 2**20, collective_id=0, has_side_effects=True
        ),
    )(*operands, *tables)
    return pl.pallas_call(
        finish_kernel,
        out_shape=jax.ShapeDtypeStruct((2, BINS, PULSES), F32),
        in_specs=[IN_HBM],
        out_specs=IN_HBM,
        scratch_shapes=[
            pltpu.VMEM((2, 16, BINS, LANES), F32),
            pltpu.VMEM((2, BINS, PULSES), F32),
            DMA((BINS // 8,)),
            DMA((BINS // 8,)),
        ],
        compiler_params=pltpu.CompilerParams(vmem_limit_bytes=60 * 2**20),
    )(turned)


def solution(mesh):
    in_specs = (P(None, "pulse", "rng"), P(), P(None, ("pulse", "rng"), None), P(), P(), P())
    out_specs = P(None, ("pulse", "rng"), None)
    return jax.shard_map(shards, mesh=mesh, in_specs=in_specs, out_specs=out_specs, check_vma=False)
```

```python
import functools
import math

import jax
import jax.numpy as jnp
import ml_dtypes
import numpy as np
from jax import lax
from jax.experimental import pallas as pl
from jax.experimental.pallas import tpu as pltpu
from jax.sharding import PartitionSpec as P

MESH = pl.DeviceIdType.MESH
F32 = jnp.float32
BF16 = jnp.bfloat16

PULSES = 2048
SAMPLES = 24576
ROWS = 192
LANES = 128
PLANES = 16
PEERS = 32
CHIPS = 16
LANE_PULSES = 4
BINS = 48
CHUNKS = 4
CHUNK_ROWS = 3
CHUNK = CHUNK_ROWS * LANES
BLOCKS = (24, 24, 16, 16, 8, 8)
BELOW = 8
ABOVE = 24
WINDOW = BELOW + BINS + ABOVE
PAIR = BELOW + 2 * BINS + ABOVE
TAPS = 8
ORDER = ((2, 1, 3, 0), (2, 3, 1, 0))


def turn(product, period, sign):
    angle = sign * 2.0 * math.pi * (product % period) / period
    return np.cos(angle), np.sin(angle)


def halves(table):
    high = table.astype(ml_dtypes.bfloat16)
    low = (table - high.astype(np.float64)).astype(ml_dtypes.bfloat16)
    return high, low


def left_factor(table):
    high, low = halves(table)
    return np.concatenate([high, high, low], axis=1)


def right_factor(table):
    high, low = halves(table)
    return np.concatenate([high, high, low], axis=-2)


def lane_bins():
    lanes = np.arange(LANES)
    return 8 * (lanes % 16) + lanes // 16


def table_first():
    ids = np.arange(ROWS)
    re, im = turn(np.outer(ids, ids), ROWS, -1)
    return left_factor(np.block([[re, -im], [im, re]]))


def table_last():
    ids = np.arange(ROWS)
    re, im = turn(np.outer(ids, ids), ROWS, 1)
    full = np.stack([np.concatenate([re, -im], axis=1), np.concatenate([im, re], axis=1)]) / SAMPLES
    full = full.reshape(2, PLANES, CHUNKS, CHUNK_ROWS, 2 * ROWS).transpose(2, 1, 0, 3, 4)
    return left_factor(full.reshape(2 * ROWS, 2 * ROWS)).reshape(CHUNKS, 2 * ROWS // CHUNKS, -1)


def filter_order():
    lanes = np.arange(LANES)
    return 2 * (lanes % 64) + lanes // 64


def table_columns(rows, cols, sign, scale=1.0):
    re, im = turn(np.outer(rows, cols), LANES, sign)
    return np.block([[re, im], [-im, re]]) * scale


def table_twist():
    re, im = turn(np.outer(np.arange(ROWS), np.arange(LANES)), SAMPLES, -1)
    return np.stack([re, im]).astype(np.float32)


def table_planes():
    place = np.arange(PEERS)[:, None, None, None]
    r = np.arange(LANE_PULSES)[None, :, None, None]
    z = np.arange(PLANES)[None, None, :, None]
    k1 = np.arange(16)[None, None, None, :]
    re, im = turn((128 * z + 4 * place + r) * k1, PULSES, -1)
    full = np.zeros((PEERS, 2, LANE_PULSES, PLANES, 16, 2, LANE_PULSES))
    for q in range(LANE_PULSES):
        full[:, 0, q, :, :, 0, q] = re[:, q]
        full[:, 1, q, :, :, 0, q] = -im[:, q]
        full[:, 0, q, :, :, 1, q] = im[:, q]
        full[:, 1, q, :, :, 1, q] = re[:, q]
    return right_factor(full.reshape(PEERS, 128, 128))


def table_azimuth():
    place = np.arange(PEERS)[:, None, None]
    r = np.arange(LANE_PULSES)[None, :, None]
    re, im = turn((4 * place + r) * lane_bins()[None, None, :], LANES, -1)
    full = np.zeros((PEERS, 2, LANE_PULSES, 2, LANES))
    full[:, 0, :, 0] = re
    full[:, 1, :, 0] = -im
    full[:, 0, :, 1] = im
    full[:, 1, :, 1] = re
    by_core = full.reshape(CHIPS, 2, 8, 2 * LANES).transpose(1, 0, 2, 3)
    return right_factor(by_core.reshape(2, LANES, 2 * LANES))


def table_back():
    return right_factor(table_columns(lane_bins(), np.arange(LANES), 1, 1.0 / PULSES))


def table_back_twist():
    re, im = turn(np.outer(np.arange(16), np.arange(LANES)), PULSES, 1)
    return np.stack([re, im]).astype(np.float32)


def split(values):
    high = values.astype(BF16)
    low = (values - high.astype(F32)).astype(BF16)
    return high, low


def times_left(table, values):
    high, low = split(values)
    return jnp.dot(table, jnp.concatenate([high, low, high], axis=0), preferred_element_type=F32)


def times_right(values, table):
    high, low = split(values)
    return jnp.dot(jnp.concatenate([high, low, high], axis=1), table, preferred_element_type=F32)


def cmul(a_re, a_im, b_re, b_im):
    return a_re * b_re - a_im * b_im, a_re * b_im + a_im * b_re


def fft_list(values, sign):
    count = len(values)
    if count == 1:
        return values
    even = fft_list(values[0::2], sign)
    odd = fft_list(values[1::2], sign)
    low, high = [], []
    for k in range(count // 2):
        re, im = odd[k]
        if 4 * k == count:
            re, im = (-im, re) if sign > 0 else (im, -re)
        elif k:
            w_re = math.cos(2.0 * math.pi * k / count)
            w_im = sign * math.sin(2.0 * math.pi * k / count)
            re, im = re * w_re - im * w_im, re * w_im + im * w_re
        low.append((even[k][0] + re, even[k][1] + im))
        high.append((even[k][0] - re, even[k][1] - im))
    return low + high


def swap_blocks(arrays, width):
    arrays = list(arrays)
    lane = lax.broadcasted_iota(jnp.int32, arrays[0].shape, 1)
    for bit in (1, 2, 4, 8):
        keep = (lane // width) & bit == 0
        for a in range(16):
            if a & bit:
                continue
            first, second = arrays[a], arrays[a + bit]
            arrays[a] = jnp.where(keep, first, pltpu.roll(second, bit * width, 1))
            arrays[a + bit] = jnp.where(keep, pltpu.roll(first, LANES - bit * width, 1), second)
    return arrays


def kernel(
    raw_hbm, filt_hbm, azf_hbm, shift_hbm, frac_hbm, ktab_hbm,
    first_hbm, last_hbm, twist_hbm, fwd_hbm, back_hbm, planes_hbm, az_fwd_hbm, az_back_hbm, az_twist_hbm,
    out_hbm,
    filt_in, azf_in, shift_in, frac_in, ktab, first, last, twist, fwd, back, planes, az_fwd, az_back, az_twist,
    load_sem,
    tiles, to_like, to_cross, to_core, x_ref, filt, v_ref, y0, y1, y2, y3, y4, y5, z0, z1, z2, z3, z4, z5, t_ref, g_ref, o_ref,
    shift_ref, w_ref, a_ref, h_ref, d_ref, m_ref, e_ref, f_ref,
    tile_sem, x_send, x_recv, z_send, z_recv,
    p_send, p_recv, h_send, h_recv, fwd_send, fwd_recv, out_sem,
):
    pulse = lax.axis_index("pulse")
    lane = lax.axis_index("rng")
    z = lax.div(pulse, 8)
    y = lax.rem(lax.div(pulse, 2), 4)
    xh = lax.div(lane, 2)
    core = lax.rem(lane, 2)
    q_me = 2 * lax.rem(pulse, 2) + xh
    chip = 4 * y + q_me
    has_below = z > 0
    has_above = z < PLANES - 1

    def device(plane, other_chip, other_core):
        return (8 * plane + lax.div(other_chip, 2), 2 * lax.rem(other_chip, 2) + other_core)

    x_partner = (pulse, 2 * (1 - xh) + core)
    x_cross = (pulse, 2 * (1 - xh) + 1 - core)
    core_partner = (pulse, 2 * xh + 1 - core)

    place = 2 * chip + core
    loads = [
        (filt_hbm, filt_in), (first_hbm, first), (twist_hbm, twist), (fwd_hbm, fwd), (back_hbm, back),
        (last_hbm, last), (planes_hbm.at[place], planes), (azf_hbm, azf_in), (shift_hbm, shift_in),
        (frac_hbm, frac_in), (ktab_hbm, ktab), (az_fwd_hbm, az_fwd), (az_back_hbm, az_back),
        (az_twist_hbm, az_twist),
    ]
    loads = [pltpu.make_async_copy(src, dst, load_sem.at[k]) for k, (src, dst) in enumerate(loads)]
    tile_loads = [
        pltpu.make_async_copy(raw_hbm.at[:, 1 - xh], tiles.at[1], tile_sem.at[1]),
        pltpu.make_async_copy(raw_hbm.at[:, xh], tiles.at[0], tile_sem.at[0]),
    ]
    for load in tile_loads:
        load.start()

    barrier = pltpu.get_barrier_semaphore()

    def greet(to):
        pl.semaphore_signal(barrier, inc=1, device_id=to, device_id_type=MESH)

    greet(x_partner)
    greet(x_cross)
    greet(core_partner)

    def greet_z(off, _):
        greet(device(lax.rem(z + off, PLANES), chip, core))
        return 0

    def greet_plane(off, _):
        greet(device(z, lax.rem(chip + off, CHIPS), core))
        return 0

    def greet_all(plane):
        def body(other, _):
            greet(device(plane, other, core))
            return 0

        lax.fori_loop(0, CHIPS, body, 0)

    lax.fori_loop(1, PLANES, greet_z, 0)
    lax.fori_loop(1, CHIPS, greet_plane, 0)
    pl.when(jnp.logical_and(chip == 0, has_below))(lambda: greet_all(z - 1))
    pl.when(jnp.logical_and(chip == CHIPS - 1, has_above))(lambda: greet_all(z + 1))

    for load in loads:
        load.start()

    def blank(start, size):
        def body(other, _):
            g_ref[other, start : start + size, :] = jnp.zeros((size, LANES), F32)
            return 0

        lax.fori_loop(0, CHIPS, body, 0)

    pl.when(jnp.logical_and(chip == 0, z == 0))(lambda: blank(0, BELOW))
    pl.when(jnp.logical_and(chip == CHIPS - 1, z == PLANES - 1))(lambda: blank(PAIR - ABOVE, ABOVE))

    my_quarter = 2 * xh + core

    def quarter_rows(quarter):
        return pl.ds(pl.multiple_of(48 * quarter, 8), 48)

    for load in tile_loads:
        load.wait()
    def sort_pulse(r):
        like = pl.ds(4 * core + r, 48, stride=8)
        other = pl.ds(4 * (1 - core) + r, 48, stride=8)
        for c in range(2):
            to_like[r, c] = tiles[1, c, like, :]
            to_cross[r, c] = tiles[1, c, other, :]
            to_core[r, c] = tiles[0, c, other, :]
            x_ref[r, c, quarter_rows(my_quarter), :] = tiles[0, c, like, :]

    sort_pulse(0)
    pl.semaphore_wait(
        barrier,
        3 + PLANES - 1 + CHIPS - 1 + jnp.where(has_below, 1, 0) + jnp.where(has_above, 1, 0),
    )

    def pulse_copy(r, which):
        return pltpu.make_async_remote_copy(
            src_ref=(to_like, to_cross, to_core)[which].at[r],
            dst_ref=x_ref.at[r, :, quarter_rows(my_quarter)],
            send_sem=x_send.at[r, which],
            recv_sem=x_recv.at[r, which],
            device_id=(x_partner, x_cross, core_partner)[which],
            device_id_type=MESH,
        )

    def send_pulse(r):
        for which in range(3):
            pulse_copy(r, which).start()

    send_pulse(0)
    for r in range(1, LANE_PULSES):
        sort_pulse(r)

    for load in loads:
        load.wait()
    for c in range(2):
        cols = [filt_in[pl.ds(2 * u + c, 64, stride=6), :].T for u in range(3)]
        tall = jnp.concatenate(cols, axis=0)
        filt[c] = jnp.concatenate([tall[:ROWS], tall[ROWS:]], axis=1)

    def wait_pulse(r):
        for which in range(3):
            pulse_copy(r, which).wait_recv()

    def compress(r):
        twist_re, twist_im = twist[0], twist[1]
        v = times_left(first[...], jnp.concatenate([x_ref[r, 0], x_ref[r, 1]], axis=0))
        re, im = cmul(v[:ROWS], v[ROWS:], twist_re, twist_im)
        s = times_right(jnp.concatenate([re, im], axis=1), fwd[...])
        re, im = cmul(s[:, :LANES], s[:, LANES:], filt[0], filt[1])
        s = times_right(jnp.concatenate([re, im], axis=1), back[...])
        re, im = cmul(s[:, :LANES], s[:, LANES:], twist_re, -twist_im)
        high, low = split(jnp.concatenate([re, im], axis=0))
        v_ref[r, 0 : 2 * ROWS] = high
        v_ref[r, 2 * ROWS : 4 * ROWS] = low
        v_ref[r, 4 * ROWS : 6 * ROWS] = high

    ys, zs = (y0, y1, y2, y3, y4, y5), (z0, z1, z2, z3, z4, z5)

    def chunk_of(t):
        if t in (0, 3):
            return lax.rem(y + (2 if t == 0 else 0), CHUNKS)
        return lax.rem(y + jnp.where(core == t - 1, 1, 3), CHUNKS)

    def z_mine_rows(block):
        return pl.ds(pl.multiple_of(BLOCKS[block] * z, 8), BLOCKS[block])

    def z_copy(block, off):
        to = lax.rem(z + off, PLANES)
        return pltpu.make_async_remote_copy(
            src_ref=ys[block].at[to],
            dst_ref=zs[block].at[z_mine_rows(block)],
            send_sem=z_send.at[block],
            recv_sem=z_recv.at[block],
            device_id=device(to, chip, core),
            device_id_type=MESH,
        )

    def z_mine(block):
        return pltpu.make_async_copy(ys[block].at[z], zs[block].at[z_mine_rows(block)], z_recv.at[block])

    def send_block(block):
        def start(step, _):
            near = PLANES // 2 - step
            z_copy(block, near).start()
            z_copy(block, PLANES - near).start()
            return 0

        z_copy(block, PLANES // 2).start()
        lax.fori_loop(1, PLANES // 2, start, 0)
        z_mine(block).start()

    def wait_for(ref, sem):
        pltpu.make_async_copy(ref, ref, sem).wait()

    def sent_block(block):
        wait_for(ys[block].at[pl.ds(0, PLANES - 1)], z_send.at[block])

    size = 2 * CHUNK_ROWS

    def place_of(t, r, c, row):
        rows = {0: (0, 1, 2), 1: (0,) if row == 0 else (1, 2), 2: (0, 1) if row < 2 else (2,)}
        rows[3] = rows[1]
        rows = rows[t]
        block, start = {(0, 0): (2, 0), (1, 0): (2, 12), (1, 1): (3, 0), (2, 0): (3, 8), (2, 2): (4, 0), (3, 0): (4, 4), (3, 1): (5, 0)}[
            t, rows[0]
        ]
        return block, start + len(rows) * (2 * (r - 2) + c) + row - rows[0]

    for r in range(2):
        wait_pulse(r)
        send_pulse(r + 1)
        compress(r)
        for chunk in range(CHUNKS):
            out = jnp.dot(last[chunk], v_ref[r], preferred_element_type=F32)
            for to in range(PLANES):
                ys[r][to, size * chunk : size * (chunk + 1), :] = out[size * to : size * (to + 1)]
        send_block(r)

    def later_pulse(r, _):
        wait_pulse(r)
        pl.when(r < LANE_PULSES - 1)(lambda: send_pulse(r + 1))
        compress(r)
        return 0

    lax.fori_loop(2, 4, later_pulse, 0)
    both = jnp.concatenate([v_ref[2], v_ref[3]], axis=1)

    def make_chunk(t):
        out = jnp.dot(last[chunk_of(t)], both, preferred_element_type=F32)
        for r in (2, 3):
            lanes = slice(LANES * (r - 2), LANES * (r - 1))
            pieces = [(0, 6)] if t == 0 else [(0, 2), (2, 3), (3, 5), (5, 6)]
            if t in (1, 3):
                pieces = [(0, 1), (1, 3), (3, 4), (4, 6)]
            for first_row, end in pieces:
                block, place = place_of(t, r, first_row // 3, first_row % 3)
                for to in range(PLANES):
                    ys[block][to, place : place + end - first_row, :] = out[
                        size * to + first_row : size * to + end, lanes
                    ]

    for t in range(2):
        make_chunk(t)
    sent_block(0)
    send_block(2)
    for t in (2, 3):
        make_chunk(t)

    def turn_filter(step, _):
        rows = pl.ds(pl.multiple_of(8 * step, 8), 8)
        for c in range(2):
            got = swap_blocks([azf_in[c, rows, LANES * k : LANES * (k + 1)] for k in range(16)], 1)
            for k1 in range(16):
                a_ref[c, k1, rows, :] = got[k1]
        return 0

    lax.fori_loop(0, BINS // 8, turn_filter, 0)

    def by_bin(values):
        tall = values.T
        return jnp.concatenate([tall[16 * u : 16 * (u + 1)] for u in range(8)], axis=1)

    shift_ref[...] = by_bin(shift_in[...])
    frac = by_bin(frac_in[...])
    for tap in range(TAPS):
        weight = jnp.zeros(frac.shape, F32)
        for row in range(16):
            weight = jnp.where(frac == row, ktab[tap, row], weight)
        w_ref[tap] = weight

    for r in range(LANE_PULSES):
        for which in range(3):
            pulse_copy(r, which).wait_send()

    sent_block(1)
    send_block(3)
    sent_block(2)
    send_block(4)

    def window(q):
        if q == 0:
            return 0, BELOW, PAIR - BELOW
        if q == 3:
            return CHUNK - BELOW - 2 * BINS, 0, PAIR - ABOVE
        return 2 * BINS * q - BELOW, 0, PAIR

    def main_copy(t, q):
        src, dst, size = window(q)
        return pltpu.make_async_remote_copy(
            src_ref=t_ref.at[t, pl.ds(src, size)],
            dst_ref=g_ref.at[chip, pl.ds(dst, size)],
            send_sem=p_send.at[t, q],
            recv_sem=p_recv.at[y],
            device_id=device(z, 4 * chunk_of(t) + q, core),
            device_id_type=MESH,
        )

    def main_own(q):
        src, dst, size = window(q)
        return pltpu.make_async_copy(
            t_ref.at[CHUNKS - 1, pl.ds(src, size)], g_ref.at[chip, pl.ds(dst, size)], p_recv.at[y]
        )

    def each_main(t, qs, act, local):
        for q in qs:
            if t < CHUNKS - 1:
                act(main_copy(t, q))
            else:
                pl.when(q_me != q)(functools.partial(lambda q: act(main_copy(t, q)), q))
                if local:
                    pl.when(q_me == q)(functools.partial(lambda q: local(main_own(q)), q))

    def on_window(act):
        for q in range(4):
            pl.when(q_me == q)(functools.partial(lambda q: act(*window(q)), q))

    def halo_targets(chunk):
        down_chip = lax.rem(4 * chunk + CHIPS - 1, CHIPS)
        up_chip = lax.rem(4 * chunk + 4, CHIPS)
        down_plane = jnp.where(chunk == 0, z - 1, z)
        up_plane = jnp.where(chunk == CHUNKS - 1, z + 1, z)
        return down_plane, down_chip, up_plane, up_chip

    DOWN = (0, PAIR - ABOVE, ABOVE)
    UP = (CHUNK - BELOW, 0, BELOW)

    def halo_copy(t, which, plane, to):
        src, dst, size = (DOWN, UP)[which]
        return pltpu.make_async_remote_copy(
            src_ref=t_ref.at[t, pl.ds(src, size)],
            dst_ref=g_ref.at[chip, pl.ds(dst, size)],
            send_sem=h_send.at[t, which],
            recv_sem=h_recv.at[y],
            device_id=device(plane, to, core),
            device_id_type=MESH,
        )

    def halo_mine(t, which):
        src, dst, size = (DOWN, UP)[which]
        return pltpu.make_async_copy(
            t_ref.at[t, pl.ds(src, size)], g_ref.at[chip, pl.ds(dst, size)], h_recv.at[y]
        )

    def each_halo(t, whichs, act, local):
        down_plane, down_chip, up_plane, up_chip = halo_targets(chunk_of(t))
        for which, plane, to in ((0, down_plane, down_chip), (1, up_plane, up_chip)):
            if which not in whichs:
                continue
            inside = jnp.logical_and(plane >= 0, plane < PLANES)
            me = jnp.logical_and(plane == z, to == chip)
            pl.when(jnp.logical_and(inside, jnp.logical_not(me)))(
                functools.partial(lambda *a: act(halo_copy(*a)), t, which, plane, to)
            )
            if local:
                pl.when(me)(functools.partial(lambda *a: local(halo_mine(*a)), t, which))

    def wait_block(block):
        wait_for(zs[block], z_recv.at[block])

    def start(copy):
        copy.start()

    def sent_chunk(t):
        each_main(t, range(4), lambda copy: copy.wait_send(), None)
        each_halo(t, (0, 1), lambda copy: copy.wait_send(), None)

    def turn_chunk(t, rows):
        chunk = chunk_of(t)
        for row in rows:
            parts = []
            for c in range(2):
                for r in range(2):
                    place = size * chunk + CHUNK_ROWS * c + row
                    parts.append(zs[r][pl.ds(place, PLANES, stride=BLOCKS[r]), :])
                for r in (2, 3):
                    block, place = place_of(t, r, c, row)
                    parts.append(zs[block][pl.ds(place, PLANES, stride=BLOCKS[block]), :])
            t_ref[t, LANES * row : LANES * (row + 1), :] = times_right(
                jnp.concatenate(parts, axis=0).T, planes[...]
            )

    for block in range(3):
        wait_block(block)
    turn_chunk(0, range(CHUNK_ROWS))
    each_main(0, range(4), start, start)
    each_halo(0, (0, 1), start, start)
    wait_block(3)
    sent_block(3)
    send_block(5)
    turn_chunk(1, range(CHUNK_ROWS))
    each_main(1, range(4), start, start)
    each_halo(1, (0, 1), start, start)
    turn_chunk(2, range(2))
    each_main(2, (0, 1), start, start)
    each_halo(2, (0,), start, start)
    sent_chunk(0)
    wait_block(4)
    turn_chunk(2, (2,))
    each_main(2, (2, 3), start, start)
    each_halo(2, (1,), start, start)
    turn_chunk(3, (0,))
    each_main(3, (0,), start, start)
    each_halo(3, (0,), start, start)
    wait_block(5)
    turn_chunk(3, (1, 2))
    each_main(3, (1, 2, 3), start, start)
    each_halo(3, (1,), start, start)

    def core_copy(row):
        return pltpu.make_async_remote_copy(
            src_ref=g_ref.at[pl.ds(4 * row, 4), pl.ds(pl.multiple_of(BINS * (1 - core), 8), WINDOW)],
            dst_ref=o_ref.at[pl.ds(4 * row, 4)],
            send_sem=fwd_send.at[row],
            recv_sem=fwd_recv.at[row],
            device_id=core_partner,
            device_id_type=MESH,
        )

    takes_up = jnp.logical_and(q_me == 0, jnp.logical_or(y > 0, has_below))
    takes_down = jnp.logical_and(q_me == 3, jnp.logical_or(y < 3, has_above))

    def gather(t):
        row = lax.rem(2 * y + CHUNKS - chunk_of(t), CHUNKS)

        def rows_of(first_row, count):
            return g_ref.at[pl.ds(4 * row, 4), pl.ds(first_row, count)]

        on_window(lambda src, dst, count: wait_for(rows_of(dst, count), p_recv.at[row]))
        pl.when(takes_up)(lambda: wait_for(rows_of(0, BELOW), h_recv.at[row]))
        pl.when(takes_down)(lambda: wait_for(rows_of(PAIR - ABOVE, ABOVE), h_recv.at[row]))
        core_copy(row).start()

    for t in range(CHUNKS):
        gather(t)

    part = WINDOW // 2

    def turn_rows(read):
        def body(step, _):
            rows = pl.ds(pl.multiple_of(part * step, 8), part)
            got = swap_blocks([read(k, part * step) for k in range(CHIPS)], 8)
            for k1 in range(16):
                h_ref[k1, rows, :] = got[k1]
            return 0

        lax.fori_loop(0, WINDOW // part, body, 0)

    group = 4

    def transform(from_core, add):
        def body(step, _):
            high, low = split(h_ref[pl.ds(group * step, group)].reshape(group * WINDOW, LANES))
            d = jnp.dot(
                jnp.concatenate([high, low, high], axis=1), az_fwd[from_core], preferred_element_type=F32
            )
            for k in range(group):
                for c in range(2):
                    piece = d[WINDOW * k : WINDOW * (k + 1), LANES * c : LANES * (c + 1)]
                    if add:
                        piece = piece + d_ref[group * step + k, c]
                    d_ref[group * step + k, c] = piece
            return 0

        lax.fori_loop(0, 16 // group, body, 0)

    turn_rows(lambda k, start: g_ref[k, pl.ds(pl.multiple_of(BINS * core + start, 8), part), :])
    transform(core, False)

    def wait_core(row, _):
        core_copy(row).wait_recv()
        return 0

    for t in (1, 2, 3):
        sent_chunk(t)
    sent_block(4)
    sent_block(5)
    lax.fori_loop(0, 4, wait_core, 0)
    turn_rows(lambda k, start: o_ref[k, pl.ds(pl.multiple_of(start, 8), part), :])
    transform(1 - core, True)

    def migrate(k1, slot):
        shift = shift_ref[pl.ds(k1, 1), :]
        weights = [w_ref[tap, pl.ds(k1, 1), :] for tap in range(TAPS)]
        moved = []
        for c in range(2):
            x = d_ref[k1, c]
            near = jnp.where((shift & 16) != 0, x[16:80], x[0:64])
            x = jnp.concatenate([near, x[64:80]], axis=0)
            m, e = m_ref.at[slot, c], e_ref.at[slot, c]
            m[0:72] = jnp.where((shift & 8) != 0, x[8:80], x[0:72])
            e[0:64] = jnp.where((shift & 4) != 0, m[4:68], m[0:64])
            m[0:62] = jnp.where((shift & 2) != 0, e[2:64], e[0:62])
            e[0:61] = jnp.where((shift & 1) != 0, m[1:62], m[0:61])
            total = weights[0] * e[5 : 5 + BINS]
            for tap in range(1, TAPS):
                total = total + weights[tap] * e[5 + tap : 5 + tap + BINS]
            moved.append(total)
        return jnp.concatenate(cmul(moved[0], moved[1], a_ref[0, k1], a_ref[1, k1]), axis=1)

    def result_copy(step):
        some = pl.ds(group * step, group)
        return pltpu.make_async_copy(f_ref.at[:, some], out_hbm.at[:, some], out_sem.at[step])

    def per_group(step, _):
        ks = [group * step + k for k in range(group)]
        s = times_right(jnp.concatenate([migrate(k1, k) for k, k1 in enumerate(ks)], axis=0), az_back[...])
        for k, k1 in enumerate(ks):
            rows = slice(BINS * k, BINS * (k + 1))
            f_ref[0, k1], f_ref[1, k1] = cmul(
                s[rows, :LANES], s[rows, LANES:], az_twist[0, pl.ds(k1, 1), :], az_twist[1, pl.ds(k1, 1), :]
            )
        result_copy(step).start()
        return 0

    lax.fori_loop(0, 16 // group, per_group, 0)

    def sent_core(row, _):
        core_copy(row).wait_send()
        return 0

    lax.fori_loop(0, 4, sent_core, 0)
    for step in range(16 // group):
        result_copy(step).wait()


def finish_kernel(f_hbm, out_hbm, f_ref, out_ref, in_sem, out_sem):
    def fetch(step):
        rows = slice(8 * step, 8 * (step + 1))
        return pltpu.make_async_copy(f_hbm.at[:, :, rows], f_ref.at[:, :, rows], in_sem.at[step])

    def store(step):
        rows = slice(8 * step, 8 * (step + 1))
        return pltpu.make_async_copy(out_ref.at[:, rows], out_hbm.at[:, rows], out_sem.at[step])

    for step in range(BINS // 8):
        fetch(step).start()
    for step in range(BINS // 8):
        rows = slice(8 * step, 8 * (step + 1))
        fetch(step).wait()
        got = fft_list([(f_ref[0, k1, rows, :], f_ref[1, k1, rows, :]) for k1 in range(16)], 1)
        for tile in range(16):
            for c in range(2):
                out_ref[c, rows, LANES * tile : LANES * (tile + 1)] = got[tile][c]
        store(step).start()
    for step in range(BINS // 8):
        store(step).wait()


IN_HBM = pl.BlockSpec(memory_space=pltpu.HBM)
DMA = pltpu.SemaphoreType.DMA


def shards(raw, range_filter, azimuth_filter, shifts, frac_index, kernel_table):
    order = filter_order()
    tables = [
        table_first(),
        table_last(),
        table_twist(),
        right_factor(table_columns(np.arange(LANES), order, -1)),
        right_factor(table_columns(order, np.arange(LANES), 1)),
        table_planes(),
        table_azimuth(),
        table_back(),
        table_back_twist(),
    ]
    operands = [
        raw.reshape(2, 2, 8, 48, LANES).transpose(0, 1, 3, 2, 4).reshape(2, 2, 384, LANES),
        range_filter.reshape(2, ROWS, LANES).transpose(1, 0, 2).reshape(2 * ROWS, LANES),
        azimuth_filter,
        shifts.reshape(16, LANES),
        frac_index.reshape(16, LANES),
        kernel_table.T,
    ]

    def like(array, shape=None):
        return pltpu.VMEM(array.shape if shape is None else shape, array.dtype)

    loads = [like(a) for a in operands[1:5]] + [pltpu.SMEM(operands[5].shape, F32)]
    loads += [like(a) for a in tables]
    loads[5 + 5] = like(tables[5], tables[5].shape[1:])
    scratch = [
        pltpu.VMEM((2, 2, 384, LANES), F32),
        pltpu.VMEM((LANE_PULSES, 2, 48, LANES), F32),
        pltpu.VMEM((LANE_PULSES, 2, 48, LANES), F32),
        pltpu.VMEM((LANE_PULSES, 2, 48, LANES), F32),
        pltpu.VMEM((LANE_PULSES, 2, ROWS, LANES), F32),
        pltpu.VMEM((2, ROWS, LANES), F32),
        pltpu.VMEM((LANE_PULSES, 6 * ROWS, LANES), BF16),
        *[pltpu.VMEM((PLANES, rows, LANES), F32) for rows in BLOCKS],
        *[pltpu.VMEM((PLANES * rows, LANES), F32) for rows in BLOCKS],
        pltpu.VMEM((CHUNKS, CHUNK, LANES), F32),
        pltpu.VMEM((CHIPS, PAIR, LANES), F32),
        pltpu.VMEM((CHIPS, WINDOW, LANES), F32),
        pltpu.VMEM((16, LANES), jnp.int32),
        pltpu.VMEM((TAPS, 16, LANES), F32),
        pltpu.VMEM((2, 16, BINS, LANES), F32),
        pltpu.VMEM((16, WINDOW, LANES), F32),
        pltpu.VMEM((16, 2, WINDOW, LANES), F32),
        pltpu.VMEM((4, 2, WINDOW, LANES), F32),
        pltpu.VMEM((4, 2, WINDOW, LANES), F32),
        pltpu.VMEM((2, 16, BINS, LANES), F32),
        DMA((2,)), DMA((4, 3)), DMA((4, 3)),
        DMA((len(BLOCKS),)), DMA((len(BLOCKS),)),
        DMA((CHUNKS, 4)), DMA((4,)), DMA((CHUNKS, 2)), DMA((4,)), DMA((4,)), DMA((4,)), DMA((4,)),
    ]
    turned = pl.pallas_call(
        kernel,
        out_shape=jax.ShapeDtypeStruct((2, 16, BINS, LANES), F32),
        in_specs=[IN_HBM] * (len(operands) + len(tables)),
        out_specs=IN_HBM,
        scratch_shapes=loads + [DMA((len(loads),))] + scratch,
        compiler_params=pltpu.CompilerParams(
            vmem_limit_bytes=60 * 2**20, collective_id=0, has_side_effects=True
        ),
    )(*operands, *tables)
    return pl.pallas_call(
        finish_kernel,
        out_shape=jax.ShapeDtypeStruct((2, BINS, PULSES), F32),
        in_specs=[IN_HBM],
        out_specs=IN_HBM,
        scratch_shapes=[
            pltpu.VMEM((2, 16, BINS, LANES), F32),
            pltpu.VMEM((2, BINS, PULSES), F32),
            DMA((BINS // 8,)),
            DMA((BINS // 8,)),
        ],
        compiler_params=pltpu.CompilerParams(vmem_limit_bytes=60 * 2**20),
    )(turned)


def solution(mesh):
    in_specs = (P(None, "pulse", "rng"), P(), P(None, ("pulse", "rng"), None), P(), P(), P())
    out_specs = P(None, ("pulse", "rng"), None)
    return jax.shard_map(shards, mesh=mesh, in_specs=in_specs, out_specs=out_specs, check_vma=False)
```

```python
import functools
import math

import jax
import jax.numpy as jnp
import ml_dtypes
import numpy as np
from jax import lax
from jax.experimental import pallas as pl
from jax.experimental.pallas import tpu as pltpu
from jax.sharding import PartitionSpec as P

MESH = pl.DeviceIdType.MESH
F32 = jnp.float32
BF16 = jnp.bfloat16

PULSES = 2048
SAMPLES = 24576
ROWS = 192
LANES = 128
PLANES = 16
PEERS = 32
CHIPS = 16
LANE_PULSES = 4
BINS = 48
CHUNKS = 4
CHUNK_ROWS = 3
CHUNK = CHUNK_ROWS * LANES
BLOCKS = (24, 24, 16, 16, 16)
BELOW = 8
ABOVE = 24
WINDOW = BELOW + BINS + ABOVE
PAIR = BELOW + 2 * BINS + ABOVE
TAPS = 8
ORDER = ((2, 1, 3, 0), (2, 3, 1, 0))


def turn(product, period, sign):
    angle = sign * 2.0 * math.pi * (product % period) / period
    return np.cos(angle), np.sin(angle)


def halves(table):
    high = table.astype(ml_dtypes.bfloat16)
    low = (table - high.astype(np.float64)).astype(ml_dtypes.bfloat16)
    return high, low


def left_factor(table):
    high, low = halves(table)
    return np.concatenate([high, high, low], axis=1)


def right_factor(table):
    high, low = halves(table)
    return np.concatenate([high, high, low], axis=-2)


def lane_bins():
    lanes = np.arange(LANES)
    return 8 * (lanes % 16) + lanes // 16


def table_first():
    ids = np.arange(ROWS)
    re, im = turn(np.outer(ids, ids), ROWS, -1)
    return left_factor(np.block([[re, -im], [im, re]]))


def table_last():
    ids = np.arange(ROWS)
    re, im = turn(np.outer(ids, ids), ROWS, 1)
    full = np.stack([np.concatenate([re, -im], axis=1), np.concatenate([im, re], axis=1)]) / SAMPLES
    full = full.reshape(2, PLANES, CHUNKS, CHUNK_ROWS, 2 * ROWS).transpose(2, 1, 0, 3, 4)
    return left_factor(full.reshape(2 * ROWS, 2 * ROWS)).reshape(CHUNKS, 2 * ROWS // CHUNKS, -1)


def filter_order():
    lanes = np.arange(LANES)
    return 2 * (lanes % 64) + lanes // 64


def table_columns(rows, cols, sign, scale=1.0):
    re, im = turn(np.outer(rows, cols), LANES, sign)
    return np.block([[re, im], [-im, re]]) * scale


def table_twist():
    re, im = turn(np.outer(np.arange(ROWS), np.arange(LANES)), SAMPLES, -1)
    return np.stack([re, im]).astype(np.float32)


def table_planes():
    place = np.arange(PEERS)[:, None, None, None]
    r = np.arange(LANE_PULSES)[None, :, None, None]
    z = np.arange(PLANES)[None, None, :, None]
    k1 = np.arange(16)[None, None, None, :]
    re, im = turn((128 * z + 4 * place + r) * k1, PULSES, -1)
    full = np.zeros((PEERS, 2, LANE_PULSES, PLANES, 16, 2, LANE_PULSES))
    for q in range(LANE_PULSES):
        full[:, 0, q, :, :, 0, q] = re[:, q]
        full[:, 1, q, :, :, 0, q] = -im[:, q]
        full[:, 0, q, :, :, 1, q] = im[:, q]
        full[:, 1, q, :, :, 1, q] = re[:, q]
    return right_factor(full.reshape(PEERS, 128, 128))


def table_azimuth():
    place = np.arange(PEERS)[:, None, None]
    r = np.arange(LANE_PULSES)[None, :, None]
    re, im = turn((4 * place + r) * lane_bins()[None, None, :], LANES, -1)
    full = np.zeros((PEERS, 2, LANE_PULSES, 2, LANES))
    full[:, 0, :, 0] = re
    full[:, 1, :, 0] = -im
    full[:, 0, :, 1] = im
    full[:, 1, :, 1] = re
    by_core = full.reshape(CHIPS, 2, 8, 2 * LANES).transpose(1, 0, 2, 3)
    return right_factor(by_core.reshape(2, LANES, 2 * LANES))


def table_back():
    return right_factor(table_columns(lane_bins(), np.arange(LANES), 1, 1.0 / PULSES))


def table_back_twist():
    re, im = turn(np.outer(np.arange(16), np.arange(LANES)), PULSES, 1)
    return np.stack([re, im]).astype(np.float32)


def split(values):
    high = values.astype(BF16)
    low = (values - high.astype(F32)).astype(BF16)
    return high, low


def times_left(table, values):
    high, low = split(values)
    return jnp.dot(table, jnp.concatenate([high, low, high], axis=0), preferred_element_type=F32)


def times_right(values, table):
    high, low = split(values)
    return jnp.dot(jnp.concatenate([high, low, high], axis=1), table, preferred_element_type=F32)


def cmul(a_re, a_im, b_re, b_im):
    return a_re * b_re - a_im * b_im, a_re * b_im + a_im * b_re


def fft_list(values, sign):
    count = len(values)
    if count == 1:
        return values
    even = fft_list(values[0::2], sign)
    odd = fft_list(values[1::2], sign)
    low, high = [], []
    for k in range(count // 2):
        re, im = odd[k]
        if 4 * k == count:
            re, im = (-im, re) if sign > 0 else (im, -re)
        elif k:
            w_re = math.cos(2.0 * math.pi * k / count)
            w_im = sign * math.sin(2.0 * math.pi * k / count)
            re, im = re * w_re - im * w_im, re * w_im + im * w_re
        low.append((even[k][0] + re, even[k][1] + im))
        high.append((even[k][0] - re, even[k][1] - im))
    return low + high


def swap_blocks(arrays, width):
    arrays = list(arrays)
    lane = lax.broadcasted_iota(jnp.int32, arrays[0].shape, 1)
    for bit in (1, 2, 4, 8):
        keep = (lane // width) & bit == 0
        for a in range(16):
            if a & bit:
                continue
            first, second = arrays[a], arrays[a + bit]
            arrays[a] = jnp.where(keep, first, pltpu.roll(second, bit * width, 1))
            arrays[a + bit] = jnp.where(keep, pltpu.roll(first, LANES - bit * width, 1), second)
    return arrays


def kernel(
    raw_hbm, filt_hbm, azf_hbm, shift_hbm, frac_hbm, ktab_hbm,
    first_hbm, last_hbm, twist_hbm, fwd_hbm, back_hbm, planes_hbm, az_fwd_hbm, az_back_hbm, az_twist_hbm,
    out_hbm,
    filt_in, azf_in, shift_in, frac_in, ktab, first, last, twist, fwd, back, planes, az_fwd, az_back, az_twist,
    load_sem,
    tiles, to_like, to_cross, to_core, x_ref, filt, v_ref, y0, y1, y2, y3, y4, z0, z1, z2, z3, z4, t_ref, g_ref, o_ref,
    shift_ref, w_ref, a_ref, h_ref, d_ref, m_ref, e_ref, f_ref,
    tile_sem, x_send, x_recv, z_send, z_recv,
    p_send, p_recv, h_send, h_recv, fwd_send, fwd_recv, out_sem,
):
    pulse = lax.axis_index("pulse")
    lane = lax.axis_index("rng")
    z = lax.div(pulse, 8)
    y = lax.rem(lax.div(pulse, 2), 4)
    xh = lax.div(lane, 2)
    core = lax.rem(lane, 2)
    q_me = 2 * lax.rem(pulse, 2) + xh
    chip = 4 * y + q_me
    has_below = z > 0
    has_above = z < PLANES - 1

    def device(plane, other_chip, other_core):
        return (8 * plane + lax.div(other_chip, 2), 2 * lax.rem(other_chip, 2) + other_core)

    x_partner = (pulse, 2 * (1 - xh) + core)
    x_cross = (pulse, 2 * (1 - xh) + 1 - core)
    core_partner = (pulse, 2 * xh + 1 - core)

    place = 2 * chip + core
    loads = [
        (filt_hbm, filt_in), (first_hbm, first), (twist_hbm, twist), (fwd_hbm, fwd), (back_hbm, back),
        (last_hbm, last), (planes_hbm.at[place], planes), (azf_hbm, azf_in), (shift_hbm, shift_in),
        (frac_hbm, frac_in), (ktab_hbm, ktab), (az_fwd_hbm, az_fwd), (az_back_hbm, az_back),
        (az_twist_hbm, az_twist),
    ]
    loads = [pltpu.make_async_copy(src, dst, load_sem.at[k]) for k, (src, dst) in enumerate(loads)]
    tile_loads = [
        pltpu.make_async_copy(raw_hbm.at[:, 1 - xh], tiles.at[1], tile_sem.at[1]),
        pltpu.make_async_copy(raw_hbm.at[:, xh], tiles.at[0], tile_sem.at[0]),
    ]
    for load in tile_loads:
        load.start()

    barrier = pltpu.get_barrier_semaphore()

    def greet(to):
        pl.semaphore_signal(barrier, inc=1, device_id=to, device_id_type=MESH)

    greet(x_partner)
    greet(x_cross)
    greet(core_partner)

    def greet_z(off, _):
        greet(device(lax.rem(z + off, PLANES), chip, core))
        return 0

    def greet_plane(off, _):
        greet(device(z, lax.rem(chip + off, CHIPS), core))
        return 0

    def greet_all(plane):
        def body(other, _):
            greet(device(plane, other, core))
            return 0

        lax.fori_loop(0, CHIPS, body, 0)

    lax.fori_loop(1, PLANES, greet_z, 0)
    lax.fori_loop(1, CHIPS, greet_plane, 0)
    pl.when(jnp.logical_and(chip == 0, has_below))(lambda: greet_all(z - 1))
    pl.when(jnp.logical_and(chip == CHIPS - 1, has_above))(lambda: greet_all(z + 1))

    for load in loads:
        load.start()

    def blank(start, size):
        def body(other, _):
            g_ref[other, start : start + size, :] = jnp.zeros((size, LANES), F32)
            return 0

        lax.fori_loop(0, CHIPS, body, 0)

    pl.when(jnp.logical_and(chip == 0, z == 0))(lambda: blank(0, BELOW))
    pl.when(jnp.logical_and(chip == CHIPS - 1, z == PLANES - 1))(lambda: blank(PAIR - ABOVE, ABOVE))

    my_quarter = 2 * xh + core

    def quarter_rows(quarter):
        return pl.ds(pl.multiple_of(48 * quarter, 8), 48)

    for load in tile_loads:
        load.wait()
    def sort_pulse(r):
        like = pl.ds(4 * core + r, 48, stride=8)
        other = pl.ds(4 * (1 - core) + r, 48, stride=8)
        for c in range(2):
            to_like[r, c] = tiles[1, c, like, :]
            to_cross[r, c] = tiles[1, c, other, :]
            to_core[r, c] = tiles[0, c, other, :]
            x_ref[r, c, quarter_rows(my_quarter), :] = tiles[0, c, like, :]

    sort_pulse(0)
    pl.semaphore_wait(
        barrier,
        3 + PLANES - 1 + CHIPS - 1 + jnp.where(has_below, 1, 0) + jnp.where(has_above, 1, 0),
    )

    def pulse_copy(r, which):
        return pltpu.make_async_remote_copy(
            src_ref=(to_like, to_cross, to_core)[which].at[r],
            dst_ref=x_ref.at[r, :, quarter_rows(my_quarter)],
            send_sem=x_send.at[r, which],
            recv_sem=x_recv.at[r, which],
            device_id=(x_partner, x_cross, core_partner)[which],
            device_id_type=MESH,
        )

    def send_pulse(r):
        for which in range(3):
            pulse_copy(r, which).start()

    send_pulse(0)
    for r in range(1, LANE_PULSES):
        sort_pulse(r)

    for load in loads:
        load.wait()
    for c in range(2):
        cols = [filt_in[pl.ds(2 * u + c, 64, stride=6), :].T for u in range(3)]
        tall = jnp.concatenate(cols, axis=0)
        filt[c] = jnp.concatenate([tall[:ROWS], tall[ROWS:]], axis=1)

    def wait_pulse(r):
        for which in range(3):
            pulse_copy(r, which).wait_recv()

    def compress(r):
        twist_re, twist_im = twist[0], twist[1]
        v = times_left(first[...], jnp.concatenate([x_ref[r, 0], x_ref[r, 1]], axis=0))
        re, im = cmul(v[:ROWS], v[ROWS:], twist_re, twist_im)
        s = times_right(jnp.concatenate([re, im], axis=1), fwd[...])
        re, im = cmul(s[:, :LANES], s[:, LANES:], filt[0], filt[1])
        s = times_right(jnp.concatenate([re, im], axis=1), back[...])
        re, im = cmul(s[:, :LANES], s[:, LANES:], twist_re, -twist_im)
        high, low = split(jnp.concatenate([re, im], axis=0))
        v_ref[r, 0 : 2 * ROWS] = high
        v_ref[r, 2 * ROWS : 4 * ROWS] = low
        v_ref[r, 4 * ROWS : 6 * ROWS] = high

    ys, zs = (y0, y1, y2, y3, y4), (z0, z1, z2, z3, z4)

    def chunk_of(t):
        if t in (0, 3):
            return lax.rem(y + (2 if t == 0 else 0), CHUNKS)
        return lax.rem(y + jnp.where(core == t - 1, 1, 3), CHUNKS)

    def z_mine_rows(block):
        return pl.ds(pl.multiple_of(BLOCKS[block] * z, 8), BLOCKS[block])

    def z_copy(block, off):
        to = lax.rem(z + off, PLANES)
        return pltpu.make_async_remote_copy(
            src_ref=ys[block].at[to],
            dst_ref=zs[block].at[z_mine_rows(block)],
            send_sem=z_send.at[block],
            recv_sem=z_recv.at[block],
            device_id=device(to, chip, core),
            device_id_type=MESH,
        )

    def z_mine(block):
        return pltpu.make_async_copy(ys[block].at[z], zs[block].at[z_mine_rows(block)], z_recv.at[block])

    def send_block(block):
        def start(step, _):
            near = PLANES // 2 - step
            z_copy(block, near).start()
            z_copy(block, PLANES - near).start()
            return 0

        z_copy(block, PLANES // 2).start()
        lax.fori_loop(1, PLANES // 2, start, 0)
        z_mine(block).start()

    def wait_for(ref, sem):
        pltpu.make_async_copy(ref, ref, sem).wait()

    def sent_block(block):
        wait_for(ys[block].at[pl.ds(0, PLANES - 1)], z_send.at[block])

    size = 2 * CHUNK_ROWS

    def place_of(t, r, c, row):
        rows = {0: (0, 1, 2), 1: (0,) if row == 0 else (1, 2), 2: (0, 1) if row < 2 else (2,), 3: (0, 1, 2)}[t]
        block, start = {(0, 0): (2, 0), (1, 0): (2, 12), (1, 1): (3, 0), (2, 0): (3, 8), (2, 2): (4, 0), (3, 0): (4, 4)}[
            t, rows[0]
        ]
        return block, start + len(rows) * (2 * (r - 2) + c) + row - rows[0]

    for r in range(2):
        wait_pulse(r)
        send_pulse(r + 1)
        compress(r)
        for chunk in range(CHUNKS):
            out = jnp.dot(last[chunk], v_ref[r], preferred_element_type=F32)
            for to in range(PLANES):
                ys[r][to, size * chunk : size * (chunk + 1), :] = out[size * to : size * (to + 1)]
        send_block(r)

    def later_pulse(r, _):
        wait_pulse(r)
        pl.when(r < LANE_PULSES - 1)(lambda: send_pulse(r + 1))
        compress(r)
        return 0

    lax.fori_loop(2, 4, later_pulse, 0)
    both = jnp.concatenate([v_ref[2], v_ref[3]], axis=1)

    def make_chunk(t):
        out = jnp.dot(last[chunk_of(t)], both, preferred_element_type=F32)
        for r in (2, 3):
            lanes = slice(LANES * (r - 2), LANES * (r - 1))
            pieces = {1: [(0, 1), (1, 3), (3, 4), (4, 6)], 2: [(0, 2), (2, 3), (3, 5), (5, 6)]}.get(t, [(0, 6)])
            for first_row, end in pieces:
                block, place = place_of(t, r, first_row // 3, first_row % 3)
                for to in range(PLANES):
                    ys[block][to, place : place + end - first_row, :] = out[
                        size * to + first_row : size * to + end, lanes
                    ]

    for t in range(2):
        make_chunk(t)
    sent_block(0)
    send_block(2)
    for t in (2, 3):
        make_chunk(t)

    def turn_filter(step, _):
        rows = pl.ds(pl.multiple_of(8 * step, 8), 8)
        for c in range(2):
            got = swap_blocks([azf_in[c, rows, LANES * k : LANES * (k + 1)] for k in range(16)], 1)
            for k1 in range(16):
                a_ref[c, k1, rows, :] = got[k1]
        return 0

    lax.fori_loop(0, BINS // 8, turn_filter, 0)

    def by_bin(values):
        tall = values.T
        return jnp.concatenate([tall[16 * u : 16 * (u + 1)] for u in range(8)], axis=1)

    shift_ref[...] = by_bin(shift_in[...])
    frac = by_bin(frac_in[...])
    for tap in range(TAPS):
        weight = jnp.zeros(frac.shape, F32)
        for row in range(16):
            weight = jnp.where(frac == row, ktab[tap, row], weight)
        w_ref[tap] = weight

    for r in range(LANE_PULSES):
        for which in range(3):
            pulse_copy(r, which).wait_send()

    sent_block(1)
    send_block(3)
    sent_block(2)
    send_block(4)

    def window(q):
        if q == 0:
            return 0, BELOW, PAIR - BELOW
        if q == 3:
            return CHUNK - BELOW - 2 * BINS, 0, PAIR - ABOVE
        return 2 * BINS * q - BELOW, 0, PAIR

    def main_copy(t, q):
        src, dst, size = window(q)
        return pltpu.make_async_remote_copy(
            src_ref=t_ref.at[t, pl.ds(src, size)],
            dst_ref=g_ref.at[chip, pl.ds(dst, size)],
            send_sem=p_send.at[t, q],
            recv_sem=p_recv.at[y],
            device_id=device(z, 4 * chunk_of(t) + q, core),
            device_id_type=MESH,
        )

    def main_own(q):
        src, dst, size = window(q)
        return pltpu.make_async_copy(
            t_ref.at[CHUNKS - 1, pl.ds(src, size)], g_ref.at[chip, pl.ds(dst, size)], p_recv.at[y]
        )

    def each_main(t, qs, act, local):
        for q in qs:
            if t < CHUNKS - 1:
                act(main_copy(t, q))
            else:
                pl.when(q_me != q)(functools.partial(lambda q: act(main_copy(t, q)), q))
                if local:
                    pl.when(q_me == q)(functools.partial(lambda q: local(main_own(q)), q))

    def on_window(act):
        for q in range(4):
            pl.when(q_me == q)(functools.partial(lambda q: act(*window(q)), q))

    def halo_targets(chunk):
        down_chip = lax.rem(4 * chunk + CHIPS - 1, CHIPS)
        up_chip = lax.rem(4 * chunk + 4, CHIPS)
        down_plane = jnp.where(chunk == 0, z - 1, z)
        up_plane = jnp.where(chunk == CHUNKS - 1, z + 1, z)
        return down_plane, down_chip, up_plane, up_chip

    DOWN = (0, PAIR - ABOVE, ABOVE)
    UP = (CHUNK - BELOW, 0, BELOW)

    def halo_copy(t, which, plane, to):
        src, dst, size = (DOWN, UP)[which]
        return pltpu.make_async_remote_copy(
            src_ref=t_ref.at[t, pl.ds(src, size)],
            dst_ref=g_ref.at[chip, pl.ds(dst, size)],
            send_sem=h_send.at[t, which],
            recv_sem=h_recv.at[y],
            device_id=device(plane, to, core),
            device_id_type=MESH,
        )

    def halo_mine(t, which):
        src, dst, size = (DOWN, UP)[which]
        return pltpu.make_async_copy(
            t_ref.at[t, pl.ds(src, size)], g_ref.at[chip, pl.ds(dst, size)], h_recv.at[y]
        )

    def each_halo(t, whichs, act, local):
        down_plane, down_chip, up_plane, up_chip = halo_targets(chunk_of(t))
        for which, plane, to in ((0, down_plane, down_chip), (1, up_plane, up_chip)):
            if which not in whichs:
                continue
            inside = jnp.logical_and(plane >= 0, plane < PLANES)
            me = jnp.logical_and(plane == z, to == chip)
            pl.when(jnp.logical_and(inside, jnp.logical_not(me)))(
                functools.partial(lambda *a: act(halo_copy(*a)), t, which, plane, to)
            )
            if local:
                pl.when(me)(functools.partial(lambda *a: local(halo_mine(*a)), t, which))

    def wait_block(block):
        wait_for(zs[block], z_recv.at[block])

    def start(copy):
        copy.start()

    def sent_chunk(t):
        each_main(t, range(4), lambda copy: copy.wait_send(), None)
        each_halo(t, (0, 1), lambda copy: copy.wait_send(), None)

    def turn_chunk(t, rows):
        chunk = chunk_of(t)
        for row in rows:
            parts = []
            for c in range(2):
                for r in range(2):
                    place = size * chunk + CHUNK_ROWS * c + row
                    parts.append(zs[r][pl.ds(place, PLANES, stride=BLOCKS[r]), :])
                for r in (2, 3):
                    block, place = place_of(t, r, c, row)
                    parts.append(zs[block][pl.ds(place, PLANES, stride=BLOCKS[block]), :])
            t_ref[t, LANES * row : LANES * (row + 1), :] = times_right(
                jnp.concatenate(parts, axis=0).T, planes[...]
            )

    for block in range(3):
        wait_block(block)
    turn_chunk(0, range(CHUNK_ROWS))
    each_main(0, range(4), start, start)
    each_halo(0, (0, 1), start, start)
    wait_block(3)
    turn_chunk(1, range(CHUNK_ROWS))
    each_main(1, range(4), start, start)
    each_halo(1, (0, 1), start, start)
    turn_chunk(2, range(2))
    each_main(2, (0, 1), start, start)
    each_halo(2, (0,), start, start)
    sent_chunk(0)
    wait_block(4)
    turn_chunk(2, (2,))
    each_main(2, (2, 3), start, start)
    each_halo(2, (1,), start, start)
    turn_chunk(3, range(CHUNK_ROWS))
    each_main(3, range(4), start, start)
    each_halo(3, (0, 1), start, start)

    def core_copy(row):
        return pltpu.make_async_remote_copy(
            src_ref=g_ref.at[pl.ds(4 * row, 4), pl.ds(pl.multiple_of(BINS * (1 - core), 8), WINDOW)],
            dst_ref=o_ref.at[pl.ds(4 * row, 4)],
            send_sem=fwd_send.at[row],
            recv_sem=fwd_recv.at[row],
            device_id=core_partner,
            device_id_type=MESH,
        )

    takes_up = jnp.logical_and(q_me == 0, jnp.logical_or(y > 0, has_below))
    takes_down = jnp.logical_and(q_me == 3, jnp.logical_or(y < 3, has_above))

    def gather(t):
        row = lax.rem(2 * y + CHUNKS - chunk_of(t), CHUNKS)

        def rows_of(first_row, count):
            return g_ref.at[pl.ds(4 * row, 4), pl.ds(first_row, count)]

        on_window(lambda src, dst, count: wait_for(rows_of(dst, count), p_recv.at[row]))
        pl.when(takes_up)(lambda: wait_for(rows_of(0, BELOW), h_recv.at[row]))
        pl.when(takes_down)(lambda: wait_for(rows_of(PAIR - ABOVE, ABOVE), h_recv.at[row]))
        core_copy(row).start()

    for t in range(CHUNKS):
        gather(t)

    part = WINDOW // 2

    def turn_rows(read):
        def body(step, _):
            rows = pl.ds(pl.multiple_of(part * step, 8), part)
            got = swap_blocks([read(k, part * step) for k in range(CHIPS)], 8)
            for k1 in range(16):
                h_ref[k1, rows, :] = got[k1]
            return 0

        lax.fori_loop(0, WINDOW // part, body, 0)

    group = 8

    def transform(from_core, add):
        def body(step, _):
            high, low = split(h_ref[pl.ds(group * step, group)].reshape(group * WINDOW, LANES))
            d = jnp.dot(
                jnp.concatenate([high, low, high], axis=1), az_fwd[from_core], preferred_element_type=F32
            )
            for k in range(group):
                for c in range(2):
                    piece = d[WINDOW * k : WINDOW * (k + 1), LANES * c : LANES * (c + 1)]
                    if add:
                        piece = piece + d_ref[group * step + k, c]
                    d_ref[group * step + k, c] = piece
            return 0

        lax.fori_loop(0, 16 // group, body, 0)

    turn_rows(lambda k, start: g_ref[k, pl.ds(pl.multiple_of(BINS * core + start, 8), part), :])
    transform(core, False)

    def wait_core(row, _):
        core_copy(row).wait_recv()
        return 0

    for t in (1, 2, 3):
        sent_chunk(t)
    sent_block(3)
    sent_block(4)
    lax.fori_loop(0, 4, wait_core, 0)
    turn_rows(lambda k, start: o_ref[k, pl.ds(pl.multiple_of(start, 8), part), :])
    transform(1 - core, True)

    def migrate(k1, slot):
        shift = shift_ref[pl.ds(k1, 1), :]
        weights = [w_ref[tap, pl.ds(k1, 1), :] for tap in range(TAPS)]
        moved = []
        for c in range(2):
            x = d_ref[k1, c]
            near = jnp.where((shift & 16) != 0, x[16:80], x[0:64])
            x = jnp.concatenate([near, x[64:80]], axis=0)
            m, e = m_ref.at[slot, c], e_ref.at[slot, c]
            m[0:72] = jnp.where((shift & 8) != 0, x[8:80], x[0:72])
            e[0:64] = jnp.where((shift & 4) != 0, m[4:68], m[0:64])
            m[0:62] = jnp.where((shift & 2) != 0, e[2:64], e[0:62])
            e[0:61] = jnp.where((shift & 1) != 0, m[1:62], m[0:61])
            total = weights[0] * e[5 : 5 + BINS]
            for tap in range(1, TAPS):
                total = total + weights[tap] * e[5 + tap : 5 + tap + BINS]
            moved.append(total)
        return jnp.concatenate(cmul(moved[0], moved[1], a_ref[0, k1], a_ref[1, k1]), axis=1)

    def result_copy(step):
        some = pl.ds(group * step, group)
        return pltpu.make_async_copy(f_ref.at[:, some], out_hbm.at[:, some], out_sem.at[step])

    def per_group(step, _):
        ks = [group * step + k for k in range(group)]
        s = times_right(jnp.concatenate([migrate(k1, k) for k, k1 in enumerate(ks)], axis=0), az_back[...])
        for k, k1 in enumerate(ks):
            rows = slice(BINS * k, BINS * (k + 1))
            f_ref[0, k1], f_ref[1, k1] = cmul(
                s[rows, :LANES], s[rows, LANES:], az_twist[0, pl.ds(k1, 1), :], az_twist[1, pl.ds(k1, 1), :]
            )
        result_copy(step).start()
        return 0

    lax.fori_loop(0, 16 // group, per_group, 0)

    def sent_core(row, _):
        core_copy(row).wait_send()
        return 0

    lax.fori_loop(0, 4, sent_core, 0)
    for step in range(16 // group):
        result_copy(step).wait()


def finish_kernel(f_hbm, out_hbm, f_ref, out_ref, in_sem, out_sem):
    def fetch(step):
        rows = slice(8 * step, 8 * (step + 1))
        return pltpu.make_async_copy(f_hbm.at[:, :, rows], f_ref.at[:, :, rows], in_sem.at[step])

    def store(step):
        rows = slice(8 * step, 8 * (step + 1))
        return pltpu.make_async_copy(out_ref.at[:, rows], out_hbm.at[:, rows], out_sem.at[step])

    for step in range(BINS // 8):
        fetch(step).start()
    for step in range(BINS // 8):
        rows = slice(8 * step, 8 * (step + 1))
        fetch(step).wait()
        got = fft_list([(f_ref[0, k1, rows, :], f_ref[1, k1, rows, :]) for k1 in range(16)], 1)
        for tile in range(16):
            for c in range(2):
                out_ref[c, rows, LANES * tile : LANES * (tile + 1)] = got[tile][c]
        store(step).start()
    for step in range(BINS // 8):
        store(step).wait()


IN_HBM = pl.BlockSpec(memory_space=pltpu.HBM)
DMA = pltpu.SemaphoreType.DMA


def shards(raw, range_filter, azimuth_filter, shifts, frac_index, kernel_table):
    order = filter_order()
    tables = [
        table_first(),
        table_last(),
        table_twist(),
        right_factor(table_columns(np.arange(LANES), order, -1)),
        right_factor(table_columns(order, np.arange(LANES), 1)),
        table_planes(),
        table_azimuth(),
        table_back(),
        table_back_twist(),
    ]
    operands = [
        raw.reshape(2, 2, 8, 48, LANES).transpose(0, 1, 3, 2, 4).reshape(2, 2, 384, LANES),
        range_filter.reshape(2, ROWS, LANES).transpose(1, 0, 2).reshape(2 * ROWS, LANES),
        azimuth_filter,
        shifts.reshape(16, LANES),
        frac_index.reshape(16, LANES),
        kernel_table.T,
    ]

    def like(array, shape=None):
        return pltpu.VMEM(array.shape if shape is None else shape, array.dtype)

    loads = [like(a) for a in operands[1:5]] + [pltpu.SMEM(operands[5].shape, F32)]
    loads += [like(a) for a in tables]
    loads[5 + 5] = like(tables[5], tables[5].shape[1:])
    scratch = [
        pltpu.VMEM((2, 2, 384, LANES), F32),
        pltpu.VMEM((LANE_PULSES, 2, 48, LANES), F32),
        pltpu.VMEM((LANE_PULSES, 2, 48, LANES), F32),
        pltpu.VMEM((LANE_PULSES, 2, 48, LANES), F32),
        pltpu.VMEM((LANE_PULSES, 2, ROWS, LANES), F32),
        pltpu.VMEM((2, ROWS, LANES), F32),
        pltpu.VMEM((LANE_PULSES, 6 * ROWS, LANES), BF16),
        *[pltpu.VMEM((PLANES, rows, LANES), F32) for rows in BLOCKS],
        *[pltpu.VMEM((PLANES * rows, LANES), F32) for rows in BLOCKS],
        pltpu.VMEM((CHUNKS, CHUNK, LANES), F32),
        pltpu.VMEM((CHIPS, PAIR, LANES), F32),
        pltpu.VMEM((CHIPS, WINDOW, LANES), F32),
        pltpu.VMEM((16, LANES), jnp.int32),
        pltpu.VMEM((TAPS, 16, LANES), F32),
        pltpu.VMEM((2, 16, BINS, LANES), F32),
        pltpu.VMEM((16, WINDOW, LANES), F32),
        pltpu.VMEM((16, 2, WINDOW, LANES), F32),
        pltpu.VMEM((8, 2, WINDOW, LANES), F32),
        pltpu.VMEM((8, 2, WINDOW, LANES), F32),
        pltpu.VMEM((2, 16, BINS, LANES), F32),
        DMA((2,)), DMA((4, 3)), DMA((4, 3)),
        DMA((len(BLOCKS),)), DMA((len(BLOCKS),)),
        DMA((CHUNKS, 4)), DMA((4,)), DMA((CHUNKS, 2)), DMA((4,)), DMA((4,)), DMA((4,)), DMA((4,)),
    ]
    turned = pl.pallas_call(
        kernel,
        out_shape=jax.ShapeDtypeStruct((2, 16, BINS, LANES), F32),
        in_specs=[IN_HBM] * (len(operands) + len(tables)),
        out_specs=IN_HBM,
        scratch_shapes=loads + [DMA((len(loads),))] + scratch,
        compiler_params=pltpu.CompilerParams(
            vmem_limit_bytes=60 * 2**20, collective_id=0, has_side_effects=True
        ),
    )(*operands, *tables)
    return pl.pallas_call(
        finish_kernel,
        out_shape=jax.ShapeDtypeStruct((2, BINS, PULSES), F32),
        in_specs=[IN_HBM],
        out_specs=IN_HBM,
        scratch_shapes=[
            pltpu.VMEM((2, 16, BINS, LANES), F32),
            pltpu.VMEM((2, BINS, PULSES), F32),
            DMA((BINS // 8,)),
            DMA((BINS // 8,)),
        ],
        compiler_params=pltpu.CompilerParams(vmem_limit_bytes=60 * 2**20),
    )(turned)


def solution(mesh):
    in_specs = (P(None, "pulse", "rng"), P(), P(None, ("pulse", "rng"), None), P(), P(), P())
    out_specs = P(None, ("pulse", "rng"), None)
    return jax.shard_map(shards, mesh=mesh, in_specs=in_specs, out_specs=out_specs, check_vma=False)
```
